32 devices in a mesh: req: 4 (over y, x), tp: 8 (over z, core).
Axes of the slice: x: 2, y: 2, z: 4, core: 2. Of those that a mesh axis runs over, the one named last changes fastest.
Arguments:
- hidden_states: bfloat16 [16, 4, 1024], P('req'), may hold values from -48 to 48
- lengths: int32 [16], P('req'), may hold values from 16 to 1024, as said below
- qkv_weight: bfloat16 [2048, 1024], P('tp'), may hold values from -1 to 1
- rotated_key_cache: bfloat16 [16, 1024, 512], P('req', 'tp'), may hold values from -1000 to 1000
- earlier_value_cache: bfloat16 [16, 1024, 512], P('req', 'tp'), may hold values from -16 to 16
- out_weight: bfloat16 [1024, 1024], P('tp'), may hold values from -0.1875 to 0.1875
- expert_ids: int32 [16, 4, 8], P('req'), may hold values from 0 to 31, all different within a row
- combine_weights: int32 [16, 4, 8], P('req'), may hold values from 4096 to 65535
- gate_up_weight: bfloat16 [32, 1024, 1024], P('tp'), may hold values from -0.1875 to 0.1875
- down_weight: bfloat16 [32, 512, 1024], P('tp'), may hold values from -0.25 to 0.25
Outputs:
- layer_output: bfloat16 [16, 4, 1024], P('req')
The draws below stay inside these ranges and needn't reach their ends.
Inputs may be any that keep to these rules, and one draw needn't show every extreme that they name: `lengths`: cache length of each request; some request has exactly 1024. `expert_ids`: each token's 8 experts are distinct.
All inputs are finite; a program needn't handle non-finite values.
Results may differ from the reference program's by a relative error of at most 0.008.
Values may be sent and summed in bfloat16 or wider, within the bound.
No kernel may reach another device: no remote copies, remote signals or barrier semaphores. Data moves between devices by JAX's collectives and lax.ppermute only.
A program may use at most 64 MiB of HBM per device.

```python
from functools import partial
import jax
import jax.numpy as jnp
from jax import lax

D = 1024
QUERY_HEADS = 16
KEY_VALUE_HEADS = 8
HEAD_DIMENSION = 64
FF = 512
EXPERTS = 32
TOPK = 8
DECODE_STEPS = 4
CACHE_POSITIONS = 1024
REQUEST_TOTAL = 16
QKV = 2048
N_TP = 8


def length_table(key):
    base_key = jax.random.fold_in(key, 11)
    first_key, second_key, third_key = jax.random.split(base_key, 3)
    spread = jax.random.randint(first_key, (REQUEST_TOTAL,), 0, CACHE_POSITIONS - 15, dtype=jnp.int32)
    shifts = jax.random.randint(second_key, (REQUEST_TOTAL,), 0, 8, dtype=jnp.int32)
    value_rows = 16 + jnp.right_shift(spread, shifts)
    longest = jax.random.randint(third_key, (), 0, REQUEST_TOTAL, dtype=jnp.int32)
    return jnp.where(jnp.arange(REQUEST_TOTAL, dtype=jnp.int32) == longest, CACHE_POSITIONS, value_rows).astype(jnp.int32)


def hidden_table(key):
    base_key = jax.random.fold_in(key, 12)
    first_key, second_key = jax.random.split(base_key, 2)
    columns = jnp.exp(jax.random.uniform(second_key, (D,), jnp.float32, jnp.log(0.33), jnp.log(3.0)))
    random_jitter = jax.random.truncated_normal(first_key, -4.0, 4.0, (REQUEST_TOTAL, DECODE_STEPS, D), jnp.float32)
    return jnp.clip(random_jitter * columns, -48.0, 48.0)


def projection_table(key):
    base_key = jax.random.fold_in(key, 13)
    value_rows = jax.random.truncated_normal(base_key, -4.0, 4.0, (QKV, D), jnp.float32) * D ** (-0.5)
    return jnp.clip(value_rows, -1.0, 1.0)


def draw_hidden_states(key, part):
    return hidden_table(key).astype(jnp.bfloat16)


def draw_lengths(key, part):
    return length_table(key)


def draw_qkv_weight(key, part):
    return projection_table(key).astype(jnp.bfloat16)


def draw_rotated_key_cache(key, part):
    base_key = jax.random.fold_in(key, 14)
    first_key, second_key = jax.random.split(base_key, 2)
    random_jitter = jax.random.truncated_normal(first_key, -4.0, 4.0, (REQUEST_TOTAL, CACHE_POSITIONS, KEY_VALUE_HEADS * HEAD_DIMENSION), jnp.float32)
    scales = jnp.exp(jax.random.uniform(second_key, (REQUEST_TOTAL, CACHE_POSITIONS, 1), jnp.float32, jnp.log(0.3), jnp.log(3.0)))
    key_rows = random_jitter * scales
    return jnp.clip(key_rows, -1000.0, 1000.0).astype(jnp.bfloat16)


def draw_earlier_value_cache(key, part):
    base_key = jax.random.fold_in(key, 15)
    first_key, second_key = jax.random.split(base_key, 2)
    band_length = max(1, CACHE_POSITIONS // 32)
    rough_scores = jax.random.truncated_normal(second_key, -4.0, 4.0, (REQUEST_TOTAL, CACHE_POSITIONS // band_length, 1, KEY_VALUE_HEADS * HEAD_DIMENSION), jnp.float32)
    random_jitter = jax.random.truncated_normal(first_key, -4.0, 4.0, (REQUEST_TOTAL, CACHE_POSITIONS // band_length, band_length, KEY_VALUE_HEADS * HEAD_DIMENSION), jnp.float32)
    value_rows = random_jitter + 2.0 * rough_scores
    return jnp.clip(value_rows.reshape(REQUEST_TOTAL, CACHE_POSITIONS, KEY_VALUE_HEADS * HEAD_DIMENSION), -16.0, 16.0).astype(jnp.bfloat16)


def place_ends(drawn, own_key, least, high):
    place = [jax.random.randint(jax.random.fold_in(own_key, axis), (), 0, length) for axis, length in enumerate(drawn.shape)]
    widest = drawn.shape.index(max(drawn.shape))
    neighbour = place[:widest] + [(place[widest] + 1) % drawn.shape[widest]] + place[widest + 1:]
    return drawn.at[tuple(place)].set(least).at[tuple(neighbour)].set(high)


def block_levels(own_key, extent, pieces, low, largest):
    level, own = 1.0, jax.random.fold_in(own_key, 6)
    for dim, parts in pieces:
        heights = jnp.exp(jax.random.uniform(jax.random.fold_in(own, dim), (parts,), jnp.float32, low / len(pieces), largest / len(pieces)))
        level = level * jnp.repeat(heights, extent[dim] // parts).reshape([-1 if axis == dim else 1 for axis in range(len(extent))])
    return level


def choose_distinct(stream_key, rows, count, top, lift):
    sequence = jax.random.permutation(jax.random.fold_in(stream_key, 1), count)
    pull = sequence
    for power in range(3):
        pull = pull * pull // count
    pull = pull * lift // count
    chance = jax.random.randint(jax.random.fold_in(stream_key, 2), (rows, count), 0, 4096) + pull
    fixed_rows = jax.random.permutation(jax.random.fold_in(stream_key, 3), rows)[jnp.arange(count) % rows]
    chance = jnp.where(jnp.arange(rows)[:, None] == fixed_rows[None, :], 1 << 14, chance)
    priority = chance * count + jnp.arange(count)
    return lax.top_k(priority.astype(jnp.int32), top)[1].astype(jnp.int32)


def noise(key, extent, deviation, limit, shards=(), kind=jnp.bfloat16):
    values = jax.random.normal(key, extent, jnp.float32) * deviation
    if len(shards) > 0:
        values = block_levels(key, extent, shards, -0.22, 0.18) * values
    return jnp.clip(values, min=-limit, max=limit).astype(kind)


def setup_inputs(seed: int = 0) -> dict:
    key_of = jax.random.split(jax.random.key(seed), 11)
    return {
        "hidden_states": draw_hidden_states(jax.random.fold_in(key_of[10], 71), 0),
        "lengths": draw_lengths(jax.random.fold_in(key_of[10], 71), 0),
        "qkv_weight": draw_qkv_weight(jax.random.fold_in(key_of[10], 71), 0),
        "rotated_key_cache": draw_rotated_key_cache(jax.random.fold_in(key_of[10], 71), 0),
        "earlier_value_cache": draw_earlier_value_cache(jax.random.fold_in(key_of[10], 71), 0),
        "out_weight": noise(key_of[5], (QUERY_HEADS * HEAD_DIMENSION, D), (QUERY_HEADS * HEAD_DIMENSION) ** -0.5, 0.1875, ((0, 8),)),
        "expert_ids": choose_distinct(key_of[6], REQUEST_TOTAL * DECODE_STEPS, EXPERTS, TOPK, 2048).reshape((REQUEST_TOTAL, DECODE_STEPS, TOPK)),
        "combine_weights": place_ends(jax.random.randint(key_of[7], (REQUEST_TOTAL, DECODE_STEPS, TOPK), 4096, 65536), jax.random.fold_in(key_of[7], 1), 4096, 65535).astype(jnp.int32),
        "gate_up_weight": noise(key_of[8], (EXPERTS, D, 2 * FF), D ** -0.5, 0.1875, ((0, 8),)),
        "down_weight": noise(key_of[9], (EXPERTS, FF, D), FF ** -0.5, 0.25, ((0, 8),)),
    }


EPSILON = 1e-05
ROPE_BASE = 10000.0
NEGATIVE = -1e+30

def rms_rows(value_rows):
    return value_rows * lax.rsqrt(lax.optimization_barrier(jnp.mean(value_rows * value_rows, axis=-1, keepdims=True)) + EPSILON)

def apply_rotation(value_rows, position_index):
    half_width = value_rows.shape[-1] // 2
    rates = ROPE_BASE ** (-2.0 * jnp.arange(half_width, dtype=jnp.float32) / value_rows.shape[-1])
    angles = position_index[:, None, None] * rates
    cosine = jnp.cos(angles)
    sines = jnp.sin(angles)
    front_half = value_rows[..., :half_width]
    back_half = value_rows[..., half_width:]
    return jnp.concatenate([front_half * cosine - back_half * sines, back_half * cosine + front_half * sines], axis=-1)

def attend_one(item, qkv_weight):
    tokens, length, key_rows, value_rows = item
    query_total_width = QUERY_HEADS * HEAD_DIMENSION
    key_value_width = KEY_VALUE_HEADS * HEAD_DIMENSION
    group_count = QUERY_HEADS // KEY_VALUE_HEADS
    normed = rms_rows(tokens.astype(jnp.float32)).astype(jnp.bfloat16)
    projected_rows = jnp.dot(normed, qkv_weight.T, preferred_element_type=jnp.float32).astype(jnp.bfloat16)
    position_index = (length + jnp.arange(DECODE_STEPS, dtype=jnp.int32)).astype(jnp.float32)
    query_rows = apply_rotation(projected_rows[:, :query_total_width].reshape(DECODE_STEPS, QUERY_HEADS, HEAD_DIMENSION).astype(jnp.float32), position_index).astype(jnp.bfloat16)
    fresh_keys = apply_rotation(projected_rows[:, query_total_width:query_total_width + key_value_width].reshape(DECODE_STEPS, KEY_VALUE_HEADS, HEAD_DIMENSION).astype(jnp.float32), position_index).astype(jnp.bfloat16)
    fresh_values = projected_rows[:, query_total_width + key_value_width:].reshape(DECODE_STEPS, KEY_VALUE_HEADS, HEAD_DIMENSION).astype(jnp.float32)
    grouped_rows = query_rows.reshape(DECODE_STEPS, KEY_VALUE_HEADS, group_count, HEAD_DIMENSION).transpose(1, 0, 2, 3).reshape(KEY_VALUE_HEADS, DECODE_STEPS * group_count, HEAD_DIMENSION).astype(jnp.float32)
    block_extent = CACHE_POSITIONS // N_TP
    stored_keys = key_rows.reshape(N_TP, block_extent, KEY_VALUE_HEADS, HEAD_DIMENSION).astype(jnp.float32)
    stored_values = value_rows.reshape(N_TP, block_extent, KEY_VALUE_HEADS, HEAD_DIMENSION).astype(jnp.float32)
    score_scale = HEAD_DIMENSION ** (-0.5)
    scores = jnp.einsum('gqd,ncgd->ngqc', grouped_rows, stored_keys) * score_scale
    live_mask = (jnp.arange(CACHE_POSITIONS, dtype=jnp.int32) < length).reshape(N_TP, 1, 1, block_extent)
    masked = jnp.where(live_mask, scores, NEGATIVE)
    highest = lax.optimization_barrier(jnp.max(masked, axis=-1))
    weights = jnp.where(live_mask, jnp.exp(masked - highest[..., None]), 0.0)
    weight_sum = lax.optimization_barrier(jnp.sum(weights, axis=-1))
    rounded = lax.optimization_barrier(weights.astype(jnp.bfloat16)).astype(jnp.float32)
    value_sum = jnp.einsum('ngqc,ncgd->ngqd', rounded, stored_values)
    top_score = lax.optimization_barrier(jnp.max(highest, axis=0))
    rescale = jnp.exp(highest - top_score)
    total_all = lax.optimization_barrier(jnp.sum(weight_sum * rescale, axis=0))
    sum_all = lax.optimization_barrier(jnp.sum(value_sum * rescale[..., None], axis=0))
    new_scores = jnp.einsum('gqd,sgd->gqs', grouped_rows, fresh_keys.astype(jnp.float32)) * score_scale
    query_step = jnp.arange(DECODE_STEPS * group_count, dtype=jnp.int32) // group_count
    causal = jnp.arange(DECODE_STEPS, dtype=jnp.int32)[None, :] <= query_step[:, None]
    new_masked = jnp.where(causal, new_scores, NEGATIVE)
    final_peak = jnp.maximum(top_score, lax.optimization_barrier(jnp.max(new_masked, axis=-1)))
    new_weights = jnp.where(causal, jnp.exp(new_masked - final_peak[..., None]), 0.0)
    carried = jnp.exp(top_score - final_peak)
    denominator = total_all * carried + lax.optimization_barrier(jnp.sum(new_weights, axis=-1))
    new_rounded = lax.optimization_barrier(new_weights.astype(jnp.bfloat16)).astype(jnp.float32)
    numerator = sum_all * carried[..., None] + jnp.einsum('gqs,sgd->gqd', new_rounded, fresh_values)
    final_result = numerator / denominator[..., None]
    return final_result.reshape(KEY_VALUE_HEADS, DECODE_STEPS, group_count, HEAD_DIMENSION).transpose(1, 0, 2, 3).reshape(DECODE_STEPS, query_total_width).astype(jnp.bfloat16)

def reference(hidden_states, lengths, qkv_weight, rotated_key_cache, earlier_value_cache, out_weight, expert_ids, combine_weights, gate_up_weight, down_weight):
    attended = lax.map(partial(attend_one, qkv_weight=qkv_weight), (hidden_states, lengths, rotated_key_cache, earlier_value_cache))
    token_count = REQUEST_TOTAL * DECODE_STEPS
    projected_rows = jnp.dot(attended.reshape(token_count, QUERY_HEADS * HEAD_DIMENSION), out_weight, preferred_element_type=jnp.float32)
    residual = hidden_states.reshape(token_count, D).astype(jnp.float32) + projected_rows
    normed_second = rms_rows(residual).astype(jnp.bfloat16)
    shares = combine_weights.reshape(token_count, TOPK).astype(jnp.float32) / 65536.0
    chosen = expert_ids.reshape(token_count, TOPK)

    def add_expert(running, item):
        expert_index, gate_up, down_part = item
        united_out = jnp.dot(normed_second, gate_up, preferred_element_type=jnp.float32)
        activation = (jax.nn.silu(united_out[:, :FF]) * united_out[:, FF:]).astype(jnp.bfloat16)
        outcome = jnp.dot(activation, down_part, preferred_element_type=jnp.float32)
        factors = lax.optimization_barrier(jnp.sum(jnp.where(chosen == expert_index, shares, 0.0), axis=-1))
        return (running + factors[:, None] * outcome, None)
    mixture, _ = lax.scan(add_expert, jnp.zeros((token_count, D), jnp.float32), (jnp.arange(EXPERTS, dtype=jnp.int32), gate_up_weight, down_weight))
    return (residual + mixture).astype(jnp.bfloat16).reshape(REQUEST_TOTAL, DECODE_STEPS, D)
```

```python
import functools

import jax
import jax.numpy as jnp
from jax import lax
from jax.experimental import pallas as pl
from jax.experimental.pallas import tpu as pltpu
from jax.sharding import PartitionSpec as P

QUERY_HEADS = 16
KEY_VALUE_HEADS = 8
HEAD_DIMENSION = 64
GROUP = QUERY_HEADS // KEY_VALUE_HEADS
EPSILON = 1e-05
ROPE_BASE = 10000.0
NEGATIVE = -1e30
F32 = jnp.float32
BF16 = jnp.bfloat16
VMEM_LIMIT = 8 * 1024 * 1024


def iota(shape, dim):
    return lax.broadcasted_iota(jnp.int32, shape, dim)


def merge_rows(blocks):
    return jnp.concatenate(blocks, axis=0)


def in_vmem(x):
    return pltpu.with_memory_space_constraint(x, pltpu.VMEM)


def whole(memory_space=pltpu.VMEM):
    return pl.BlockSpec(memory_space=memory_space)


def call(kernel, outs, operands, name, scratch=(), smem=(), hbm_out=False):
    args = [x if i in smem else in_vmem(x) for i, x in enumerate(operands)]
    return pl.pallas_call(
        kernel,
        out_shape=[
            jax.ShapeDtypeStruct(s, d) if hbm_out else pltpu.VMEM(s, d) for s, d in outs
        ],
        in_specs=[whole(pltpu.SMEM if i in smem else pltpu.VMEM) for i in range(len(args))],
        out_specs=[whole() for _ in outs],
        scratch_shapes=list(scratch),
        compiler_params=pltpu.CompilerParams(vmem_limit_bytes=VMEM_LIMIT),
        name=name,
    )(*args)


def project_kernel(requests, steps, lengths, hidden, weight, out):
    device = lax.axis_index("tp")
    devices = lax.axis_size("tp")
    x = merge_rows([hidden[b].astype(F32) for b in range(requests)])
    normed = (x * lax.rsqrt(jnp.mean(x * x, axis=-1, keepdims=True) + EPSILON)).astype(BF16)
    y = lax.dot_general(normed, weight[...], (((1,), (1,)), ((), ())), preferred_element_type=F32)
    y = y.astype(BF16).astype(F32)
    tokens, width = y.shape
    row = iota((tokens, 128), 0)
    lane = iota((tokens, 128), 1)
    position = jnp.zeros((tokens, 128), jnp.int32)
    for b in range(requests):
        position = jnp.where(row // steps == b, lengths[b] + row - b * steps, position)
    half = HEAD_DIMENSION // 2
    rates = jnp.exp((lane % half).astype(F32) * (-2.0 / HEAD_DIMENSION * 9.210340371976184))
    angles = position.astype(F32) * rates
    turned = device < devices * 3 // 4
    cosine = jnp.where(turned, jnp.cos(angles), 1.0)
    sine = jnp.where(turned, jnp.sin(angles), 0.0)
    first = lane % HEAD_DIMENSION < half
    sine = jnp.where(first, -sine, sine)
    parts = []
    for k in range(width // 128):
        v = y[:, k * 128 : (k + 1) * 128]
        other = jnp.where(first, pltpu.roll(v, 128 - half, 1), pltpu.roll(v, half, 1))
        parts.append(v * cosine + other * sine)
    a, b = parts
    low = lane < HEAD_DIMENSION
    even = jnp.where(low, a, pltpu.roll(b, HEAD_DIMENSION, 1))
    odd = jnp.where(low, pltpu.roll(a, HEAD_DIMENSION, 1), b)
    rows = []
    for r in range(requests):
        rows += [even[r * steps : (r + 1) * steps], odd[r * steps : (r + 1) * steps]]
    query = merge_rows(rows)
    plain = merge_rows([a, b])
    out[...] = jnp.where(device < devices // 2, query, plain).astype(BF16)


def fold(x, rows, lanes):
    groups = lanes // HEAD_DIMENSION
    lane = iota((rows, lanes), 1) // HEAD_DIMENSION
    total = jnp.broadcast_to(x[0:rows], (rows, lanes))
    for g in range(1, groups):
        total = jnp.where(lane == g, jnp.broadcast_to(x[g * rows : (g + 1) * rows], (rows, lanes)), total)
    return total


def spread(x, groups):
    rows, lanes = x.shape
    lane = iota((rows, lanes), 1) // HEAD_DIMENSION
    return merge_rows([jnp.where(lane == g, x, 0.0) for g in range(groups)]).astype(BF16)


def pack_stats(peak, total):
    lane = iota(peak.shape, 1)
    return jnp.where(lane % HEAD_DIMENSION < HEAD_DIMENSION // 2, peak, total)


def unpack_stats(stats):
    half = HEAD_DIMENSION // 2
    low = iota(stats.shape, 1) % HEAD_DIMENSION < half
    return (
        jnp.where(low, stats, pltpu.roll(stats, half, 1)),
        jnp.where(low, pltpu.roll(stats, stats.shape[1] - half, 1), stats),
    )


def soft(scores, live, values):
    masked = jnp.where(live, scores, NEGATIVE)
    peak = jnp.max(masked, axis=-1, keepdims=True)
    weights = jnp.where(live, jnp.exp(masked - peak), 0.0)
    total = jnp.sum(weights, axis=-1, keepdims=True)
    return peak, total, jnp.dot(weights.astype(BF16), values, preferred_element_type=F32)


def attend_kernel(
    requests, steps, lengths, own, sibling, keys, values, out0, out1, out2, out3, fresh, heads, blocks
):
    device = lax.axis_index("tp")
    chip, core = device // 2, device % 2
    chips = own.shape[0]
    for k in range(chips):
        heads[2 * (chip ^ k) + core] = own[k]
        heads[2 * (chip ^ k) + 1 - core] = sibling[k]
    rows = steps * GROUP
    count = keys.shape[1]
    scale = HEAD_DIMENSION**-0.5
    query = jnp.concatenate([heads[t].astype(F32) for t in range(chips)], axis=1) * scale
    lanes = query.shape[1]
    groups = lanes // HEAD_DIMENSION
    position = device * count + iota((groups * rows, count), 1)
    for r in range(requests):
        q = spread(query[r * rows : (r + 1) * rows], groups)
        scores = lax.dot_general(q, keys[r], (((1,), (1,)), ((), ())), preferred_element_type=F32)
        peak, total, summed = soft(scores, position < lengths[r], values[r])
        summed = fold(summed, rows, lanes)
        stats = pack_stats(fold(peak, rows, lanes), fold(total, rows, lanes))
        for k in range(chips):
            blocks[k, r * rows : (r + 1) * rows, :] = summed[:, k * 128 : (k + 1) * 128]
            blocks[k, (requests + r) * rows : (requests + r + 1) * rows, :] = stats[:, k * 128 : (k + 1) * 128]
    for k, out in enumerate((out0, out1, out2, out3)):
        out[...] = blocks[chip ^ k]
    tokens = requests * steps
    place = chips + chip // 2
    second = chip % 2 == 1
    pick = lambda x: jnp.where(second, x[tokens:].astype(F32), x[:tokens].astype(F32)).astype(BF16)
    new_keys = pick(heads[place])
    new_values = pick(heads[place + chips // 2])
    q = spread(heads[chip].astype(F32) * scale, 2)
    scores = lax.dot_general(q, new_keys, (((1,), (1,)), ((), ())), preferred_element_type=F32)
    shape = scores.shape
    row, column = iota(shape, 0) % (requests * rows), iota(shape, 1)
    live = (row // rows == column // steps) & (column % steps <= row % steps)
    peak, total, summed = soft(scores, live, new_values)
    n = requests * rows
    fresh[0:n] = fold(summed, n, 128)
    fresh[n : 2 * n] = pack_stats(fold(peak, n, 128), fold(total, n, 128))


def join(a, b):
    peak = jnp.maximum(a[0], b[0])
    left, right = jnp.exp(a[0] - peak), jnp.exp(b[0] - peak)
    return peak, a[1] * left + b[1] * right, a[2] * left + b[2] * right


def read_part(ref):
    n = ref.shape[0] // 2
    return (*unpack_stats(ref[n:]), ref[0:n])


def join_kernel(a, b, c, d, out):
    peak, total, summed = join(join(read_part(a), read_part(b)), join(read_part(c), read_part(d)))
    n = summed.shape[0]
    out[0:n] = summed
    out[n:] = pack_stats(peak, total)


def output_kernel(requests, steps, own, sibling, fresh, weight, sibling_weight, out):
    core = lax.axis_index("tp") % 2
    _, total, summed = join(join(read_part(own), read_part(sibling)), read_part(fresh))
    attended = summed / total
    rows = steps * GROUP
    heads = []
    for j in range(GROUP):
        heads.append(merge_rows([attended[r * rows + j * steps : r * rows + (j + 1) * steps] for r in range(requests)]))
    low = iota(heads[0].shape, 1) < HEAD_DIMENSION
    zero = jnp.where(low, heads[0], pltpu.roll(heads[1], HEAD_DIMENSION, 1))
    one = jnp.where(low, pltpu.roll(heads[0], HEAD_DIMENSION, 1), heads[1])
    mine = jnp.where(core == 0, zero, one).astype(BF16)
    theirs = jnp.where(core == 0, one, zero).astype(BF16)
    out[...] = jnp.dot(mine, weight[...], preferred_element_type=F32) + jnp.dot(
        theirs, sibling_weight[...], preferred_element_type=F32
    )


def expert_kernel(requests, hidden, a, b, c, d, ids, shares, gate_up, down, out, residual_out):
    device = lax.axis_index("tp")
    x = merge_rows([hidden[r].astype(F32) for r in range(requests)])
    residual = x + ((a[...] + b[...]) + (c[...] + d[...]))
    residual_out[...] = residual
    normed = (
        residual * lax.rsqrt(jnp.mean(residual * residual, axis=-1, keepdims=True) + EPSILON)
    ).astype(BF16)
    chosen = merge_rows([ids[r] for r in range(requests)])
    share = merge_rows([shares[r].astype(F32) for r in range(requests)]) * (1.0 / 65536.0)
    experts, _, width = gate_up.shape
    total = None
    for e in range(experts):
        united = jnp.dot(normed, gate_up[e], preferred_element_type=F32)
        gate, up = united[:, : width // 2], united[:, width // 2 :]
        active = (gate / (1.0 + jnp.exp(-gate)) * up).astype(BF16)
        outcome = jnp.dot(active, down[e], preferred_element_type=F32)
        factor = jnp.sum(jnp.where(chosen == device * experts + e, share, 0.0), axis=-1, keepdims=True)
        total = factor * outcome if total is None else total + factor * outcome
    out[...] = total.astype(BF16)


def final_kernel(requests, steps, residual, a, b, c, d, out):
    mixture = (a[...].astype(F32) + b[...].astype(F32)) + (c[...].astype(F32) + d[...].astype(F32))
    result = residual[...] + mixture
    for r in range(requests):
        out[r] = result[r * steps : (r + 1) * steps].astype(BF16)


def other_chip(x, k, devices):
    return lax.ppermute(x, "tp", [(i, i ^ (2 * k)) for i in range(devices)])


def other_core(x, devices):
    return lax.ppermute(x, "tp", [(i, i ^ 1) for i in range(devices)])


def fast_device(
    hidden_states,
    lengths,
    qkv_weight,
    rotated_key_cache,
    earlier_value_cache,
    out_weight,
    expert_ids,
    combine_weights,
    gate_up_weight,
    down_weight,
):
    requests, steps, model_width = hidden_states.shape
    tokens = requests * steps
    devices = lax.axis_size("tp")
    chips = devices // 2
    rows = tokens * GROUP
    sibling_weight = other_core(out_weight, devices)
    (heads,) = call(
        functools.partial(project_kernel, requests, steps),
        [((rows, 128), BF16)],
        [lengths, hidden_states, qkv_weight],
        "project",
        smem=(0,),
    )
    gathered = jnp.stack([heads] + [other_chip(heads, k, devices) for k in range(1, chips)])
    parts = call(
        functools.partial(attend_kernel, requests, steps),
        [((2 * rows, 128), F32)] * (chips + 1),
        [lengths, gathered, other_core(gathered, devices), rotated_key_cache, earlier_value_cache],
        "attend",
        scratch=[pltpu.VMEM((devices, rows, 128), BF16), pltpu.VMEM((chips, 2 * rows, 128), F32)],
        smem=(0,),
    )
    fresh = parts[chips]
    arrived = [parts[0]] + [other_chip(parts[k], k, devices) for k in range(1, chips)]
    (joined,) = call(join_kernel, [((2 * rows, 128), F32)], arrived, "join")
    (projected,) = call(
        functools.partial(output_kernel, requests, steps),
        [((tokens, model_width), F32)],
        [joined, other_core(joined, devices), fresh, out_weight, sibling_weight],
        "output",
    )
    projections = [projected] + [other_chip(projected, k, devices) for k in range(1, chips)]
    mixture, residual = call(
        functools.partial(expert_kernel, requests),
        [((tokens, model_width), BF16), ((tokens, model_width), F32)],
        [hidden_states, *projections, expert_ids, combine_weights, gate_up_weight, down_weight],
        "experts",
    )
    mixture = (mixture.astype(F32) + other_core(mixture, devices).astype(F32)).astype(BF16)
    mixtures = [mixture] + [other_chip(mixture, k, devices) for k in range(1, chips)]
    (result,) = call(
        functools.partial(final_kernel, requests, steps),
        [(hidden_states.shape, BF16)],
        [residual, *mixtures],
        "final",
        hbm_out=True,
    )
    return result


def merged(part, axis, combine):
    gathered = jax.tree.map(lambda a: lax.all_gather(a, axis), part)

    def take(source):
        return jax.tree.map(lambda a: lax.dynamic_index_in_dim(a, source, 0, False), gathered)

    return lax.fori_loop(
        1, lax.axis_size(axis), lambda source, state: combine(state, take(source)), take(0)
    )


def rms_rows(value_rows):
    return value_rows * lax.rsqrt(
        jnp.mean(value_rows * value_rows, axis=-1, keepdims=True) + EPSILON
    )


def apply_rotation(value_rows, position_index):
    half_width = value_rows.shape[-1] // 2
    rates = ROPE_BASE ** (-2.0 * jnp.arange(half_width, dtype=jnp.float32) / value_rows.shape[-1])
    angles = position_index[:, None, None] * rates
    cosine = jnp.cos(angles)
    sines = jnp.sin(angles)
    front_half = value_rows[..., :half_width]
    back_half = value_rows[..., half_width:]
    return jnp.concatenate(
        [front_half * cosine - back_half * sines, back_half * cosine + front_half * sines], axis=-1
    )


def join_parts(earlier, later):
    highest = jnp.maximum(earlier[0], later[0])
    scale_earlier = jnp.exp(earlier[0] - highest)
    scale_later = jnp.exp(later[0] - highest)
    weight_sum = earlier[1] * scale_earlier + later[1] * scale_later
    value_sum = earlier[2] * scale_earlier[..., None] + later[2] * scale_later[..., None]
    return (highest, weight_sum, value_sum)


def to_columns(value_rows, step_number, group_count):
    request_list, kv_heads, _, head_size = value_rows.shape
    return (
        value_rows.reshape(request_list, kv_heads, step_number, group_count, head_size)
        .transpose(0, 2, 1, 3, 4)
        .reshape(request_list * step_number, kv_heads * group_count * head_size)
    )


def expert_terms(normed, chosen, shares, gate_up_weight, down_weight, first_expert):
    ff_width = down_weight.shape[1]
    united_out = jnp.einsum(
        "nd,edf->enf", normed, gate_up_weight, preferred_element_type=jnp.float32
    )
    activation = (jax.nn.silu(united_out[..., :ff_width]) * united_out[..., ff_width:]).astype(
        jnp.bfloat16
    )
    outcome = jnp.einsum(
        "enf,efd->end", activation, down_weight, preferred_element_type=jnp.float32
    )
    owners = first_expert + jnp.arange(gate_up_weight.shape[0], dtype=jnp.int32)
    factors = jnp.sum(
        jnp.where(chosen[None, :, :] == owners[:, None, None], shares[None, :, :], 0.0), axis=-1
    )
    return jnp.sum(factors[:, :, None] * outcome, axis=0)


def general_device(
    hidden_states,
    lengths,
    qkv_weight,
    rotated_key_cache,
    earlier_value_cache,
    out_weight,
    expert_ids,
    combine_weights,
    gate_up_weight,
    down_weight,
):
    request_list, step_number, model_width = hidden_states.shape
    token_rows = request_list * step_number
    group_count = QUERY_HEADS // KEY_VALUE_HEADS
    query_total_width = QUERY_HEADS * HEAD_DIMENSION
    key_value_width = KEY_VALUE_HEADS * HEAD_DIMENSION
    score_scale = HEAD_DIMENSION ** (-0.5)
    inputs_flat = hidden_states.reshape(token_rows, model_width)
    normed = rms_rows(inputs_flat.astype(jnp.float32)).astype(jnp.bfloat16)
    projected_part = lax.dot_general(
        qkv_weight, normed, (((1,), (1,)), ((), ())), preferred_element_type=jnp.float32
    ).astype(jnp.bfloat16)
    projected_all = lax.all_gather(projected_part, "tp", axis=0, tiled=True)
    query_key_value_rows = projected_all.T
    position_index = (
        (lengths[:, None] + jnp.arange(step_number, dtype=jnp.int32)[None, :])
        .reshape(token_rows)
        .astype(jnp.float32)
    )
    query_rows = apply_rotation(
        query_key_value_rows[:, :query_total_width]
        .reshape(token_rows, QUERY_HEADS, HEAD_DIMENSION)
        .astype(jnp.float32),
        position_index,
    ).astype(jnp.bfloat16)
    fresh_keys = apply_rotation(
        query_key_value_rows[:, query_total_width : query_total_width + key_value_width]
        .reshape(token_rows, KEY_VALUE_HEADS, HEAD_DIMENSION)
        .astype(jnp.float32),
        position_index,
    ).astype(jnp.bfloat16)
    fresh_values = query_key_value_rows[:, query_total_width + key_value_width :].reshape(
        request_list, step_number, KEY_VALUE_HEADS, HEAD_DIMENSION
    )
    grouped_rows = (
        query_rows.reshape(request_list, step_number, KEY_VALUE_HEADS, group_count, HEAD_DIMENSION)
        .transpose(0, 2, 1, 3, 4)
        .reshape(request_list, KEY_VALUE_HEADS, step_number * group_count, HEAD_DIMENSION)
    )
    cache_extent = rotated_key_cache.shape[1]
    stored_keys = rotated_key_cache.reshape(
        request_list, cache_extent, KEY_VALUE_HEADS, HEAD_DIMENSION
    )
    stored_values = earlier_value_cache.reshape(
        request_list, cache_extent, KEY_VALUE_HEADS, HEAD_DIMENSION
    )
    scores = (
        jnp.einsum("bgqd,bcgd->bgqc", grouped_rows, stored_keys, preferred_element_type=jnp.float32)
        * score_scale
    )
    start_pos = lax.axis_index("tp") * cache_extent
    live_rows = (start_pos + jnp.arange(cache_extent, dtype=jnp.int32))[None, :] < lengths[:, None]
    live_mask = live_rows[:, None, None, :]
    masked = jnp.where(live_mask, scores, NEGATIVE)
    highest = jnp.max(masked, axis=-1)
    weights = jnp.where(live_mask, jnp.exp(masked - highest[..., None]), 0.0)
    weight_sum = jnp.sum(weights, axis=-1)
    value_sum = jnp.einsum(
        "bgqc,bcgd->bgqd",
        weights.astype(jnp.bfloat16),
        stored_values,
        preferred_element_type=jnp.float32,
    )
    feature_rows = out_weight.shape[0]
    column_begin = lax.axis_index("tp") * feature_rows
    top_score, total_all, sum_all = merged((highest, weight_sum, value_sum), "tp", join_parts)
    grouped_keys = fresh_keys.reshape(request_list, step_number, KEY_VALUE_HEADS, HEAD_DIMENSION)
    new_scores = (
        jnp.einsum(
            "bgqd,bsgd->bgqs", grouped_rows, grouped_keys, preferred_element_type=jnp.float32
        )
        * score_scale
    )
    query_step = jnp.arange(step_number * group_count, dtype=jnp.int32) // group_count
    causal = jnp.arange(step_number, dtype=jnp.int32)[None, :] <= query_step[:, None]
    new_masked = jnp.where(causal, new_scores, NEGATIVE)
    final_peak = jnp.maximum(top_score, jnp.max(new_masked, axis=-1))
    new_weights = jnp.where(causal, jnp.exp(new_masked - final_peak[..., None]), 0.0)
    carried = jnp.exp(top_score - final_peak)
    denominator = total_all * carried + jnp.sum(new_weights, axis=-1)
    new_part = jnp.einsum(
        "bgqs,bsgd->bgqd",
        new_weights.astype(jnp.bfloat16),
        fresh_values,
        preferred_element_type=jnp.float32,
    )
    numerator = sum_all * carried[..., None] + new_part
    attended = to_columns(numerator / denominator[..., None], step_number, group_count).astype(
        jnp.bfloat16
    )
    attended_part = lax.dynamic_slice_in_dim(attended, column_begin, feature_rows, 1)
    first_expert = lax.axis_index("tp") * gate_up_weight.shape[0]
    chosen = expert_ids.reshape(token_rows, -1)
    shares = combine_weights.reshape(token_rows, -1).astype(jnp.float32) / 65536.0
    head_terms = jnp.dot(attended_part, out_weight, preferred_element_type=jnp.float32)
    projected_rows = lax.psum(head_terms, "tp")
    residual = inputs_flat.astype(jnp.float32) + projected_rows
    normed_second = rms_rows(residual).astype(jnp.bfloat16)
    mixture = lax.psum(
        expert_terms(
            normed_second, chosen, shares, gate_up_weight, down_weight, first_expert
        ).astype(jnp.bfloat16),
        "tp",
    ).astype(jnp.float32)
    final_result = (residual + mixture).astype(jnp.bfloat16)
    return final_result.reshape(request_list, step_number, model_width)


def solution(mesh):
    in_specs = (
        P("req", None, None),
        P("req"),
        P("tp", None),
        P("req", "tp", None),
        P("req", "tp", None),
        P("tp", None),
        P("req", None, None),
        P("req", None, None),
        P("tp", None, None),
        P("tp", None, None),
    )
    out_specs = P("req", None, None)
    per_device = fast_device if mesh.shape["tp"] == 8 else general_device
    return jax.shard_map(
        per_device, mesh=mesh, in_specs=in_specs, out_specs=out_specs, check_vma=False
    )
```

```python
import functools

import jax
import jax.numpy as jnp
from jax import lax
from jax.experimental import pallas as pl
from jax.experimental.pallas import tpu as pltpu
from jax.sharding import PartitionSpec as P

QUERY_HEADS = 16
KEY_VALUE_HEADS = 8
HEAD_DIMENSION = 64
GROUP = QUERY_HEADS // KEY_VALUE_HEADS
EPSILON = 1e-05
ROPE_BASE = 10000.0
NEGATIVE = -1e30
F32 = jnp.float32
BF16 = jnp.bfloat16
VMEM_LIMIT = 16 * 1024 * 1024
ORDER = ((3, 2, 1),) * 4
COST = (8_000_000, 6_000_000, 1_000_000, 12_000_000)


def iota(shape, dim):
    return lax.broadcasted_iota(jnp.int32, shape, dim)


def merge_rows(blocks):
    return jnp.concatenate(blocks, axis=0)


def on(space):
    return pl.BlockSpec(memory_space=space)


def call(kernel, outs, operands, name, stay=(), scratch=(), hbm_out=False, cost=0):
    operands = [
        pltpu.with_memory_space_constraint(x, pltpu.HBM) if i in stay else x for i, x in enumerate(operands)
    ]
    return pl.pallas_call(
        kernel,
        out_shape=[
            jax.ShapeDtypeStruct(s, d) if hbm_out else pltpu.VMEM(s, d) for s, d in outs
        ],
        in_specs=[on(pltpu.HBM if i in stay else pltpu.VMEM) for i in range(len(operands))],
        out_specs=[on(pltpu.VMEM) for _ in outs],
        scratch_shapes=list(scratch),
        compiler_params=pltpu.CompilerParams(vmem_limit_bytes=VMEM_LIMIT),
        cost_estimate=pl.CostEstimate(flops=0, bytes_accessed=cost, transcendentals=0),
        name=name,
    )(*operands)


def start_all(pairs, semaphores):
    copies = [
        pltpu.make_async_copy(source, target, semaphores.at[i]) for i, (source, target) in enumerate(pairs)
    ]
    for copy in copies:
        copy.start()
    return copies


def project_kernel(
    lengths_in,
    hidden_in,
    weight_in,
    keys_in,
    values_in,
    out_weight_in,
    ids_in,
    shares_in,
    out,
    limits,
    inputs,
    keys,
    values,
    out_weight,
    ids,
    shares,
    lengths,
    hidden,
    weight,
    semaphores,
):
    copies = start_all(
        [
            (lengths_in, lengths),
            (hidden_in, hidden),
            (weight_in, weight),
            (keys_in, keys),
            (values_in, values),
            (out_weight_in, out_weight),
            (ids_in, ids),
            (shares_in, shares),
        ],
        semaphores,
    )
    requests, steps, _ = hidden.shape
    device = lax.axis_index("tp")
    devices = lax.axis_size("tp")
    copies[1].wait()
    x = merge_rows([hidden[b].astype(F32) for b in range(requests)])
    inputs[...] = x
    normed = (x * lax.rsqrt(jnp.mean(x * x, axis=-1, keepdims=True) + EPSILON)).astype(BF16)
    copies[0].wait()
    tokens = requests * steps
    row = iota((tokens, 128), 0)
    lane = iota((tokens, 128), 1)
    position = jnp.zeros((tokens, 128), jnp.int32)
    for b in range(requests):
        position = jnp.where(row // steps == b, lengths[b] + row - b * steps, position)
        limits[b] = jnp.full(limits.shape[1:], lengths[b], jnp.int32)
    half = HEAD_DIMENSION // 2
    rates = jnp.exp((lane % half).astype(F32) * (-2.0 / HEAD_DIMENSION * 9.210340371976184))
    angles = position.astype(F32) * rates
    turned = device < devices * 3 // 4
    cosine = jnp.where(turned, jnp.cos(angles), 1.0)
    sine = jnp.where(turned, jnp.sin(angles), 0.0)
    first = lane % HEAD_DIMENSION < half
    sine = jnp.where(first, -sine, sine)
    copies[2].wait()
    y = lax.dot_general(normed, weight[...], (((1,), (1,)), ((), ())), preferred_element_type=F32)
    y = y.astype(BF16).astype(F32)
    parts = []
    for k in range(y.shape[1] // 128):
        v = y[:, k * 128 : (k + 1) * 128]
        other = jnp.where(first, pltpu.roll(v, 128 - half, 1), pltpu.roll(v, half, 1))
        parts.append(v * cosine + other * sine)
    a, b = parts
    low = lane < HEAD_DIMENSION
    even = jnp.where(low, a, pltpu.roll(b, HEAD_DIMENSION, 1))
    odd = jnp.where(low, pltpu.roll(a, HEAD_DIMENSION, 1), b)
    rows = []
    for r in range(requests):
        rows += [even[r * steps : (r + 1) * steps], odd[r * steps : (r + 1) * steps]]
    query = merge_rows(rows)
    plain = merge_rows([a, b])
    out[...] = jnp.where(device < devices // 2, query, plain).astype(BF16)
    for copy in copies[3:]:
        copy.wait()


def fetch_kernel(after, source, target, semaphores):
    for copy in start_all([(source.at[i], target.at[i]) for i in range(target.shape[0])], semaphores):
        copy.wait()


def fetch(x, after, name):
    (there,) = call(
        fetch_kernel,
        [(x.shape, x.dtype)],
        [after, x],
        name,
        stay=(1,),
        scratch=[pltpu.SemaphoreType.DMA((x.shape[0],))],
        cost=x.size * 2,
    )
    return there


def fold(x, rows, lanes):
    groups = lanes // HEAD_DIMENSION
    lane = iota((rows, lanes), 1) // HEAD_DIMENSION
    total = jnp.broadcast_to(x[0:rows], (rows, lanes))
    for g in range(1, groups):
        total = jnp.where(lane == g, jnp.broadcast_to(x[g * rows : (g + 1) * rows], (rows, lanes)), total)
    return total


def spread(x, groups):
    rows, lanes = x.shape
    lane = iota((rows, lanes), 1) // HEAD_DIMENSION
    return merge_rows([jnp.where(lane == g, x, 0.0) for g in range(groups)]).astype(BF16)


def pack_stats(peak, total):
    lane = iota(peak.shape, 1)
    return jnp.where(lane % HEAD_DIMENSION < HEAD_DIMENSION // 2, peak, total)


def unpack_stats(stats):
    half = HEAD_DIMENSION // 2
    low = iota(stats.shape, 1) % HEAD_DIMENSION < half
    return (
        jnp.where(low, stats, pltpu.roll(stats, half, 1)),
        jnp.where(low, pltpu.roll(stats, stats.shape[1] - half, 1), stats),
    )


def soft(scores, live, values):
    masked = jnp.where(live, scores, NEGATIVE)
    peak = jnp.max(masked, axis=-1, keepdims=True)
    weights = jnp.where(live, jnp.exp(masked - peak), 0.0)
    total = jnp.sum(weights, axis=-1, keepdims=True)
    return peak, total, jnp.dot(weights.astype(BF16), values, preferred_element_type=F32)


def attend_kernel(
    steps,
    limits,
    own,
    sibling,
    keys,
    values,
    out0,
    out1,
    out2,
    out3,
    fresh,
    heads,
    blocks,
):
    requests = keys.shape[0]
    device = lax.axis_index("tp")
    chip, core = device // 2, device % 2
    chips = own.shape[0]
    for k in range(chips):
        heads[2 * (chip ^ k) + core] = own[k]
        heads[2 * (chip ^ k) + 1 - core] = sibling[k]
    rows = steps * GROUP
    count = keys.shape[1]
    scale = HEAD_DIMENSION**-0.5
    query = jnp.concatenate([heads[t].astype(F32) for t in range(chips)], axis=1) * scale
    lanes = query.shape[1]
    groups = lanes // HEAD_DIMENSION
    position = device * count + iota((groups * rows, count), 1)
    for r in range(requests):
        q = spread(query[r * rows : (r + 1) * rows], groups)
        scores = lax.dot_general(q, keys[r], (((1,), (1,)), ((), ())), preferred_element_type=F32)
        peak, total, summed = soft(scores, position < limits[r, 0:1], values[r])
        summed = fold(summed, rows, lanes)
        stats = pack_stats(fold(peak, rows, lanes), fold(total, rows, lanes))
        for k in range(chips):
            blocks[k, r * rows : (r + 1) * rows, :] = summed[:, k * 128 : (k + 1) * 128]
            blocks[k, (requests + r) * rows : (requests + r + 1) * rows, :] = stats[:, k * 128 : (k + 1) * 128]
    for k, out in enumerate((out0, out1, out2, out3)):
        out[...] = blocks[chip ^ k]
    tokens = requests * steps
    place = chips + chip // 2
    second = chip % 2 == 1
    pick = lambda x: jnp.where(second, x[tokens:].astype(F32), x[:tokens].astype(F32)).astype(BF16)
    new_keys = pick(heads[place])
    new_values = pick(heads[place + chips // 2])
    q = spread(heads[chip].astype(F32) * scale, 2)
    scores = lax.dot_general(q, new_keys, (((1,), (1,)), ((), ())), preferred_element_type=F32)
    shape = scores.shape
    row, column = iota(shape, 0) % (requests * rows), iota(shape, 1)
    live = (row // rows == column // steps) & (column % steps <= row % steps)
    peak, total, summed = soft(scores, live, new_values)
    n = requests * rows
    fresh[0:n] = fold(summed, n, 128)
    fresh[n : 2 * n] = pack_stats(fold(peak, n, 128), fold(total, n, 128))


def join(a, b):
    peak = jnp.maximum(a[0], b[0])
    left, right = jnp.exp(a[0] - peak), jnp.exp(b[0] - peak)
    return peak, a[1] * left + b[1] * right, a[2] * left + b[2] * right


def read_part(ref):
    n = ref.shape[0] // 2
    return (*unpack_stats(ref[n:]), ref[0:n])


def join_kernel(order, a, b, c, d, fetched, out):
    a, b, c, d = sort_chips(order, a, (b, c, d))
    peak, total, summed = join(join(read_part(a), read_part(b)), join(read_part(c), read_part(d)))
    n = summed.shape[0]
    out[0:n] = summed
    out[n:] = pack_stats(peak, total)


def output_kernel(requests, steps, own, sibling, fresh, weight, sibling_weight, out):
    core = lax.axis_index("tp") % 2
    _, total, summed = join(join(read_part(own), read_part(sibling)), read_part(fresh))
    attended = summed / total
    rows = steps * GROUP
    heads = []
    for j in range(GROUP):
        heads.append(merge_rows([attended[r * rows + j * steps : r * rows + (j + 1) * steps] for r in range(requests)]))
    low = iota(heads[0].shape, 1) < HEAD_DIMENSION
    zero = jnp.where(low, heads[0], pltpu.roll(heads[1], HEAD_DIMENSION, 1))
    one = jnp.where(low, pltpu.roll(heads[0], HEAD_DIMENSION, 1), heads[1])
    mine = jnp.where(core == 0, zero, one).astype(BF16)
    theirs = jnp.where(core == 0, one, zero).astype(BF16)
    projected = jnp.dot(mine, weight[...], preferred_element_type=F32) + jnp.dot(
        theirs, sibling_weight[...], preferred_element_type=F32
    )
    out[...] = projected.astype(BF16)


def sort_chips(order, first, parts):
    return [first] + [part for _, part in sorted(zip(order, parts), key=lambda pair: pair[0])]


def gather_kernel(order, a, b, c, d, fetched, out):
    for k, x in enumerate(sort_chips(order, a, (b, c, d))):
        out[k] = x[...]


def sum_chips(order, a, b, c, d):
    a, b, c, d = sort_chips(order, a, (b, c, d))
    return (a[...].astype(F32) + b[...].astype(F32)) + (c[...].astype(F32) + d[...].astype(F32))


def expert_kernel(order, inputs, a, b, c, d, ids, shares, gate_up, down, out, residual_out):
    device = lax.axis_index("tp")
    residual = inputs[...] + sum_chips(order, a, b, c, d)
    residual_out[...] = residual
    normed = (
        residual * lax.rsqrt(jnp.mean(residual * residual, axis=-1, keepdims=True) + EPSILON)
    ).astype(BF16)
    requests = ids.shape[0]
    chosen = merge_rows([ids[r] for r in range(requests)])
    share = merge_rows([shares[r].astype(F32) for r in range(requests)]) * (1.0 / 65536.0)
    experts = gate_up.shape[0]
    total = None
    for e in range(experts):
        united = jnp.dot(normed, gate_up[e], preferred_element_type=F32)
        width = united.shape[1] // 2
        gate, up = united[:, :width], united[:, width:]
        active = (gate / (1.0 + jnp.exp(-gate)) * up).astype(BF16)
        outcome = jnp.dot(active, down[e], preferred_element_type=F32)
        factor = jnp.sum(jnp.where(chosen == device * experts + e, share, 0.0), axis=-1, keepdims=True)
        total = factor * outcome if total is None else total + factor * outcome
    out[...] = total.astype(BF16)


def final_kernel(order, requests, steps, residual, a, b, c, d, out):
    result = residual[...] + sum_chips(order, a, b, c, d)
    for r in range(requests):
        out[r] = result[r * steps : (r + 1) * steps].astype(BF16)


def other_chip(x, k, devices):
    return lax.ppermute(x, "tp", [(i, i ^ (2 * k)) for i in range(devices)])


def to_chips(parts, devices, order):
    return [parts[0]] + [other_chip(parts[k], k, devices) for k in order]


def other_core(x, devices):
    return lax.ppermute(x, "tp", [(i, i ^ 1) for i in range(devices)])


def fast_device(
    hidden_states,
    lengths,
    qkv_weight,
    rotated_key_cache,
    earlier_value_cache,
    out_weight,
    expert_ids,
    combine_weights,
    gate_up_weight,
    down_weight,
):
    requests, steps, model_width = hidden_states.shape
    tokens = requests * steps
    devices = lax.axis_size("tp")
    chips = devices // 2
    rows = tokens * GROUP
    sibling_weight = other_core(out_weight, devices)
    copied = [rotated_key_cache, earlier_value_cache, out_weight, expert_ids, combine_weights]
    heads, limits, inputs, keys, values, own_weight, ids, shares = call(
        project_kernel,
        [((rows, 128), BF16), ((requests, 8, 128), jnp.int32), ((tokens, model_width), F32)]
        + [(x.shape, x.dtype) for x in copied],
        [lengths, hidden_states, qkv_weight, *copied],
        "project",
        cost=COST[0],
        stay=range(8),
        scratch=[
            pltpu.SMEM(lengths.shape, jnp.int32),
            pltpu.VMEM(hidden_states.shape, BF16),
            pltpu.VMEM(qkv_weight.shape, BF16),
            pltpu.SemaphoreType.DMA((8,)),
        ],
    )
    gate_up = fetch(gate_up_weight, heads, "fetch_gate_up")
    (gathered,) = call(
        functools.partial(gather_kernel, ORDER[0]),
        [((chips, rows, 128), BF16)],
        [*to_chips([heads] * chips, devices, ORDER[0]), gate_up],
        "gather",
    )
    parts = call(
        functools.partial(attend_kernel, steps),
        [((2 * rows, 128), F32)] * (chips + 1),
        [limits, gathered, other_core(gathered, devices), keys, values],
        "attend",
        cost=COST[1],
        scratch=[
            pltpu.VMEM((devices, rows, 128), BF16),
            pltpu.VMEM((chips, 2 * rows, 128), F32),
        ],
    )
    fresh = parts[chips]
    down = fetch(down_weight, fresh, "fetch_down")
    arrived = to_chips(parts[:chips], devices, ORDER[1])
    (joined,) = call(functools.partial(join_kernel, ORDER[1]), [((2 * rows, 128), F32)], [*arrived, down], "join", cost=COST[2])
    (projected,) = call(
        functools.partial(output_kernel, requests, steps),
        [((tokens, model_width), BF16)],
        [joined, other_core(joined, devices), fresh, own_weight, sibling_weight],
        "output",
        cost=COST[2],
    )
    projections = to_chips([projected] * chips, devices, ORDER[2])
    mixture, residual = call(
        functools.partial(expert_kernel, ORDER[2]),
        [((tokens, model_width), BF16), ((tokens, model_width), F32)],
        [inputs, *projections, ids, shares, gate_up, down],
        "experts",
        cost=COST[3],
    )
    mixture = (mixture.astype(F32) + other_core(mixture, devices).astype(F32)).astype(BF16)
    mixtures = to_chips([mixture] * chips, devices, ORDER[3])
    (result,) = call(
        functools.partial(final_kernel, ORDER[3], requests, steps),
        [(hidden_states.shape, BF16)],
        [residual, *mixtures],
        "final",
        hbm_out=True,
    )
    return result


def merged(part, axis, combine):
    gathered = jax.tree.map(lambda a: lax.all_gather(a, axis), part)

    def take(source):
        return jax.tree.map(lambda a: lax.dynamic_index_in_dim(a, source, 0, False), gathered)

    return lax.fori_loop(
        1, lax.axis_size(axis), lambda source, state: combine(state, take(source)), take(0)
    )


def rms_rows(value_rows):
    return value_rows * lax.rsqrt(
        jnp.mean(value_rows * value_rows, axis=-1, keepdims=True) + EPSILON
    )


def apply_rotation(value_rows, position_index):
    half_width = value_rows.shape[-1] // 2
    rates = ROPE_BASE ** (-2.0 * jnp.arange(half_width, dtype=jnp.float32) / value_rows.shape[-1])
    angles = position_index[:, None, None] * rates
    cosine = jnp.cos(angles)
    sines = jnp.sin(angles)
    front_half = value_rows[..., :half_width]
    back_half = value_rows[..., half_width:]
    return jnp.concatenate(
        [front_half * cosine - back_half * sines, back_half * cosine + front_half * sines], axis=-1
    )


def join_parts(earlier, later):
    highest = jnp.maximum(earlier[0], later[0])
    scale_earlier = jnp.exp(earlier[0] - highest)
    scale_later = jnp.exp(later[0] - highest)
    weight_sum = earlier[1] * scale_earlier + later[1] * scale_later
    value_sum = earlier[2] * scale_earlier[..., None] + later[2] * scale_later[..., None]
    return (highest, weight_sum, value_sum)


def to_columns(value_rows, step_number, group_count):
    request_list, kv_heads, _, head_size = value_rows.shape
    return (
        value_rows.reshape(request_list, kv_heads, step_number, group_count, head_size)
        .transpose(0, 2, 1, 3, 4)
        .reshape(request_list * step_number, kv_heads * group_count * head_size)
    )


def expert_terms(normed, chosen, shares, gate_up_weight, down_weight, first_expert):
    ff_width = down_weight.shape[1]
    united_out = jnp.einsum(
        "nd,edf->enf", normed, gate_up_weight, preferred_element_type=jnp.float32
    )
    activation = (jax.nn.silu(united_out[..., :ff_width]) * united_out[..., ff_width:]).astype(
        jnp.bfloat16
    )
    outcome = jnp.einsum(
        "enf,efd->end", activation, down_weight, preferred_element_type=jnp.float32
    )
    owners = first_expert + jnp.arange(gate_up_weight.shape[0], dtype=jnp.int32)
    factors = jnp.sum(
        jnp.where(chosen[None, :, :] == owners[:, None, None], shares[None, :, :], 0.0), axis=-1
    )
    return jnp.sum(factors[:, :, None] * outcome, axis=0)


def general_device(
    hidden_states,
    lengths,
    qkv_weight,
    rotated_key_cache,
    earlier_value_cache,
    out_weight,
    expert_ids,
    combine_weights,
    gate_up_weight,
    down_weight,
):
    request_list, step_number, model_width = hidden_states.shape
    token_rows = request_list * step_number
    group_count = QUERY_HEADS // KEY_VALUE_HEADS
    query_total_width = QUERY_HEADS * HEAD_DIMENSION
    key_value_width = KEY_VALUE_HEADS * HEAD_DIMENSION
    score_scale = HEAD_DIMENSION ** (-0.5)
    inputs_flat = hidden_states.reshape(token_rows, model_width)
    normed = rms_rows(inputs_flat.astype(jnp.float32)).astype(jnp.bfloat16)
    projected_part = lax.dot_general(
        qkv_weight, normed, (((1,), (1,)), ((), ())), preferred_element_type=jnp.float32
    ).astype(jnp.bfloat16)
    projected_all = lax.all_gather(projected_part, "tp", axis=0, tiled=True)
    query_key_value_rows = projected_all.T
    position_index = (
        (lengths[:, None] + jnp.arange(step_number, dtype=jnp.int32)[None, :])
        .reshape(token_rows)
        .astype(jnp.float32)
    )
    query_rows = apply_rotation(
        query_key_value_rows[:, :query_total_width]
        .reshape(token_rows, QUERY_HEADS, HEAD_DIMENSION)
        .astype(jnp.float32),
        position_index,
    ).astype(jnp.bfloat16)
    fresh_keys = apply_rotation(
        query_key_value_rows[:, query_total_width : query_total_width + key_value_width]
        .reshape(token_rows, KEY_VALUE_HEADS, HEAD_DIMENSION)
        .astype(jnp.float32),
        position_index,
    ).astype(jnp.bfloat16)
    fresh_values = query_key_value_rows[:, query_total_width + key_value_width :].reshape(
        request_list, step_number, KEY_VALUE_HEADS, HEAD_DIMENSION
    )
    grouped_rows = (
        query_rows.reshape(request_list, step_number, KEY_VALUE_HEADS, group_count, HEAD_DIMENSION)
        .transpose(0, 2, 1, 3, 4)
        .reshape(request_list, KEY_VALUE_HEADS, step_number * group_count, HEAD_DIMENSION)
    )
    cache_extent = rotated_key_cache.shape[1]
    stored_keys = rotated_key_cache.reshape(
        request_list, cache_extent, KEY_VALUE_HEADS, HEAD_DIMENSION
    )
    stored_values = earlier_value_cache.reshape(
        request_list, cache_extent, KEY_VALUE_HEADS, HEAD_DIMENSION
    )
    scores = (
        jnp.einsum("bgqd,bcgd->bgqc", grouped_rows, stored_keys, preferred_element_type=jnp.float32)
        * score_scale
    )
    start_pos = lax.axis_index("tp") * cache_extent
    live_rows = (start_pos + jnp.arange(cache_extent, dtype=jnp.int32))[None, :] < lengths[:, None]
    live_mask = live_rows[:, None, None, :]
    masked = jnp.where(live_mask, scores, NEGATIVE)
    highest = jnp.max(masked, axis=-1)
    weights = jnp.where(live_mask, jnp.exp(masked - highest[..., None]), 0.0)
    weight_sum = jnp.sum(weights, axis=-1)
    value_sum = jnp.einsum(
        "bgqc,bcgd->bgqd",
        weights.astype(jnp.bfloat16),
        stored_values,
        preferred_element_type=jnp.float32,
    )
    feature_rows = out_weight.shape[0]
    column_begin = lax.axis_index("tp") * feature_rows
    top_score, total_all, sum_all = merged((highest, weight_sum, value_sum), "tp", join_parts)
    grouped_keys = fresh_keys.reshape(request_list, step_number, KEY_VALUE_HEADS, HEAD_DIMENSION)
    new_scores = (
        jnp.einsum(
            "bgqd,bsgd->bgqs", grouped_rows, grouped_keys, preferred_element_type=jnp.float32
        )
        * score_scale
    )
    query_step = jnp.arange(step_number * group_count, dtype=jnp.int32) // group_count
    causal = jnp.arange(step_number, dtype=jnp.int32)[None, :] <= query_step[:, None]
    new_masked = jnp.where(causal, new_scores, NEGATIVE)
    final_peak = jnp.maximum(top_score, jnp.max(new_masked, axis=-1))
    new_weights = jnp.where(causal, jnp.exp(new_masked - final_peak[..., None]), 0.0)
    carried = jnp.exp(top_score - final_peak)
    denominator = total_all * carried + jnp.sum(new_weights, axis=-1)
    new_part = jnp.einsum(
        "bgqs,bsgd->bgqd",
        new_weights.astype(jnp.bfloat16),
        fresh_values,
        preferred_element_type=jnp.float32,
    )
    numerator = sum_all * carried[..., None] + new_part
    attended = to_columns(numerator / denominator[..., None], step_number, group_count).astype(
        jnp.bfloat16
    )
    attended_part = lax.dynamic_slice_in_dim(attended, column_begin, feature_rows, 1)
    first_expert = lax.axis_index("tp") * gate_up_weight.shape[0]
    chosen = expert_ids.reshape(token_rows, -1)
    shares = combine_weights.reshape(token_rows, -1).astype(jnp.float32) / 65536.0
    head_terms = jnp.dot(attended_part, out_weight, preferred_element_type=jnp.float32)
    projected_rows = lax.psum(head_terms, "tp")
    residual = inputs_flat.astype(jnp.float32) + projected_rows
    normed_second = rms_rows(residual).astype(jnp.bfloat16)
    mixture = lax.psum(
        expert_terms(
            normed_second, chosen, shares, gate_up_weight, down_weight, first_expert
        ).astype(jnp.bfloat16),
        "tp",
    ).astype(jnp.float32)
    final_result = (residual + mixture).astype(jnp.bfloat16)
    return final_result.reshape(request_list, step_number, model_width)


def solution(mesh):
    in_specs = (
        P("req", None, None),
        P("req"),
        P("tp", None),
        P("req", "tp", None),
        P("req", "tp", None),
        P("tp", None),
        P("req", None, None),
        P("req", None, None),
        P("tp", None, None),
        P("tp", None, None),
    )
    out_specs = P("req", None, None)
    per_device = fast_device if mesh.shape["tp"] == 8 else general_device
    return jax.shard_map(
        per_device, mesh=mesh, in_specs=in_specs, out_specs=out_specs, check_vma=False
    )
```

```python
import functools

import jax
import jax.numpy as jnp
from jax import lax
from jax.experimental import pallas as pl
from jax.experimental.pallas import tpu as pltpu
from jax.sharding import PartitionSpec as P

QUERY_HEADS = 16
KEY_VALUE_HEADS = 8
HEAD_DIMENSION = 64
GROUP = QUERY_HEADS // KEY_VALUE_HEADS
EPSILON = 1e-05
ROPE_BASE = 10000.0
NEGATIVE = -1e30
F32 = jnp.float32
BF16 = jnp.bfloat16
VMEM_LIMIT = 16 * 1024 * 1024
SPLIT = (1, 3)
ORDER = ((1, 2, 3), (3, 2, 1), (1, 2, 3), (1, 2, 3))
COST = (8_000_000, 6_000_000, 1_000_000, 12_000_000)


def iota(shape, dim):
    return lax.broadcasted_iota(jnp.int32, shape, dim)


def merge_rows(blocks):
    return jnp.concatenate(blocks, axis=0)


def on(space):
    return pl.BlockSpec(memory_space=space)


def call(kernel, outs, operands, name, stay=(), scratch=(), hbm_out=False, cost=0):
    operands = [
        pltpu.with_memory_space_constraint(x, pltpu.HBM) if i in stay else x for i, x in enumerate(operands)
    ]
    return pl.pallas_call(
        kernel,
        out_shape=[
            jax.ShapeDtypeStruct(s, d) if hbm_out else pltpu.VMEM(s, d) for s, d in outs
        ],
        in_specs=[on(pltpu.HBM if i in stay else pltpu.VMEM) for i in range(len(operands))],
        out_specs=[on(pltpu.VMEM) for _ in outs],
        scratch_shapes=list(scratch),
        compiler_params=pltpu.CompilerParams(vmem_limit_bytes=VMEM_LIMIT),
        cost_estimate=pl.CostEstimate(flops=0, bytes_accessed=cost, transcendentals=0),
        name=name,
    )(*operands)


def start_all(pairs, semaphores):
    copies = [
        pltpu.make_async_copy(source, target, semaphores.at[i]) for i, (source, target) in enumerate(pairs)
    ]
    for copy in copies:
        copy.start()
    return copies


def project_kernel(
    lengths_in,
    hidden_in,
    weight_in,
    out,
    limits,
    inputs,
    lengths,
    hidden,
    weight,
    semaphores,
):
    copies = start_all(
        [
            (lengths_in, lengths),
            (hidden_in, hidden),
            (weight_in, weight),
        ],
        semaphores,
    )
    requests, steps, _ = hidden.shape
    device = lax.axis_index("tp")
    devices = lax.axis_size("tp")
    copies[1].wait()
    x = merge_rows([hidden[b].astype(F32) for b in range(requests)])
    inputs[...] = x
    normed = (x * lax.rsqrt(jnp.mean(x * x, axis=-1, keepdims=True) + EPSILON)).astype(BF16)
    copies[0].wait()
    tokens = requests * steps
    row = iota((tokens, 128), 0)
    lane = iota((tokens, 128), 1)
    position = jnp.zeros((tokens, 128), jnp.int32)
    for b in range(requests):
        position = jnp.where(row // steps == b, lengths[b] + row - b * steps, position)
        limits[b] = jnp.full(limits.shape[1:], lengths[b], jnp.int32)
    half = HEAD_DIMENSION // 2
    rates = jnp.exp((lane % half).astype(F32) * (-2.0 / HEAD_DIMENSION * 9.210340371976184))
    angles = position.astype(F32) * rates
    turned = device < devices * 3 // 4
    cosine = jnp.where(turned, jnp.cos(angles), 1.0)
    sine = jnp.where(turned, jnp.sin(angles), 0.0)
    first = lane % HEAD_DIMENSION < half
    sine = jnp.where(first, -sine, sine)
    copies[2].wait()
    y = lax.dot_general(normed, weight[...], (((1,), (1,)), ((), ())), preferred_element_type=F32)
    y = y.astype(BF16).astype(F32)
    parts = []
    for k in range(y.shape[1] // 128):
        v = y[:, k * 128 : (k + 1) * 128]
        other = jnp.where(first, pltpu.roll(v, 128 - half, 1), pltpu.roll(v, half, 1))
        parts.append(v * cosine + other * sine)
    a, b = parts
    low = lane < HEAD_DIMENSION
    even = jnp.where(low, a, pltpu.roll(b, HEAD_DIMENSION, 1))
    odd = jnp.where(low, pltpu.roll(a, HEAD_DIMENSION, 1), b)
    rows = []
    for r in range(requests):
        rows += [even[r * steps : (r + 1) * steps], odd[r * steps : (r + 1) * steps]]
    query = merge_rows(rows)
    plain = merge_rows([a, b])
    out[...] = jnp.where(device < devices // 2, query, plain).astype(BF16)


def fetch_kernel(pieces, beside, operands, *refs):
    count = len(pieces)
    inputs, sources = refs[:operands], refs[operands : operands + count]
    outs, semaphores = refs[operands + count : -1], refs[-1]
    targets = outs[:count]
    pairs = [
        (source.at[first + i], target.at[i])
        for source, target, (first, size) in zip(sources, targets, pieces)
        for i in range(size)
    ]
    copies = start_all(pairs, semaphores)
    if beside is not None:
        beside(*inputs, *outs[count:])
    for copy in copies:
        copy.wait()


def fetch(pieces, after, name, beside=None, outs=()):
    rows = [(first, size) for _, first, size in pieces]
    return call(
        functools.partial(fetch_kernel, rows, beside, len(after)),
        [((size,) + x.shape[1:], x.dtype) for x, _, size in pieces] + list(outs),
        [*after] + [x for x, _, _ in pieces],
        name,
        stay=range(len(after), len(after) + len(pieces)),
        scratch=[pltpu.SemaphoreType.DMA((sum(size for _, size in rows),))],
        cost=sum(x.size * 2 // x.shape[0] * size for x, _, size in pieces),
    )


def fold(x, rows, lanes):
    groups = lanes // HEAD_DIMENSION
    lane = iota((rows, lanes), 1) // HEAD_DIMENSION
    total = jnp.broadcast_to(x[0:rows], (rows, lanes))
    for g in range(1, groups):
        total = jnp.where(lane == g, jnp.broadcast_to(x[g * rows : (g + 1) * rows], (rows, lanes)), total)
    return total


def spread(x, groups):
    rows, lanes = x.shape
    lane = iota((rows, lanes), 1) // HEAD_DIMENSION
    return merge_rows([jnp.where(lane == g, x, 0.0) for g in range(groups)]).astype(BF16)


def pack_stats(peak, total):
    lane = iota(peak.shape, 1)
    return jnp.where(lane % HEAD_DIMENSION < HEAD_DIMENSION // 2, peak, total)


def unpack_stats(stats):
    half = HEAD_DIMENSION // 2
    low = iota(stats.shape, 1) % HEAD_DIMENSION < half
    return (
        jnp.where(low, stats, pltpu.roll(stats, half, 1)),
        jnp.where(low, pltpu.roll(stats, stats.shape[1] - half, 1), stats),
    )


def soft(scores, live):
    masked = jnp.where(live, scores, NEGATIVE)
    peak = jnp.max(masked, axis=-1, keepdims=True)
    weights = jnp.where(live, jnp.exp(masked - peak), 0.0)
    return peak, weights.astype(BF16), jnp.sum(weights, axis=-1, keepdims=True)


def attend_blocks(steps, limits, heads, core, keys, values, store):
    device = lax.axis_index("tp")
    requests, count, _ = keys.shape
    rows = steps * GROUP
    scale = HEAD_DIMENSION**-0.5
    pairs = [(s, r) for s in range(2) for r in range(requests)]
    columns = [pl.ds(pl.multiple_of((2 * s + core) * 128, 128), 128) for s in range(2)]
    scores = []
    for s, r in pairs:
        q = spread(heads[s, r * rows : (r + 1) * rows].astype(F32) * scale, GROUP)
        scores.append(
            lax.dot_general(q, keys[r, :, columns[s]], (((1,), (1,)), ((), ())), preferred_element_type=F32)
        )
    scores = merge_rows(scores)
    position = device * count + iota(scores.shape, 1)
    limit = merge_rows([limits[r, 0:rows] for _, r in pairs for _ in range(GROUP)])
    peak, weights, total = soft(scores, position < limit)
    n = GROUP * rows
    for i, (s, r) in enumerate(pairs):
        own = slice(i * n, (i + 1) * n)
        summed = jnp.dot(weights[own], values[r, :, columns[s]], preferred_element_type=F32)
        store(s, r * rows, fold(summed, rows, 128))
        store(s, (requests + r) * rows, pack_stats(fold(peak[own], rows, 128), fold(total[own], rows, 128)))


def attend_own_kernel(steps, limits, own, keys, values, out):
    core = lax.axis_index("tp") % 2

    def store(s, row, x):
        out[s, row : row + x.shape[0], :] = x

    attend_blocks(steps, limits, own, core, keys, values, store)


def attend_sibling_kernel(steps, limits, sibling, keys, values, blocks_own, out0, out1, out2, out3, blocks):
    device = lax.axis_index("tp")
    chip, core = device // 2, device % 2

    def store(s, row, x):
        blocks[2 * s + 1 - core, row : row + x.shape[0], :] = x

    for s in range(2):
        blocks[2 * s + core] = blocks_own[s]
    attend_blocks(steps, limits, sibling, 1 - core, keys, values, store)
    out0[...] = blocks[chip]
    for k, out in ((1, out1), (2, out2), (3, out3)):
        out[...] = blocks[partner(chip, k)]


def fresh_part(requests, steps, own, sibling, after, out):
    device = lax.axis_index("tp")
    chip, core = device // 2, device % 2
    rows = steps * GROUP
    tokens = requests * steps
    n = requests * rows

    def held(s, at_core):
        return jnp.where(core == at_core, own[s].astype(F32), sibling[s].astype(F32))

    def pick(x):
        return jnp.where(chip % 2 == 1, x[tokens:], x[:tokens]).astype(BF16)

    new_keys, new_values = pick(held(2, chip // 2)), pick(held(3, chip // 2))
    q = spread(held(chip // 2, chip % 2) * HEAD_DIMENSION**-0.5, GROUP)
    scores = lax.dot_general(q, new_keys, (((1,), (1,)), ((), ())), preferred_element_type=F32)
    row, column = iota(scores.shape, 0) % n, iota(scores.shape, 1)
    live = (row // rows == column // steps) & (column % steps <= row % steps)
    peak, weights, total = soft(scores, live)
    summed = jnp.dot(weights, new_values, preferred_element_type=F32)
    out[0:n] = fold(summed, n, 128)
    out[n : 2 * n] = pack_stats(fold(peak, n, 128), fold(total, n, 128))


def join(a, b):
    peak = jnp.maximum(a[0], b[0])
    left, right = jnp.exp(a[0] - peak), jnp.exp(b[0] - peak)
    return peak, a[1] * left + b[1] * right, a[2] * left + b[2] * right


def read_part(ref):
    n = ref.shape[0] // 2
    return (*unpack_stats(ref[n:]), ref[0:n])


def join_kernel(order, a, b, c, d, fetched, out):
    a, b, c, d = sort_chips(order, a, (b, c, d))
    peak, total, summed = join(join(read_part(a), read_part(d)), join(read_part(b), read_part(c)))
    n = summed.shape[0]
    out[0:n] = summed
    out[n:] = pack_stats(peak, total)


def output_kernel(requests, steps, own, sibling, fresh, weight, sibling_weight, out):
    core = lax.axis_index("tp") % 2
    _, total, summed = join(join(read_part(own), read_part(sibling)), read_part(fresh))
    attended = summed / total
    rows = steps * GROUP
    heads = []
    for j in range(GROUP):
        heads.append(merge_rows([attended[r * rows + j * steps : r * rows + (j + 1) * steps] for r in range(requests)]))
    low = iota(heads[0].shape, 1) < HEAD_DIMENSION
    zero = jnp.where(low, heads[0], pltpu.roll(heads[1], HEAD_DIMENSION, 1))
    one = jnp.where(low, pltpu.roll(heads[0], HEAD_DIMENSION, 1), heads[1])
    mine = jnp.where(core == 0, zero, one).astype(BF16)
    theirs = jnp.where(core == 0, one, zero).astype(BF16)
    projected = jnp.dot(mine, weight[...], preferred_element_type=F32) + jnp.dot(
        theirs, sibling_weight[...], preferred_element_type=F32
    )
    out[...] = projected.astype(BF16)


def sort_chips(order, first, parts):
    return [first] + [part for _, part in sorted(zip(order, parts), key=lambda pair: pair[0])]


def gather_kernel(order, a, b, c, d, fetched, out):
    chip = lax.axis_index("tp") // 2
    own, *others = sort_chips(order, a, (b, c, d))
    out[chip] = own[...]
    for back, x in zip((2, 1, 3), others):
        out[partner(chip, back)] = x[...]


def sum_chips(order, a, b, c, d):
    a, b, c, d = sort_chips(order, a, (b, c, d))
    return (a[...].astype(F32) + d[...].astype(F32)) + (b[...].astype(F32) + c[...].astype(F32))


def expert_kernel(order, inputs, a, b, c, d, ids, shares, down, *refs):
    *gate_up, out, residual_out = refs
    device = lax.axis_index("tp")
    residual = inputs[...] + sum_chips(order, a, b, c, d)
    residual_out[...] = residual
    normed = (
        residual * lax.rsqrt(jnp.mean(residual * residual, axis=-1, keepdims=True) + EPSILON)
    ).astype(BF16)
    requests = ids.shape[0]
    chosen = merge_rows([ids[r] for r in range(requests)])
    share = merge_rows([shares[r].astype(F32) for r in range(requests)]) * (1.0 / 65536.0)
    gate_up = [ref.at[i] for ref in gate_up for i in range(ref.shape[0])]
    experts = len(gate_up)
    total = None
    for e in range(experts):
        united = jnp.dot(normed, gate_up[e][...], preferred_element_type=F32)
        width = united.shape[1] // 2
        gate, up = united[:, :width], united[:, width:]
        active = (gate / (1.0 + jnp.exp(-gate)) * up).astype(BF16)
        outcome = jnp.dot(active, down[e], preferred_element_type=F32)
        factor = jnp.sum(jnp.where(chosen == device * experts + e, share, 0.0), axis=-1, keepdims=True)
        total = factor * outcome if total is None else total + factor * outcome
    out[...] = total.astype(BF16)


def final_kernel(order, requests, steps, residual, a, b, c, d, out):
    result = residual[...] + sum_chips(order, a, b, c, d)
    for r in range(requests):
        out[r] = result[r * steps : (r + 1) * steps].astype(BF16)


def partner(chip, k):
    outer = (chip == 0) | (chip == 3)
    if k == 3:
        return chip ^ 3
    return jnp.where(outer, chip ^ k, chip ^ (3 - k))


def other_chip(x, k, devices):
    to = {1: (1, 3, 0, 2), 2: (2, 0, 3, 1), 3: (3, 2, 1, 0)}[k]
    return lax.ppermute(x, "tp", [(i, 2 * to[i // 2] + i % 2) for i in range(devices)])


def to_chips(parts, devices, order):
    return [parts[0]] + [other_chip(parts[k], k, devices) for k in order]


def other_core(x, devices):
    return lax.ppermute(x, "tp", [(i, i ^ 1) for i in range(devices)])


def fast_device(
    hidden_states,
    lengths,
    qkv_weight,
    rotated_key_cache,
    earlier_value_cache,
    out_weight,
    expert_ids,
    combine_weights,
    gate_up_weight,
    down_weight,
):
    requests, steps, model_width = hidden_states.shape
    tokens = requests * steps
    devices = lax.axis_size("tp")
    chips = devices // 2
    rows = tokens * GROUP
    sibling_weight = other_core(out_weight, devices)
    heads, limits, inputs = call(
        project_kernel,
        [((rows, 128), BF16), ((requests, 8, 128), jnp.int32), ((tokens, model_width), F32)],
        [lengths, hidden_states, qkv_weight],
        "project",
        cost=COST[0],
        stay=range(3),
        scratch=[
            pltpu.SMEM(lengths.shape, jnp.int32),
            pltpu.VMEM(hidden_states.shape, BF16),
            pltpu.VMEM(qkv_weight.shape, BF16),
            pltpu.SemaphoreType.DMA((3,)),
        ],
    )
    caches = [(rotated_key_cache, 0, requests), (earlier_value_cache, 0, requests)]
    small = [(x[None], 0, 1) for x in (out_weight, expert_ids, combine_weights)]
    experts = gate_up_weight.shape[0]
    cuts = [(0, SPLIT[0]), (SPLIT[0], SPLIT[1] - SPLIT[0]), (SPLIT[1], experts - SPLIT[1])]
    gate_up = [[(gate_up_weight, *cut)] if cut[1] else [] for cut in cuts]
    keys, values, own_weight, ids, shares, *gate_up_a = fetch(caches + small + gate_up[0], [heads], "fetch_cache")
    (gathered,) = call(
        functools.partial(gather_kernel, ORDER[0]),
        [((chips, rows, 128), BF16)],
        [*to_chips([heads] * chips, devices, ORDER[0]), keys],
        "gather",
    )
    sibling = other_core(gathered, devices)
    (blocks_own,) = call(
        functools.partial(attend_own_kernel, steps),
        [((chips // 2, 2 * rows, 128), F32)],
        [limits, gathered, keys, values],
        "attend_own",
        cost=COST[1],
    )
    parts = call(
        functools.partial(attend_sibling_kernel, steps),
        [((2 * rows, 128), F32)] * chips,
        [limits, sibling, keys, values, blocks_own],
        "attend",
        cost=COST[1],
        scratch=[pltpu.VMEM((chips, 2 * rows, 128), F32)],
    )
    *gate_up_b, fresh = fetch(
        gate_up[1],
        [gathered, sibling, parts[0]],
        "fetch_b",
        beside=functools.partial(fresh_part, requests, steps),
        outs=[((2 * rows, 128), F32)],
    )
    arrived = to_chips(parts[:chips], devices, ORDER[1])
    (joined,) = call(functools.partial(join_kernel, ORDER[1]), [((2 * rows, 128), F32)], [*arrived, gate_up_b[0]], "join", cost=COST[2])
    (projected,) = call(
        functools.partial(output_kernel, requests, steps),
        [((tokens, model_width), BF16)],
        [joined, other_core(joined, devices), fresh, own_weight[0], sibling_weight],
        "output",
        cost=COST[2],
    )
    projections = to_chips([projected] * chips, devices, ORDER[2])
    *gate_up_c, down = fetch(gate_up[2] + [(down_weight, 0, experts)], [projected], "fetch_c")
    mixture, residual = call(
        functools.partial(expert_kernel, ORDER[2]),
        [((tokens, model_width), BF16), ((tokens, model_width), F32)],
        [inputs, *projections, ids[0], shares[0], down, *gate_up_a, *gate_up_b, *gate_up_c],
        "experts",
        cost=COST[3],
    )
    mixture = (mixture.astype(F32) + other_core(mixture, devices).astype(F32)).astype(BF16)
    mixtures = to_chips([mixture] * chips, devices, ORDER[3])
    (result,) = call(
        functools.partial(final_kernel, ORDER[3], requests, steps),
        [(hidden_states.shape, BF16)],
        [residual, *mixtures],
        "final",
        hbm_out=True,
    )
    return result


def merged(part, axis, combine):
    gathered = jax.tree.map(lambda a: lax.all_gather(a, axis), part)

    def take(source):
        return jax.tree.map(lambda a: lax.dynamic_index_in_dim(a, source, 0, False), gathered)

    return lax.fori_loop(
        1, lax.axis_size(axis), lambda source, state: combine(state, take(source)), take(0)
    )


def rms_rows(value_rows):
    return value_rows * lax.rsqrt(
        jnp.mean(value_rows * value_rows, axis=-1, keepdims=True) + EPSILON
    )


def apply_rotation(value_rows, position_index):
    half_width = value_rows.shape[-1] // 2
    rates = ROPE_BASE ** (-2.0 * jnp.arange(half_width, dtype=jnp.float32) / value_rows.shape[-1])
    angles = position_index[:, None, None] * rates
    cosine = jnp.cos(angles)
    sines = jnp.sin(angles)
    front_half = value_rows[..., :half_width]
    back_half = value_rows[..., half_width:]
    return jnp.concatenate(
        [front_half * cosine - back_half * sines, back_half * cosine + front_half * sines], axis=-1
    )


def join_parts(earlier, later):
    highest = jnp.maximum(earlier[0], later[0])
    scale_earlier = jnp.exp(earlier[0] - highest)
    scale_later = jnp.exp(later[0] - highest)
    weight_sum = earlier[1] * scale_earlier + later[1] * scale_later
    value_sum = earlier[2] * scale_earlier[..., None] + later[2] * scale_later[..., None]
    return (highest, weight_sum, value_sum)


def to_columns(value_rows, step_number, group_count):
    request_list, kv_heads, _, head_size = value_rows.shape
    return (
        value_rows.reshape(request_list, kv_heads, step_number, group_count, head_size)
        .transpose(0, 2, 1, 3, 4)
        .reshape(request_list * step_number, kv_heads * group_count * head_size)
    )


def expert_terms(normed, chosen, shares, gate_up_weight, down_weight, first_expert):
    ff_width = down_weight.shape[1]
    united_out = jnp.einsum(
        "nd,edf->enf", normed, gate_up_weight, preferred_element_type=jnp.float32
    )
    activation = (jax.nn.silu(united_out[..., :ff_width]) * united_out[..., ff_width:]).astype(
        jnp.bfloat16
    )
    outcome = jnp.einsum(
        "enf,efd->end", activation, down_weight, preferred_element_type=jnp.float32
    )
    owners = first_expert + jnp.arange(gate_up_weight.shape[0], dtype=jnp.int32)
    factors = jnp.sum(
        jnp.where(chosen[None, :, :] == owners[:, None, None], shares[None, :, :], 0.0), axis=-1
    )
    return jnp.sum(factors[:, :, None] * outcome, axis=0)


def general_device(
    hidden_states,
    lengths,
    qkv_weight,
    rotated_key_cache,
    earlier_value_cache,
    out_weight,
    expert_ids,
    combine_weights,
    gate_up_weight,
    down_weight,
):
    request_list, step_number, model_width = hidden_states.shape
    token_rows = request_list * step_number
    group_count = QUERY_HEADS // KEY_VALUE_HEADS
    query_total_width = QUERY_HEADS * HEAD_DIMENSION
    key_value_width = KEY_VALUE_HEADS * HEAD_DIMENSION
    score_scale = HEAD_DIMENSION ** (-0.5)
    inputs_flat = hidden_states.reshape(token_rows, model_width)
    normed = rms_rows(inputs_flat.astype(jnp.float32)).astype(jnp.bfloat16)
    projected_part = lax.dot_general(
        qkv_weight, normed, (((1,), (1,)), ((), ())), preferred_element_type=jnp.float32
    ).astype(jnp.bfloat16)
    projected_all = lax.all_gather(projected_part, "tp", axis=0, tiled=True)
    query_key_value_rows = projected_all.T
    position_index = (
        (lengths[:, None] + jnp.arange(step_number, dtype=jnp.int32)[None, :])
        .reshape(token_rows)
        .astype(jnp.float32)
    )
    query_rows = apply_rotation(
        query_key_value_rows[:, :query_total_width]
        .reshape(token_rows, QUERY_HEADS, HEAD_DIMENSION)
        .astype(jnp.float32),
        position_index,
    ).astype(jnp.bfloat16)
    fresh_keys = apply_rotation(
        query_key_value_rows[:, query_total_width : query_total_width + key_value_width]
        .reshape(token_rows, KEY_VALUE_HEADS, HEAD_DIMENSION)
        .astype(jnp.float32),
        position_index,
    ).astype(jnp.bfloat16)
    fresh_values = query_key_value_rows[:, query_total_width + key_value_width :].reshape(
        request_list, step_number, KEY_VALUE_HEADS, HEAD_DIMENSION
    )
    grouped_rows = (
        query_rows.reshape(request_list, step_number, KEY_VALUE_HEADS, group_count, HEAD_DIMENSION)
        .transpose(0, 2, 1, 3, 4)
        .reshape(request_list, KEY_VALUE_HEADS, step_number * group_count, HEAD_DIMENSION)
    )
    cache_extent = rotated_key_cache.shape[1]
    stored_keys = rotated_key_cache.reshape(
        request_list, cache_extent, KEY_VALUE_HEADS, HEAD_DIMENSION
    )
    stored_values = earlier_value_cache.reshape(
        request_list, cache_extent, KEY_VALUE_HEADS, HEAD_DIMENSION
    )
    scores = (
        jnp.einsum("bgqd,bcgd->bgqc", grouped_rows, stored_keys, preferred_element_type=jnp.float32)
        * score_scale
    )
    start_pos = lax.axis_index("tp") * cache_extent
    live_rows = (start_pos + jnp.arange(cache_extent, dtype=jnp.int32))[None, :] < lengths[:, None]
    live_mask = live_rows[:, None, None, :]
    masked = jnp.where(live_mask, scores, NEGATIVE)
    highest = jnp.max(masked, axis=-1)
    weights = jnp.where(live_mask, jnp.exp(masked - highest[..., None]), 0.0)
    weight_sum = jnp.sum(weights, axis=-1)
    value_sum = jnp.einsum(
        "bgqc,bcgd->bgqd",
        weights.astype(jnp.bfloat16),
        stored_values,
        preferred_element_type=jnp.float32,
    )
    feature_rows = out_weight.shape[0]
    column_begin = lax.axis_index("tp") * feature_rows
    top_score, total_all, sum_all = merged((highest, weight_sum, value_sum), "tp", join_parts)
    grouped_keys = fresh_keys.reshape(request_list, step_number, KEY_VALUE_HEADS, HEAD_DIMENSION)
    new_scores = (
        jnp.einsum(
            "bgqd,bsgd->bgqs", grouped_rows, grouped_keys, preferred_element_type=jnp.float32
        )
        * score_scale
    )
    query_step = jnp.arange(step_number * group_count, dtype=jnp.int32) // group_count
    causal = jnp.arange(step_number, dtype=jnp.int32)[None, :] <= query_step[:, None]
    new_masked = jnp.where(causal, new_scores, NEGATIVE)
    final_peak = jnp.maximum(top_score, jnp.max(new_masked, axis=-1))
    new_weights = jnp.where(causal, jnp.exp(new_masked - final_peak[..., None]), 0.0)
    carried = jnp.exp(top_score - final_peak)
    denominator = total_all * carried + jnp.sum(new_weights, axis=-1)
    new_part = jnp.einsum(
        "bgqs,bsgd->bgqd",
        new_weights.astype(jnp.bfloat16),
        fresh_values,
        preferred_element_type=jnp.float32,
    )
    numerator = sum_all * carried[..., None] + new_part
    attended = to_columns(numerator / denominator[..., None], step_number, group_count).astype(
        jnp.bfloat16
    )
    attended_part = lax.dynamic_slice_in_dim(attended, column_begin, feature_rows, 1)
    first_expert = lax.axis_index("tp") * gate_up_weight.shape[0]
    chosen = expert_ids.reshape(token_rows, -1)
    shares = combine_weights.reshape(token_rows, -1).astype(jnp.float32) / 65536.0
    head_terms = jnp.dot(attended_part, out_weight, preferred_element_type=jnp.float32)
    projected_rows = lax.psum(head_terms, "tp")
    residual = inputs_flat.astype(jnp.float32) + projected_rows
    normed_second = rms_rows(residual).astype(jnp.bfloat16)
    mixture = lax.psum(
        expert_terms(
            normed_second, chosen, shares, gate_up_weight, down_weight, first_expert
        ).astype(jnp.bfloat16),
        "tp",
    ).astype(jnp.float32)
    final_result = (residual + mixture).astype(jnp.bfloat16)
    return final_result.reshape(request_list, step_number, model_width)


def solution(mesh):
    in_specs = (
        P("req", None, None),
        P("req"),
        P("tp", None),
        P("req", "tp", None),
        P("req", "tp", None),
        P("tp", None),
        P("req", None, None),
        P("req", None, None),
        P("tp", None, None),
        P("tp", None, None),
    )
    out_specs = P("req", None, None)
    per_device = fast_device if mesh.shape["tp"] == 8 else general_device
    return jax.shard_map(
        per_device, mesh=mesh, in_specs=in_specs, out_specs=out_specs, check_vma=False
    )
```

```python
import functools

import jax
import jax.numpy as jnp
from jax import lax
from jax.experimental import pallas as pl
from jax.experimental.pallas import tpu as pltpu
from jax.sharding import PartitionSpec as P

QUERY_HEADS = 16
KEY_VALUE_HEADS = 8
HEAD_DIMENSION = 64
GROUP = QUERY_HEADS // KEY_VALUE_HEADS
EPSILON = 1e-05
ROPE_BASE = 10000.0
NEGATIVE = -1e30
F32 = jnp.float32
BF16 = jnp.bfloat16
VMEM_LIMIT = 16 * 1024 * 1024
SPLIT = (0, 3)
ORDER = ((1, 2, 3), (3, 2, 1), (1, 2, 3), (2, 3, 1))
COST = (8_000_000, 6_000_000, 1_000_000, 12_000_000)


def iota(shape, dim):
    return lax.broadcasted_iota(jnp.int32, shape, dim)


def merge_rows(blocks):
    return jnp.concatenate(blocks, axis=0)


def on(space):
    return pl.BlockSpec(memory_space=space)


def call(kernel, outs, operands, name, stay=(), scratch=(), hbm_out=False, cost=0, same=()):
    operands = [
        pltpu.with_memory_space_constraint(x, pltpu.HBM) if i in stay else x for i, x in enumerate(operands)
    ]
    return pl.pallas_call(
        kernel,
        out_shape=[
            jax.ShapeDtypeStruct(s, d) if hbm_out else pltpu.VMEM(s, d) for s, d in outs
        ],
        in_specs=[on(pltpu.HBM if i in stay else pltpu.VMEM) for i in range(len(operands))],
        out_specs=[on(pltpu.VMEM) for _ in outs],
        scratch_shapes=list(scratch),
        input_output_aliases=dict(same),
        compiler_params=pltpu.CompilerParams(vmem_limit_bytes=VMEM_LIMIT),
        cost_estimate=pl.CostEstimate(flops=0, bytes_accessed=cost, transcendentals=0),
        name=name,
    )(*operands)


def start_all(pairs, semaphores):
    copies = [
        pltpu.make_async_copy(source, target, semaphores.at[i]) for i, (source, target) in enumerate(pairs)
    ]
    for copy in copies:
        copy.start()
    return copies


def project_kernel(
    lengths_in,
    hidden_in,
    weight_in,
    out,
    limits,
    inputs,
    lengths,
    hidden,
    weight,
    semaphores,
):
    copies = start_all(
        [
            (lengths_in, lengths),
            (hidden_in, hidden),
            (weight_in, weight),
        ],
        semaphores,
    )
    requests, steps, _ = hidden.shape
    device = lax.axis_index("tp")
    devices = lax.axis_size("tp")
    copies[1].wait()
    x = merge_rows([hidden[b].astype(F32) for b in range(requests)])
    inputs[...] = x
    normed = (x * lax.rsqrt(jnp.mean(x * x, axis=-1, keepdims=True) + EPSILON)).astype(BF16)
    copies[0].wait()
    tokens = requests * steps
    row = iota((tokens, 128), 0)
    lane = iota((tokens, 128), 1)
    position = jnp.zeros((tokens, 128), jnp.int32)
    for b in range(requests):
        position = jnp.where(row // steps == b, lengths[b] + row - b * steps, position)
        limits[b] = jnp.full(limits.shape[1:], lengths[b], jnp.int32)
    half = HEAD_DIMENSION // 2
    rates = jnp.exp((lane % half).astype(F32) * (-2.0 / HEAD_DIMENSION * 9.210340371976184))
    angles = position.astype(F32) * rates
    turned = device < devices * 3 // 4
    cosine = jnp.where(turned, jnp.cos(angles), 1.0)
    sine = jnp.where(turned, jnp.sin(angles), 0.0)
    first = lane % HEAD_DIMENSION < half
    sine = jnp.where(first, -sine, sine)
    copies[2].wait()
    y = lax.dot_general(normed, weight[...], (((1,), (1,)), ((), ())), preferred_element_type=F32)
    y = y.astype(BF16).astype(F32)
    parts = []
    for k in range(y.shape[1] // 128):
        v = y[:, k * 128 : (k + 1) * 128]
        other = jnp.where(first, pltpu.roll(v, 128 - half, 1), pltpu.roll(v, half, 1))
        parts.append(v * cosine + other * sine)
    a, b = parts
    low = lane < HEAD_DIMENSION
    even = jnp.where(low, a, pltpu.roll(b, HEAD_DIMENSION, 1))
    odd = jnp.where(low, pltpu.roll(a, HEAD_DIMENSION, 1), b)
    rows = []
    for r in range(requests):
        rows += [even[r * steps : (r + 1) * steps], odd[r * steps : (r + 1) * steps]]
    query = merge_rows(rows)
    plain = merge_rows([a, b])
    out[...] = jnp.where(device < devices // 2, query, plain).astype(BF16)


def fetch_kernel(pieces, beside, operands, *refs):
    count = len(pieces)
    inputs, sources = refs[:operands], refs[operands : operands + count]
    outs, semaphores = refs[operands + count : -1], refs[-1]
    targets = outs[:count]
    pairs = [
        (source.at[first + i], target.at[i])
        for source, target, (first, size) in zip(sources, targets, pieces)
        for i in range(size)
    ]
    copies = start_all(pairs, semaphores)
    if beside is not None:
        beside(*inputs, *outs[count:])
    for copy in copies:
        copy.wait()


def fetch(pieces, after, name, beside=None, outs=()):
    rows = [(first, size) for _, first, size in pieces]
    return call(
        functools.partial(fetch_kernel, rows, beside, len(after)),
        [((size,) + x.shape[1:], x.dtype) for x, _, size in pieces] + list(outs),
        [*after] + [x for x, _, _ in pieces],
        name,
        stay=range(len(after), len(after) + len(pieces)),
        scratch=[pltpu.SemaphoreType.DMA((sum(size for _, size in rows),))],
        cost=sum(x.size * 2 // x.shape[0] * size for x, _, size in pieces),
    )


def fold(x, rows, lanes):
    groups = lanes // HEAD_DIMENSION
    lane = iota((rows, lanes), 1) // HEAD_DIMENSION
    total = jnp.broadcast_to(x[0:rows], (rows, lanes))
    for g in range(1, groups):
        total = jnp.where(lane == g, jnp.broadcast_to(x[g * rows : (g + 1) * rows], (rows, lanes)), total)
    return total


def spread(x, groups):
    rows, lanes = x.shape
    lane = iota((rows, lanes), 1) // HEAD_DIMENSION
    return merge_rows([jnp.where(lane == g, x, 0.0) for g in range(groups)]).astype(BF16)


def pack_stats(peak, total):
    lane = iota(peak.shape, 1)
    return jnp.where(lane % HEAD_DIMENSION < HEAD_DIMENSION // 2, peak, total)


def unpack_stats(stats):
    half = HEAD_DIMENSION // 2
    low = iota(stats.shape, 1) % HEAD_DIMENSION < half
    return (
        jnp.where(low, stats, pltpu.roll(stats, half, 1)),
        jnp.where(low, pltpu.roll(stats, stats.shape[1] - half, 1), stats),
    )


def soft(scores, live):
    masked = jnp.where(live, scores, NEGATIVE)
    peak = jnp.max(masked, axis=-1, keepdims=True)
    weights = jnp.where(live, jnp.exp(masked - peak), 0.0)
    return peak, weights.astype(BF16), jnp.sum(weights, axis=-1, keepdims=True)


def attend_blocks(steps, limits, heads, cores, keys, values, store):
    device = lax.axis_index("tp")
    requests, count, _ = keys.shape
    rows = steps * GROUP
    scale = HEAD_DIMENSION**-0.5
    pairs = [(s, r) for s in range(2) for r in range(requests)]
    columns = [pl.ds(pl.multiple_of((2 * s + cores[s]) * 128, 128), 128) for s in range(2)]
    scores = []
    for s, r in pairs:
        q = spread(heads[s, r * rows : (r + 1) * rows].astype(F32) * scale, GROUP)
        scores.append(
            lax.dot_general(q, keys[r, :, columns[s]], (((1,), (1,)), ((), ())), preferred_element_type=F32)
        )
    scores = merge_rows(scores)
    position = device * count + iota(scores.shape, 1)
    limit = merge_rows([limits[r, 0:rows] for _, r in pairs for _ in range(GROUP)])
    peak, weights, total = soft(scores, position < limit)
    n = GROUP * rows
    for i, (s, r) in enumerate(pairs):
        own = slice(i * n, (i + 1) * n)
        summed = jnp.dot(weights[own], values[r, :, columns[s]], preferred_element_type=F32)
        store(s, r * rows, fold(summed, rows, 128))
        store(s, (requests + r) * rows, pack_stats(fold(peak[own], rows, 128), fold(total[own], rows, 128)))


def attend_own_kernel(steps, limits, own, keys, values, out):
    def store(s, row, x):
        out[s, row : row + x.shape[0], :] = x

    attend_blocks(steps, limits, own, [near_core(s) for s in range(2)], keys, values, store)


def attend_sibling_kernel(steps, limits, sibling, keys, values, blocks_own, out0, out1, out2, out3, blocks):
    device = lax.axis_index("tp")
    chip = device // 2
    near = [near_core(s) for s in range(2)]

    def store(s, row, x):
        blocks[2 * s + 1 - near[s], row : row + x.shape[0], :] = x

    for s in range(2):
        blocks[2 * s + near[s]] = blocks_own[s]
    attend_blocks(steps, limits, sibling, [1 - x for x in near], keys, values, store)
    out0[...] = blocks[chip]
    for k, out in ((1, out1), (2, out2), (3, out3)):
        out[...] = blocks[partner(chip, k)]


def fresh_part(requests, steps, own, sibling, after, out):
    device = lax.axis_index("tp")
    chip = device // 2
    rows = steps * GROUP
    tokens = requests * steps
    n = requests * rows

    def held(s, at_core):
        return jnp.where(near_core(s) == at_core, own[s].astype(F32), sibling[s].astype(F32))

    def pick(x):
        return jnp.where(chip % 2 == 1, x[tokens:], x[:tokens]).astype(BF16)

    new_keys, new_values = pick(held(2, chip // 2)), pick(held(3, chip // 2))
    q = spread(held(chip // 2, chip % 2) * HEAD_DIMENSION**-0.5, GROUP)
    scores = lax.dot_general(q, new_keys, (((1,), (1,)), ((), ())), preferred_element_type=F32)
    row, column = iota(scores.shape, 0) % n, iota(scores.shape, 1)
    live = (row // rows == column // steps) & (column % steps <= row % steps)
    peak, weights, total = soft(scores, live)
    summed = jnp.dot(weights, new_values, preferred_element_type=F32)
    out[0:n] = fold(summed, n, 128)
    out[n : 2 * n] = pack_stats(fold(peak, n, 128), fold(total, n, 128))


def join(a, b):
    peak = jnp.maximum(a[0], b[0])
    left, right = jnp.exp(a[0] - peak), jnp.exp(b[0] - peak)
    return peak, a[1] * left + b[1] * right, a[2] * left + b[2] * right


def read_part(ref):
    n = ref.shape[0] // 2
    return (*unpack_stats(ref[n:]), ref[0:n])


def join_kernel(order, a, b, c, d, fetched, out):
    a, b, c, d = sort_chips(order, a, (b, c, d))
    peak, total, summed = join(join(read_part(a), read_part(d)), join(read_part(b), read_part(c)))
    n = summed.shape[0]
    out[0:n] = summed
    out[n:] = pack_stats(peak, total)


def output_kernel(requests, steps, own, sibling, fresh, weight, sibling_weight, out):
    core = lax.axis_index("tp") % 2
    _, total, summed = join(join(read_part(own), read_part(sibling)), read_part(fresh))
    attended = summed / total
    rows = steps * GROUP
    heads = []
    for j in range(GROUP):
        heads.append(merge_rows([attended[r * rows + j * steps : r * rows + (j + 1) * steps] for r in range(requests)]))
    low = iota(heads[0].shape, 1) < HEAD_DIMENSION
    zero = jnp.where(low, heads[0], pltpu.roll(heads[1], HEAD_DIMENSION, 1))
    one = jnp.where(low, pltpu.roll(heads[0], HEAD_DIMENSION, 1), heads[1])
    mine = jnp.where(core == 0, zero, one).astype(BF16)
    theirs = jnp.where(core == 0, one, zero).astype(BF16)
    projected = jnp.dot(mine, weight[...], preferred_element_type=F32) + jnp.dot(
        theirs, sibling_weight[...], preferred_element_type=F32
    )
    out[...] = projected.astype(BF16)


def sort_chips(order, first, parts):
    return [first] + [part for _, part in sorted(zip(order, parts), key=lambda pair: pair[0])]


def gather_kernel(order, a, b, c, d, weight, out, same_weight):
    chip = lax.axis_index("tp") // 2
    own, *others = sort_chips(order, a, (b, c, d))
    out[chip] = own[...]
    for back, x in zip((2, 1, 3), others):
        out[partner(chip, back)] = x[...]


def sum_chips(order, a, b, c, d):
    a, b, c, d = sort_chips(order, a, (b, c, d))
    return (a[...].astype(F32) + d[...].astype(F32)) + (b[...].astype(F32) + c[...].astype(F32))


def expert_kernel(order, inputs, a, b, c, d, ids, shares, down, *refs):
    *gate_up, out, residual_out = refs
    device = lax.axis_index("tp")
    residual = inputs[...] + sum_chips(order, a, b, c, d)
    residual_out[...] = residual
    normed = (
        residual * lax.rsqrt(jnp.mean(residual * residual, axis=-1, keepdims=True) + EPSILON)
    ).astype(BF16)
    requests = ids.shape[0]
    chosen = merge_rows([ids[r] for r in range(requests)])
    share = merge_rows([shares[r].astype(F32) for r in range(requests)]) * (1.0 / 65536.0)
    gate_up = [ref.at[i] for ref in gate_up for i in range(ref.shape[0])]
    experts = len(gate_up)
    total = None
    for e in range(experts):
        united = jnp.dot(normed, gate_up[e][...], preferred_element_type=F32)
        width = united.shape[1] // 2
        gate, up = united[:, :width], united[:, width:]
        active = (gate / (1.0 + jnp.exp(-gate)) * up).astype(BF16)
        outcome = jnp.dot(active, down[e], preferred_element_type=F32)
        factor = jnp.sum(jnp.where(chosen == device * experts + e, share, 0.0), axis=-1, keepdims=True)
        total = factor * outcome if total is None else total + factor * outcome
    out[...] = total.astype(BF16)


def final_kernel(order, requests, steps, residual, a, b, c, d, out):
    result = residual[...] + sum_chips(order, a, b, c, d)
    for r in range(requests):
        out[r] = result[r * steps : (r + 1) * steps].astype(BF16)


def partner(chip, k):
    outer = (chip == 0) | (chip == 3)
    if k == 3:
        return chip ^ 3
    return jnp.where(outer, chip ^ k, chip ^ (3 - k))


def other_chip(x, k, devices):
    to = {1: (1, 3, 0, 2), 2: (2, 0, 3, 1), 3: (3, 2, 1, 0)}[k]
    return lax.ppermute(x, "tp", [(i, 2 * to[i // 2] + 1 - i % 2) for i in range(devices)])


def near_core(s):
    device = lax.axis_index("tp")
    core = device % 2
    return jnp.where(device // 2 == s, core, 1 - core)


def to_chips(parts, devices, order):
    return [parts[0]] + [other_chip(parts[k], k, devices) for k in order]


def other_core(x, devices):
    return lax.ppermute(x, "tp", [(i, i ^ 1) for i in range(devices)])


def fast_device(
    hidden_states,
    lengths,
    qkv_weight,
    rotated_key_cache,
    earlier_value_cache,
    out_weight,
    expert_ids,
    combine_weights,
    gate_up_weight,
    down_weight,
):
    requests, steps, model_width = hidden_states.shape
    tokens = requests * steps
    devices = lax.axis_size("tp")
    chips = devices // 2
    rows = tokens * GROUP
    heads, limits, inputs = call(
        project_kernel,
        [((rows, 128), BF16), ((requests, 8, 128), jnp.int32), ((tokens, model_width), F32)],
        [lengths, hidden_states, qkv_weight],
        "project",
        cost=COST[0],
        stay=range(3),
        scratch=[
            pltpu.SMEM(lengths.shape, jnp.int32),
            pltpu.VMEM(hidden_states.shape, BF16),
            pltpu.VMEM(qkv_weight.shape, BF16),
            pltpu.SemaphoreType.DMA((3,)),
        ],
    )
    caches = [(rotated_key_cache, 0, requests), (earlier_value_cache, 0, requests)]
    small = [(x[None], 0, 1) for x in (out_weight, expert_ids, combine_weights)]
    experts = gate_up_weight.shape[0]
    cuts = [(0, SPLIT[0]), (SPLIT[0], SPLIT[1] - SPLIT[0]), (SPLIT[1], experts - SPLIT[1])]
    gate_up = [[(gate_up_weight, *cut)] if cut[1] else [] for cut in cuts]
    keys, values, own_weight, ids, shares, *gate_up_a = fetch(caches + small + gate_up[0], [heads], "fetch_cache")
    gathered, own_weight = call(
        functools.partial(gather_kernel, ORDER[0]),
        [((chips, rows, 128), BF16), (own_weight.shape, BF16)],
        [*to_chips([heads] * chips, devices, ORDER[0]), own_weight],
        "gather",
        same={chips: 1},
    )
    sibling_weight = other_core(own_weight[0], devices)
    sibling = other_core(gathered, devices)
    (blocks_own,) = call(
        functools.partial(attend_own_kernel, steps),
        [((chips // 2, 2 * rows, 128), F32)],
        [limits, gathered, keys, values],
        "attend_own",
        cost=COST[1],
    )
    parts = call(
        functools.partial(attend_sibling_kernel, steps),
        [((2 * rows, 128), F32)] * chips,
        [limits, sibling, keys, values, blocks_own],
        "attend",
        cost=COST[1],
        scratch=[pltpu.VMEM((chips, 2 * rows, 128), F32)],
    )
    *gate_up_b, fresh = fetch(
        gate_up[1],
        [gathered, sibling, parts[0]],
        "fetch_b",
        beside=functools.partial(fresh_part, requests, steps),
        outs=[((2 * rows, 128), F32)],
    )
    arrived = to_chips(parts[:chips], devices, ORDER[1])
    (joined,) = call(functools.partial(join_kernel, ORDER[1]), [((2 * rows, 128), F32)], [*arrived, gate_up_b[0]], "join", cost=COST[2])
    (projected,) = call(
        functools.partial(output_kernel, requests, steps),
        [((tokens, model_width), BF16)],
        [joined, other_core(joined, devices), fresh, own_weight[0], sibling_weight],
        "output",
        cost=COST[2],
    )
    projections = to_chips([projected] * chips, devices, ORDER[2])
    *gate_up_c, down = fetch(gate_up[2] + [(down_weight, 0, experts)], [projected], "fetch_c")
    mixture, residual = call(
        functools.partial(expert_kernel, ORDER[2]),
        [((tokens, model_width), BF16), ((tokens, model_width), F32)],
        [inputs, *projections, ids[0], shares[0], down, *gate_up_a, *gate_up_b, *gate_up_c],
        "experts",
        cost=COST[3],
    )
    mixture = (mixture.astype(F32) + other_core(mixture, devices).astype(F32)).astype(BF16)
    mixtures = to_chips([mixture] * chips, devices, ORDER[3])
    (result,) = call(
        functools.partial(final_kernel, ORDER[3], requests, steps),
        [(hidden_states.shape, BF16)],
        [residual, *mixtures],
        "final",
        hbm_out=True,
    )
    return result


def merged(part, axis, combine):
    gathered = jax.tree.map(lambda a: lax.all_gather(a, axis), part)

    def take(source):
        return jax.tree.map(lambda a: lax.dynamic_index_in_dim(a, source, 0, False), gathered)

    return lax.fori_loop(
        1, lax.axis_size(axis), lambda source, state: combine(state, take(source)), take(0)
    )


def rms_rows(value_rows):
    return value_rows * lax.rsqrt(
        jnp.mean(value_rows * value_rows, axis=-1, keepdims=True) + EPSILON
    )


def apply_rotation(value_rows, position_index):
    half_width = value_rows.shape[-1] // 2
    rates = ROPE_BASE ** (-2.0 * jnp.arange(half_width, dtype=jnp.float32) / value_rows.shape[-1])
    angles = position_index[:, None, None] * rates
    cosine = jnp.cos(angles)
    sines = jnp.sin(angles)
    front_half = value_rows[..., :half_width]
    back_half = value_rows[..., half_width:]
    return jnp.concatenate(
        [front_half * cosine - back_half * sines, back_half * cosine + front_half * sines], axis=-1
    )


def join_parts(earlier, later):
    highest = jnp.maximum(earlier[0], later[0])
    scale_earlier = jnp.exp(earlier[0] - highest)
    scale_later = jnp.exp(later[0] - highest)
    weight_sum = earlier[1] * scale_earlier + later[1] * scale_later
    value_sum = earlier[2] * scale_earlier[..., None] + later[2] * scale_later[..., None]
    return (highest, weight_sum, value_sum)


def to_columns(value_rows, step_number, group_count):
    request_list, kv_heads, _, head_size = value_rows.shape
    return (
        value_rows.reshape(request_list, kv_heads, step_number, group_count, head_size)
        .transpose(0, 2, 1, 3, 4)
        .reshape(request_list * step_number, kv_heads * group_count * head_size)
    )


def expert_terms(normed, chosen, shares, gate_up_weight, down_weight, first_expert):
    ff_width = down_weight.shape[1]
    united_out = jnp.einsum(
        "nd,edf->enf", normed, gate_up_weight, preferred_element_type=jnp.float32
    )
    activation = (jax.nn.silu(united_out[..., :ff_width]) * united_out[..., ff_width:]).astype(
        jnp.bfloat16
    )
    outcome = jnp.einsum(
        "enf,efd->end", activation, down_weight, preferred_element_type=jnp.float32
    )
    owners = first_expert + jnp.arange(gate_up_weight.shape[0], dtype=jnp.int32)
    factors = jnp.sum(
        jnp.where(chosen[None, :, :] == owners[:, None, None], shares[None, :, :], 0.0), axis=-1
    )
    return jnp.sum(factors[:, :, None] * outcome, axis=0)


def general_device(
    hidden_states,
    lengths,
    qkv_weight,
    rotated_key_cache,
    earlier_value_cache,
    out_weight,
    expert_ids,
    combine_weights,
    gate_up_weight,
    down_weight,
):
    request_list, step_number, model_width = hidden_states.shape
    token_rows = request_list * step_number
    group_count = QUERY_HEADS // KEY_VALUE_HEADS
    query_total_width = QUERY_HEADS * HEAD_DIMENSION
    key_value_width = KEY_VALUE_HEADS * HEAD_DIMENSION
    score_scale = HEAD_DIMENSION ** (-0.5)
    inputs_flat = hidden_states.reshape(token_rows, model_width)
    normed = rms_rows(inputs_flat.astype(jnp.float32)).astype(jnp.bfloat16)
    projected_part = lax.dot_general(
        qkv_weight, normed, (((1,), (1,)), ((), ())), preferred_element_type=jnp.float32
    ).astype(jnp.bfloat16)
    projected_all = lax.all_gather(projected_part, "tp", axis=0, tiled=True)
    query_key_value_rows = projected_all.T
    position_index = (
        (lengths[:, None] + jnp.arange(step_number, dtype=jnp.int32)[None, :])
        .reshape(token_rows)
        .astype(jnp.float32)
    )
    query_rows = apply_rotation(
        query_key_value_rows[:, :query_total_width]
        .reshape(token_rows, QUERY_HEADS, HEAD_DIMENSION)
        .astype(jnp.float32),
        position_index,
    ).astype(jnp.bfloat16)
    fresh_keys = apply_rotation(
        query_key_value_rows[:, query_total_width : query_total_width + key_value_width]
        .reshape(token_rows, KEY_VALUE_HEADS, HEAD_DIMENSION)
        .astype(jnp.float32),
        position_index,
    ).astype(jnp.bfloat16)
    fresh_values = query_key_value_rows[:, query_total_width + key_value_width :].reshape(
        request_list, step_number, KEY_VALUE_HEADS, HEAD_DIMENSION
    )
    grouped_rows = (
        query_rows.reshape(request_list, step_number, KEY_VALUE_HEADS, group_count, HEAD_DIMENSION)
        .transpose(0, 2, 1, 3, 4)
        .reshape(request_list, KEY_VALUE_HEADS, step_number * group_count, HEAD_DIMENSION)
    )
    cache_extent = rotated_key_cache.shape[1]
    stored_keys = rotated_key_cache.reshape(
        request_list, cache_extent, KEY_VALUE_HEADS, HEAD_DIMENSION
    )
    stored_values = earlier_value_cache.reshape(
        request_list, cache_extent, KEY_VALUE_HEADS, HEAD_DIMENSION
    )
    scores = (
        jnp.einsum("bgqd,bcgd->bgqc", grouped_rows, stored_keys, preferred_element_type=jnp.float32)
        * score_scale
    )
    start_pos = lax.axis_index("tp") * cache_extent
    live_rows = (start_pos + jnp.arange(cache_extent, dtype=jnp.int32))[None, :] < lengths[:, None]
    live_mask = live_rows[:, None, None, :]
    masked = jnp.where(live_mask, scores, NEGATIVE)
    highest = jnp.max(masked, axis=-1)
    weights = jnp.where(live_mask, jnp.exp(masked - highest[..., None]), 0.0)
    weight_sum = jnp.sum(weights, axis=-1)
    value_sum = jnp.einsum(
        "bgqc,bcgd->bgqd",
        weights.astype(jnp.bfloat16),
        stored_values,
        preferred_element_type=jnp.float32,
    )
    feature_rows = out_weight.shape[0]
    column_begin = lax.axis_index("tp") * feature_rows
    top_score, total_all, sum_all = merged((highest, weight_sum, value_sum), "tp", join_parts)
    grouped_keys = fresh_keys.reshape(request_list, step_number, KEY_VALUE_HEADS, HEAD_DIMENSION)
    new_scores = (
        jnp.einsum(
            "bgqd,bsgd->bgqs", grouped_rows, grouped_keys, preferred_element_type=jnp.float32
        )
        * score_scale
    )
    query_step = jnp.arange(step_number * group_count, dtype=jnp.int32) // group_count
    causal = jnp.arange(step_number, dtype=jnp.int32)[None, :] <= query_step[:, None]
    new_masked = jnp.where(causal, new_scores, NEGATIVE)
    final_peak = jnp.maximum(top_score, jnp.max(new_masked, axis=-1))
    new_weights = jnp.where(causal, jnp.exp(new_masked - final_peak[..., None]), 0.0)
    carried = jnp.exp(top_score - final_peak)
    denominator = total_all * carried + jnp.sum(new_weights, axis=-1)
    new_part = jnp.einsum(
        "bgqs,bsgd->bgqd",
        new_weights.astype(jnp.bfloat16),
        fresh_values,
        preferred_element_type=jnp.float32,
    )
    numerator = sum_all * carried[..., None] + new_part
    attended = to_columns(numerator / denominator[..., None], step_number, group_count).astype(
        jnp.bfloat16
    )
    attended_part = lax.dynamic_slice_in_dim(attended, column_begin, feature_rows, 1)
    first_expert = lax.axis_index("tp") * gate_up_weight.shape[0]
    chosen = expert_ids.reshape(token_rows, -1)
    shares = combine_weights.reshape(token_rows, -1).astype(jnp.float32) / 65536.0
    head_terms = jnp.dot(attended_part, out_weight, preferred_element_type=jnp.float32)
    projected_rows = lax.psum(head_terms, "tp")
    residual = inputs_flat.astype(jnp.float32) + projected_rows
    normed_second = rms_rows(residual).astype(jnp.bfloat16)
    mixture = lax.psum(
        expert_terms(
            normed_second, chosen, shares, gate_up_weight, down_weight, first_expert
        ).astype(jnp.bfloat16),
        "tp",
    ).astype(jnp.float32)
    final_result = (residual + mixture).astype(jnp.bfloat16)
    return final_result.reshape(request_list, step_number, model_width)


def solution(mesh):
    in_specs = (
        P("req", None, None),
        P("req"),
        P("tp", None),
        P("req", "tp", None),
        P("req", "tp", None),
        P("tp", None),
        P("req", None, None),
        P("req", None, None),
        P("tp", None, None),
        P("tp", None, None),
    )
    out_specs = P("req", None, None)
    per_device = fast_device if mesh.shape["tp"] == 8 else general_device
    return jax.shard_map(
        per_device, mesh=mesh, in_specs=in_specs, out_specs=out_specs, check_vma=False
    )
```

```python
import functools

import jax
import jax.numpy as jnp
from jax import lax
from jax.experimental import pallas as pl
from jax.experimental.pallas import tpu as pltpu
from jax.sharding import PartitionSpec as P

QUERY_HEADS = 16
KEY_VALUE_HEADS = 8
HEAD_DIMENSION = 64
GROUP = QUERY_HEADS // KEY_VALUE_HEADS
EPSILON = 1e-05
ROPE_BASE = 10000.0
NEGATIVE = -1e30
F32 = jnp.float32
BF16 = jnp.bfloat16
VMEM_LIMIT = 16 * 1024 * 1024
SPLIT = (0, 3)
ORDER = ((1, 2, 3), (3, 2, 1), (1, 2, 3), (2, 3, 1))
COST = (8_000_000, 6_000_000, 1_000_000, 12_000_000)


def iota(shape, dim):
    return lax.broadcasted_iota(jnp.int32, shape, dim)


def merge_rows(blocks):
    return jnp.concatenate(blocks, axis=0)


def on(space):
    return pl.BlockSpec(memory_space=space)


def call(kernel, outs, operands, name, stay=(), scratch=(), hbm_out=False, cost=0, same=()):
    operands = [
        pltpu.with_memory_space_constraint(x, pltpu.HBM) if i in stay else x for i, x in enumerate(operands)
    ]
    return pl.pallas_call(
        kernel,
        out_shape=[
            jax.ShapeDtypeStruct(s, d) if hbm_out else pltpu.VMEM(s, d) for s, d in outs
        ],
        in_specs=[on(pltpu.HBM if i in stay else pltpu.VMEM) for i in range(len(operands))],
        out_specs=[on(pltpu.VMEM) for _ in outs],
        scratch_shapes=list(scratch),
        input_output_aliases=dict(same),
        compiler_params=pltpu.CompilerParams(vmem_limit_bytes=VMEM_LIMIT),
        cost_estimate=pl.CostEstimate(flops=0, bytes_accessed=cost, transcendentals=0),
        name=name,
    )(*operands)


def start_all(pairs, semaphores):
    copies = [
        pltpu.make_async_copy(source, target, semaphores.at[i]) for i, (source, target) in enumerate(pairs)
    ]
    for copy in copies:
        copy.start()
    return copies


def project_kernel(
    lengths_in,
    hidden_in,
    weight_in,
    out,
    limits,
    inputs,
    lengths,
    hidden,
    weight,
    semaphores,
):
    copies = start_all(
        [
            (lengths_in, lengths),
            (hidden_in, hidden),
            (weight_in, weight),
        ],
        semaphores,
    )
    requests, steps, _ = hidden.shape
    device = lax.axis_index("tp")
    devices = lax.axis_size("tp")
    copies[1].wait()
    x = merge_rows([hidden[b].astype(F32) for b in range(requests)])
    inputs[...] = x
    normed = (x * lax.rsqrt(jnp.mean(x * x, axis=-1, keepdims=True) + EPSILON)).astype(BF16)
    copies[0].wait()
    tokens = requests * steps
    row = iota((tokens, 128), 0)
    lane = iota((tokens, 128), 1)
    position = jnp.zeros((tokens, 128), jnp.int32)
    for b in range(requests):
        position = jnp.where(row // steps == b, lengths[b] + row - b * steps, position)
        limits[b] = jnp.full(limits.shape[1:], lengths[b], jnp.int32)
    half = HEAD_DIMENSION // 2
    rates = jnp.exp((lane % half).astype(F32) * (-2.0 / HEAD_DIMENSION * 9.210340371976184))
    angles = position.astype(F32) * rates
    turned = device < devices * 3 // 4
    cosine = jnp.where(turned, jnp.cos(angles), 1.0)
    sine = jnp.where(turned, jnp.sin(angles), 0.0)
    first = lane % HEAD_DIMENSION < half
    sine = jnp.where(first, -sine, sine)
    copies[2].wait()
    y = lax.dot_general(normed, weight[...], (((1,), (1,)), ((), ())), preferred_element_type=F32)
    y = y.astype(BF16).astype(F32)
    parts = []
    for k in range(y.shape[1] // 128):
        v = y[:, k * 128 : (k + 1) * 128]
        other = jnp.where(first, pltpu.roll(v, 128 - half, 1), pltpu.roll(v, half, 1))
        parts.append(v * cosine + other * sine)
    a, b = parts
    low = lane < HEAD_DIMENSION
    even = jnp.where(low, a, pltpu.roll(b, HEAD_DIMENSION, 1))
    odd = jnp.where(low, pltpu.roll(a, HEAD_DIMENSION, 1), b)
    rows = []
    for r in range(requests):
        rows += [even[r * steps : (r + 1) * steps], odd[r * steps : (r + 1) * steps]]
    query = merge_rows(rows)
    plain = merge_rows([a, b])
    out[...] = jnp.where(device < devices // 2, query, plain).astype(BF16)


def fetch_kernel(pieces, beside, operands, *refs):
    count = len(pieces)
    inputs, sources = refs[:operands], refs[operands : operands + count]
    outs, semaphores = refs[operands + count : -1], refs[-1]
    targets = outs[:count]
    pairs = [
        (source.at[first + i], target.at[i])
        for source, target, (first, size) in zip(sources, targets, pieces)
        for i in range(size)
    ]
    copies = start_all(pairs, semaphores)
    if beside is not None:
        beside(*inputs, *outs[count:])
    for copy in copies:
        copy.wait()


def fetch(pieces, after, name, beside=None, outs=()):
    rows = [(first, size) for _, first, size in pieces]
    return call(
        functools.partial(fetch_kernel, rows, beside, len(after)),
        [((size,) + x.shape[1:], x.dtype) for x, _, size in pieces] + list(outs),
        [*after] + [x for x, _, _ in pieces],
        name,
        stay=range(len(after), len(after) + len(pieces)),
        scratch=[pltpu.SemaphoreType.DMA((sum(size for _, size in rows),))],
        cost=sum(x.size * 2 // x.shape[0] * size for x, _, size in pieces),
    )


def fold(x, rows, lanes):
    groups = lanes // HEAD_DIMENSION
    lane = iota((rows, lanes), 1) // HEAD_DIMENSION
    total = jnp.broadcast_to(x[0:rows], (rows, lanes))
    for g in range(1, groups):
        total = jnp.where(lane == g, jnp.broadcast_to(x[g * rows : (g + 1) * rows], (rows, lanes)), total)
    return total


def spread(x, groups):
    rows, lanes = x.shape
    lane = iota((rows, lanes), 1) // HEAD_DIMENSION
    return merge_rows([jnp.where(lane == g, x, 0.0) for g in range(groups)]).astype(BF16)


def pack_stats(peak, total):
    lane = iota(peak.shape, 1)
    return jnp.where(lane % HEAD_DIMENSION < HEAD_DIMENSION // 2, peak, total)


def unpack_stats(stats):
    half = HEAD_DIMENSION // 2
    low = iota(stats.shape, 1) % HEAD_DIMENSION < half
    return (
        jnp.where(low, stats, pltpu.roll(stats, half, 1)),
        jnp.where(low, pltpu.roll(stats, stats.shape[1] - half, 1), stats),
    )


def section(shape):
    return iota(shape, 1) % (HEAD_DIMENSION // 2) // 8


def write_packed(out, part):
    n = part.shape[0] // 2
    out[0:n] = part[0:n].astype(BF16)
    stats = part[n:]
    high = stats.astype(BF16).astype(F32)
    middle = (stats - high).astype(BF16).astype(F32)
    place = section(stats.shape)
    split = jnp.where(place == 0, high, jnp.where(place == 1, middle, stats - high - middle))
    out[n:] = jnp.where(place == 3, 0.0, split).astype(BF16)


def read_packed(ref):
    n = ref.shape[0] // 2
    split = ref[n:].astype(F32)
    lanes = split.shape[1]
    stats = split + pltpu.roll(split, lanes - 8, 1) + pltpu.roll(split, lanes - 16, 1)
    lane = iota(split.shape, 1) % HEAD_DIMENSION
    half = HEAD_DIMENSION // 2
    peak = jnp.where(lane < 8, stats, 0.0)
    total = jnp.where((lane >= half) & (lane < half + 8), stats, 0.0)
    for step in (8, 16):
        peak = peak + pltpu.roll(peak, step, 1)
        total = total + pltpu.roll(total, step, 1)
    peak = peak + pltpu.roll(peak, half, 1)
    total = total + pltpu.roll(total, lanes - half, 1)
    return peak, total, ref[0:n].astype(F32)


def soft(scores, live):
    masked = jnp.where(live, scores, NEGATIVE)
    peak = jnp.max(masked, axis=-1, keepdims=True)
    weights = jnp.where(live, jnp.exp(masked - peak), 0.0)
    return peak, weights.astype(BF16), jnp.sum(weights, axis=-1, keepdims=True)


def attend_blocks(steps, limits, heads, cores, keys, values, store):
    device = lax.axis_index("tp")
    requests, count, _ = keys.shape
    rows = steps * GROUP
    scale = HEAD_DIMENSION**-0.5
    pairs = [(s, r) for s in range(2) for r in range(requests)]
    columns = [pl.ds(pl.multiple_of((2 * s + cores[s]) * 128, 128), 128) for s in range(2)]
    scores = []
    for s, r in pairs:
        q = spread(heads[s, r * rows : (r + 1) * rows].astype(F32) * scale, GROUP)
        scores.append(
            lax.dot_general(q, keys[r, :, columns[s]], (((1,), (1,)), ((), ())), preferred_element_type=F32)
        )
    scores = merge_rows(scores)
    position = device * count + iota(scores.shape, 1)
    limit = merge_rows([limits[r, 0:rows] for _, r in pairs for _ in range(GROUP)])
    peak, weights, total = soft(scores, position < limit)
    n = GROUP * rows
    for i, (s, r) in enumerate(pairs):
        own = slice(i * n, (i + 1) * n)
        summed = jnp.dot(weights[own], values[r, :, columns[s]], preferred_element_type=F32)
        store(s, r * rows, fold(summed, rows, 128))
        store(s, (requests + r) * rows, pack_stats(fold(peak[own], rows, 128), fold(total[own], rows, 128)))


def attend_own_kernel(steps, limits, own, keys, values, out):
    def store(s, row, x):
        out[s, row : row + x.shape[0], :] = x

    attend_blocks(steps, limits, own, [near_core(s) for s in range(2)], keys, values, store)


def attend_sibling_kernel(steps, limits, sibling, keys, values, blocks_own, out0, out1, out2, out3, blocks):
    device = lax.axis_index("tp")
    chip = device // 2
    near = [near_core(s) for s in range(2)]

    def store(s, row, x):
        blocks[2 * s + 1 - near[s], row : row + x.shape[0], :] = x

    for s in range(2):
        blocks[2 * s + near[s]] = blocks_own[s]
    attend_blocks(steps, limits, sibling, [1 - x for x in near], keys, values, store)
    out0[...] = blocks[chip]
    for k, out in ((1, out1), (2, out2), (3, out3)):
        write_packed(out, blocks[partner(chip, k)])


def fresh_part(requests, steps, own, sibling, after, out):
    device = lax.axis_index("tp")
    chip = device // 2
    rows = steps * GROUP
    tokens = requests * steps
    n = requests * rows

    def held(s, at_core):
        return jnp.where(near_core(s) == at_core, own[s].astype(F32), sibling[s].astype(F32))

    def pick(x):
        return jnp.where(chip % 2 == 1, x[tokens:], x[:tokens]).astype(BF16)

    new_keys, new_values = pick(held(2, chip // 2)), pick(held(3, chip // 2))
    q = spread(held(chip // 2, chip % 2) * HEAD_DIMENSION**-0.5, GROUP)
    scores = lax.dot_general(q, new_keys, (((1,), (1,)), ((), ())), preferred_element_type=F32)
    row, column = iota(scores.shape, 0) % n, iota(scores.shape, 1)
    live = (row // rows == column // steps) & (column % steps <= row % steps)
    peak, weights, total = soft(scores, live)
    summed = jnp.dot(weights, new_values, preferred_element_type=F32)
    out[0:n] = fold(summed, n, 128)
    out[n : 2 * n] = pack_stats(fold(peak, n, 128), fold(total, n, 128))


def join(a, b):
    peak = jnp.maximum(a[0], b[0])
    left, right = jnp.exp(a[0] - peak), jnp.exp(b[0] - peak)
    return peak, a[1] * left + b[1] * right, a[2] * left + b[2] * right


def read_part(ref):
    n = ref.shape[0] // 2
    return (*unpack_stats(ref[n:]), ref[0:n])


def join_kernel(order, a, b, c, d, fetched, out):
    a, b, c, d = sort_chips(order, a, (b, c, d))
    peak, total, summed = join(
        join(read_part(a), read_packed(d)), join(read_packed(b), read_packed(c))
    )
    n = summed.shape[0]
    out[0:n] = summed
    out[n:] = pack_stats(peak, total)


def output_kernel(requests, steps, own, sibling, fresh, weight, sibling_weight, out):
    core = lax.axis_index("tp") % 2
    _, total, summed = join(join(read_part(own), read_part(sibling)), read_part(fresh))
    attended = summed / total
    rows = steps * GROUP
    heads = []
    for j in range(GROUP):
        heads.append(merge_rows([attended[r * rows + j * steps : r * rows + (j + 1) * steps] for r in range(requests)]))
    low = iota(heads[0].shape, 1) < HEAD_DIMENSION
    zero = jnp.where(low, heads[0], pltpu.roll(heads[1], HEAD_DIMENSION, 1))
    one = jnp.where(low, pltpu.roll(heads[0], HEAD_DIMENSION, 1), heads[1])
    mine = jnp.where(core == 0, zero, one).astype(BF16)
    theirs = jnp.where(core == 0, one, zero).astype(BF16)
    projected = jnp.dot(mine, weight[...], preferred_element_type=F32) + jnp.dot(
        theirs, sibling_weight[...], preferred_element_type=F32
    )
    out[...] = projected.astype(BF16)


def sort_chips(order, first, parts):
    return [first] + [part for _, part in sorted(zip(order, parts), key=lambda pair: pair[0])]


def gather_kernel(order, a, b, c, d, weight, out, same_weight):
    chip = lax.axis_index("tp") // 2
    own, *others = sort_chips(order, a, (b, c, d))
    out[chip] = own[...]
    for back, x in zip((2, 1, 3), others):
        out[partner(chip, back)] = x[...]


def sum_chips(order, a, b, c, d):
    a, b, c, d = sort_chips(order, a, (b, c, d))
    return (a[...].astype(F32) + d[...].astype(F32)) + (b[...].astype(F32) + c[...].astype(F32))


def expert_kernel(order, inputs, a, b, c, d, ids, shares, down, *refs):
    *gate_up, out, residual_out = refs
    device = lax.axis_index("tp")
    residual = inputs[...] + sum_chips(order, a, b, c, d)
    residual_out[...] = residual
    normed = (
        residual * lax.rsqrt(jnp.mean(residual * residual, axis=-1, keepdims=True) + EPSILON)
    ).astype(BF16)
    requests = ids.shape[0]
    chosen = merge_rows([ids[r] for r in range(requests)])
    share = merge_rows([shares[r].astype(F32) for r in range(requests)]) * (1.0 / 65536.0)
    gate_up = [ref.at[i] for ref in gate_up for i in range(ref.shape[0])]
    experts = len(gate_up)
    total = None
    for e in range(experts):
        united = jnp.dot(normed, gate_up[e][...], preferred_element_type=F32)
        width = united.shape[1] // 2
        gate, up = united[:, :width], united[:, width:]
        active = (gate / (1.0 + jnp.exp(-gate)) * up).astype(BF16)
        outcome = jnp.dot(active, down[e], preferred_element_type=F32)
        factor = jnp.sum(jnp.where(chosen == device * experts + e, share, 0.0), axis=-1, keepdims=True)
        total = factor * outcome if total is None else total + factor * outcome
    out[...] = total.astype(BF16)


def final_kernel(order, requests, steps, residual, a, b, c, d, out):
    result = residual[...] + sum_chips(order, a, b, c, d)
    for r in range(requests):
        out[r] = result[r * steps : (r + 1) * steps].astype(BF16)


def partner(chip, k):
    outer = (chip == 0) | (chip == 3)
    if k == 3:
        return chip ^ 3
    return jnp.where(outer, chip ^ k, chip ^ (3 - k))


def other_chip(x, k, devices):
    to = {1: (1, 3, 0, 2), 2: (2, 0, 3, 1), 3: (3, 2, 1, 0)}[k]
    return lax.ppermute(x, "tp", [(i, 2 * to[i // 2] + 1 - i % 2) for i in range(devices)])


def near_core(s):
    device = lax.axis_index("tp")
    core = device % 2
    return jnp.where(device // 2 == s, core, 1 - core)


def to_chips(parts, devices, order):
    return [parts[0]] + [other_chip(parts[k], k, devices) for k in order]


def other_core(x, devices):
    return lax.ppermute(x, "tp", [(i, i ^ 1) for i in range(devices)])


def fast_device(
    hidden_states,
    lengths,
    qkv_weight,
    rotated_key_cache,
    earlier_value_cache,
    out_weight,
    expert_ids,
    combine_weights,
    gate_up_weight,
    down_weight,
):
    requests, steps, model_width = hidden_states.shape
    tokens = requests * steps
    devices = lax.axis_size("tp")
    chips = devices // 2
    rows = tokens * GROUP
    heads, limits, inputs = call(
        project_kernel,
        [((rows, 128), BF16), ((requests, 8, 128), jnp.int32), ((tokens, model_width), F32)],
        [lengths, hidden_states, qkv_weight],
        "project",
        cost=COST[0],
        stay=range(3),
        scratch=[
            pltpu.SMEM(lengths.shape, jnp.int32),
            pltpu.VMEM(hidden_states.shape, BF16),
            pltpu.VMEM(qkv_weight.shape, BF16),
            pltpu.SemaphoreType.DMA((3,)),
        ],
    )
    caches = [(rotated_key_cache, 0, requests), (earlier_value_cache, 0, requests)]
    small = [(x[None], 0, 1) for x in (out_weight, expert_ids, combine_weights)]
    experts = gate_up_weight.shape[0]
    cuts = [(0, SPLIT[0]), (SPLIT[0], SPLIT[1] - SPLIT[0]), (SPLIT[1], experts - SPLIT[1])]
    gate_up = [[(gate_up_weight, *cut)] if cut[1] else [] for cut in cuts]
    keys, values, own_weight, ids, shares, *gate_up_a = fetch(caches + small + gate_up[0], [heads], "fetch_cache")
    gathered, own_weight = call(
        functools.partial(gather_kernel, ORDER[0]),
        [((chips, rows, 128), BF16), (own_weight.shape, BF16)],
        [*to_chips([heads] * chips, devices, ORDER[0]), own_weight],
        "gather",
        same={chips: 1},
    )
    sibling_weight = other_core(own_weight[0], devices)
    sibling = other_core(gathered, devices)
    (blocks_own,) = call(
        functools.partial(attend_own_kernel, steps),
        [((chips // 2, 2 * rows, 128), F32)],
        [limits, gathered, keys, values],
        "attend_own",
        cost=COST[1],
    )
    parts = call(
        functools.partial(attend_sibling_kernel, steps),
        [((2 * rows, 128), F32)] + [((2 * rows, 128), BF16)] * (chips - 1),
        [limits, sibling, keys, values, blocks_own],
        "attend",
        cost=COST[1],
        scratch=[pltpu.VMEM((chips, 2 * rows, 128), F32)],
    )
    *gate_up_b, fresh = fetch(
        gate_up[1],
        [gathered, sibling, parts[0]],
        "fetch_b",
        beside=functools.partial(fresh_part, requests, steps),
        outs=[((2 * rows, 128), F32)],
    )
    arrived = to_chips(parts[:chips], devices, ORDER[1])
    (joined,) = call(functools.partial(join_kernel, ORDER[1]), [((2 * rows, 128), F32)], [*arrived, gate_up_b[0]], "join", cost=COST[2])
    (projected,) = call(
        functools.partial(output_kernel, requests, steps),
        [((tokens, model_width), BF16)],
        [joined, other_core(joined, devices), fresh, own_weight[0], sibling_weight],
        "output",
        cost=COST[2],
    )
    projections = to_chips([projected] * chips, devices, ORDER[2])
    *gate_up_c, down = fetch(gate_up[2] + [(down_weight, 0, experts)], [projected], "fetch_c")
    mixture, residual = call(
        functools.partial(expert_kernel, ORDER[2]),
        [((tokens, model_width), BF16), ((tokens, model_width), F32)],
        [inputs, *projections, ids[0], shares[0], down, *gate_up_a, *gate_up_b, *gate_up_c],
        "experts",
        cost=COST[3],
    )
    mixture = (mixture.astype(F32) + other_core(mixture, devices).astype(F32)).astype(BF16)
    mixtures = to_chips([mixture] * chips, devices, ORDER[3])
    (result,) = call(
        functools.partial(final_kernel, ORDER[3], requests, steps),
        [(hidden_states.shape, BF16)],
        [residual, *mixtures],
        "final",
        hbm_out=True,
    )
    return result


def merged(part, axis, combine):
    gathered = jax.tree.map(lambda a: lax.all_gather(a, axis), part)

    def take(source):
        return jax.tree.map(lambda a: lax.dynamic_index_in_dim(a, source, 0, False), gathered)

    return lax.fori_loop(
        1, lax.axis_size(axis), lambda source, state: combine(state, take(source)), take(0)
    )


def rms_rows(value_rows):
    return value_rows * lax.rsqrt(
        jnp.mean(value_rows * value_rows, axis=-1, keepdims=True) + EPSILON
    )


def apply_rotation(value_rows, position_index):
    half_width = value_rows.shape[-1] // 2
    rates = ROPE_BASE ** (-2.0 * jnp.arange(half_width, dtype=jnp.float32) / value_rows.shape[-1])
    angles = position_index[:, None, None] * rates
    cosine = jnp.cos(angles)
    sines = jnp.sin(angles)
    front_half = value_rows[..., :half_width]
    back_half = value_rows[..., half_width:]
    return jnp.concatenate(
        [front_half * cosine - back_half * sines, back_half * cosine + front_half * sines], axis=-1
    )


def join_parts(earlier, later):
    highest = jnp.maximum(earlier[0], later[0])
    scale_earlier = jnp.exp(earlier[0] - highest)
    scale_later = jnp.exp(later[0] - highest)
    weight_sum = earlier[1] * scale_earlier + later[1] * scale_later
    value_sum = earlier[2] * scale_earlier[..., None] + later[2] * scale_later[..., None]
    return (highest, weight_sum, value_sum)


def to_columns(value_rows, step_number, group_count):
    request_list, kv_heads, _, head_size = value_rows.shape
    return (
        value_rows.reshape(request_list, kv_heads, step_number, group_count, head_size)
        .transpose(0, 2, 1, 3, 4)
        .reshape(request_list * step_number, kv_heads * group_count * head_size)
    )


def expert_terms(normed, chosen, shares, gate_up_weight, down_weight, first_expert):
    ff_width = down_weight.shape[1]
    united_out = jnp.einsum(
        "nd,edf->enf", normed, gate_up_weight, preferred_element_type=jnp.float32
    )
    activation = (jax.nn.silu(united_out[..., :ff_width]) * united_out[..., ff_width:]).astype(
        jnp.bfloat16
    )
    outcome = jnp.einsum(
        "enf,efd->end", activation, down_weight, preferred_element_type=jnp.float32
    )
    owners = first_expert + jnp.arange(gate_up_weight.shape[0], dtype=jnp.int32)
    factors = jnp.sum(
        jnp.where(chosen[None, :, :] == owners[:, None, None], shares[None, :, :], 0.0), axis=-1
    )
    return jnp.sum(factors[:, :, None] * outcome, axis=0)


def general_device(
    hidden_states,
    lengths,
    qkv_weight,
    rotated_key_cache,
    earlier_value_cache,
    out_weight,
    expert_ids,
    combine_weights,
    gate_up_weight,
    down_weight,
):
    request_list, step_number, model_width = hidden_states.shape
    token_rows = request_list * step_number
    group_count = QUERY_HEADS // KEY_VALUE_HEADS
    query_total_width = QUERY_HEADS * HEAD_DIMENSION
    key_value_width = KEY_VALUE_HEADS * HEAD_DIMENSION
    score_scale = HEAD_DIMENSION ** (-0.5)
    inputs_flat = hidden_states.reshape(token_rows, model_width)
    normed = rms_rows(inputs_flat.astype(jnp.float32)).astype(jnp.bfloat16)
    projected_part = lax.dot_general(
        qkv_weight, normed, (((1,), (1,)), ((), ())), preferred_element_type=jnp.float32
    ).astype(jnp.bfloat16)
    projected_all = lax.all_gather(projected_part, "tp", axis=0, tiled=True)
    query_key_value_rows = projected_all.T
    position_index = (
        (lengths[:, None] + jnp.arange(step_number, dtype=jnp.int32)[None, :])
        .reshape(token_rows)
        .astype(jnp.float32)
    )
    query_rows = apply_rotation(
        query_key_value_rows[:, :query_total_width]
        .reshape(token_rows, QUERY_HEADS, HEAD_DIMENSION)
        .astype(jnp.float32),
        position_index,
    ).astype(jnp.bfloat16)
    fresh_keys = apply_rotation(
        query_key_value_rows[:, query_total_width : query_total_width + key_value_width]
        .reshape(token_rows, KEY_VALUE_HEADS, HEAD_DIMENSION)
        .astype(jnp.float32),
        position_index,
    ).astype(jnp.bfloat16)
    fresh_values = query_key_value_rows[:, query_total_width + key_value_width :].reshape(
        request_list, step_number, KEY_VALUE_HEADS, HEAD_DIMENSION
    )
    grouped_rows = (
        query_rows.reshape(request_list, step_number, KEY_VALUE_HEADS, group_count, HEAD_DIMENSION)
        .transpose(0, 2, 1, 3, 4)
        .reshape(request_list, KEY_VALUE_HEADS, step_number * group_count, HEAD_DIMENSION)
    )
    cache_extent = rotated_key_cache.shape[1]
    stored_keys = rotated_key_cache.reshape(
        request_list, cache_extent, KEY_VALUE_HEADS, HEAD_DIMENSION
    )
    stored_values = earlier_value_cache.reshape(
        request_list, cache_extent, KEY_VALUE_HEADS, HEAD_DIMENSION
    )
    scores = (
        jnp.einsum("bgqd,bcgd->bgqc", grouped_rows, stored_keys, preferred_element_type=jnp.float32)
        * score_scale
    )
    start_pos = lax.axis_index("tp") * cache_extent
    live_rows = (start_pos + jnp.arange(cache_extent, dtype=jnp.int32))[None, :] < lengths[:, None]
    live_mask = live_rows[:, None, None, :]
    masked = jnp.where(live_mask, scores, NEGATIVE)
    highest = jnp.max(masked, axis=-1)
    weights = jnp.where(live_mask, jnp.exp(masked - highest[..., None]), 0.0)
    weight_sum = jnp.sum(weights, axis=-1)
    value_sum = jnp.einsum(
        "bgqc,bcgd->bgqd",
        weights.astype(jnp.bfloat16),
        stored_values,
        preferred_element_type=jnp.float32,
    )
    feature_rows = out_weight.shape[0]
    column_begin = lax.axis_index("tp") * feature_rows
    top_score, total_all, sum_all = merged((highest, weight_sum, value_sum), "tp", join_parts)
    grouped_keys = fresh_keys.reshape(request_list, step_number, KEY_VALUE_HEADS, HEAD_DIMENSION)
    new_scores = (
        jnp.einsum(
            "bgqd,bsgd->bgqs", grouped_rows, grouped_keys, preferred_element_type=jnp.float32
        )
        * score_scale
    )
    query_step = jnp.arange(step_number * group_count, dtype=jnp.int32) // group_count
    causal = jnp.arange(step_number, dtype=jnp.int32)[None, :] <= query_step[:, None]
    new_masked = jnp.where(causal, new_scores, NEGATIVE)
    final_peak = jnp.maximum(top_score, jnp.max(new_masked, axis=-1))
    new_weights = jnp.where(causal, jnp.exp(new_masked - final_peak[..., None]), 0.0)
    carried = jnp.exp(top_score - final_peak)
    denominator = total_all * carried + jnp.sum(new_weights, axis=-1)
    new_part = jnp.einsum(
        "bgqs,bsgd->bgqd",
        new_weights.astype(jnp.bfloat16),
        fresh_values,
        preferred_element_type=jnp.float32,
    )
    numerator = sum_all * carried[..., None] + new_part
    attended = to_columns(numerator / denominator[..., None], step_number, group_count).astype(
        jnp.bfloat16
    )
    attended_part = lax.dynamic_slice_in_dim(attended, column_begin, feature_rows, 1)
    first_expert = lax.axis_index("tp") * gate_up_weight.shape[0]
    chosen = expert_ids.reshape(token_rows, -1)
    shares = combine_weights.reshape(token_rows, -1).astype(jnp.float32) / 65536.0
    head_terms = jnp.dot(attended_part, out_weight, preferred_element_type=jnp.float32)
    projected_rows = lax.psum(head_terms, "tp")
    residual = inputs_flat.astype(jnp.float32) + projected_rows
    normed_second = rms_rows(residual).astype(jnp.bfloat16)
    mixture = lax.psum(
        expert_terms(
            normed_second, chosen, shares, gate_up_weight, down_weight, first_expert
        ).astype(jnp.bfloat16),
        "tp",
    ).astype(jnp.float32)
    final_result = (residual + mixture).astype(jnp.bfloat16)
    return final_result.reshape(request_list, step_number, model_width)


def solution(mesh):
    in_specs = (
        P("req", None, None),
        P("req"),
        P("tp", None),
        P("req", "tp", None),
        P("req", "tp", None),
        P("tp", None),
        P("req", None, None),
        P("req", None, None),
        P("tp", None, None),
        P("tp", None, None),
    )
    out_specs = P("req", None, None)
    per_device = fast_device if mesh.shape["tp"] == 8 else general_device
    return jax.shard_map(
        per_device, mesh=mesh, in_specs=in_specs, out_specs=out_specs, check_vma=False
    )
```

```python
import functools

import jax
import jax.numpy as jnp
from jax import lax
from jax.experimental import pallas as pl
from jax.experimental.pallas import tpu as pltpu
from jax.sharding import PartitionSpec as P

QUERY_HEADS = 16
KEY_VALUE_HEADS = 8
HEAD_DIMENSION = 64
GROUP = QUERY_HEADS // KEY_VALUE_HEADS
EPSILON = 1e-05
ROPE_BASE = 10000.0
NEGATIVE = -1e30
F32 = jnp.float32
BF16 = jnp.bfloat16
VMEM_LIMIT = 16 * 1024 * 1024
SPLIT = (0, 3)
ORDER = ((1, 2, 3), (3, 2, 1), (1, 2, 3), (2, 3, 1))
COST = (8_000_000, 6_000_000, 1_000_000, 12_000_000)


def iota(shape, dim):
    return lax.broadcasted_iota(jnp.int32, shape, dim)


def merge_rows(blocks):
    return jnp.concatenate(blocks, axis=0)


def on(space):
    return pl.BlockSpec(memory_space=space)


def call(kernel, outs, operands, name, stay=(), scratch=(), hbm_out=False, cost=0, same=()):
    operands = [
        pltpu.with_memory_space_constraint(x, pltpu.HBM) if i in stay else x for i, x in enumerate(operands)
    ]
    return pl.pallas_call(
        kernel,
        out_shape=[
            jax.ShapeDtypeStruct(s, d) if hbm_out else pltpu.VMEM(s, d) for s, d in outs
        ],
        in_specs=[on(pltpu.HBM if i in stay else pltpu.VMEM) for i in range(len(operands))],
        out_specs=[on(pltpu.VMEM) for _ in outs],
        scratch_shapes=list(scratch),
        input_output_aliases=dict(same),
        compiler_params=pltpu.CompilerParams(vmem_limit_bytes=VMEM_LIMIT),
        cost_estimate=pl.CostEstimate(flops=0, bytes_accessed=cost, transcendentals=0),
        name=name,
    )(*operands)


def start_all(pairs, semaphores):
    copies = [
        pltpu.make_async_copy(source, target, semaphores.at[i]) for i, (source, target) in enumerate(pairs)
    ]
    for copy in copies:
        copy.start()
    return copies


def project_kernel(
    lengths_in,
    hidden_in,
    weight_in,
    out,
    limits,
    inputs,
    lengths,
    hidden,
    weight,
    semaphores,
):
    copies = start_all(
        [
            (lengths_in, lengths),
            (hidden_in, hidden),
            (weight_in, weight),
        ],
        semaphores,
    )
    requests, steps, _ = hidden.shape
    device = lax.axis_index("tp")
    devices = lax.axis_size("tp")
    copies[1].wait()
    x = merge_rows([hidden[b].astype(F32) for b in range(requests)])
    inputs[...] = x
    normed = (x * lax.rsqrt(jnp.mean(x * x, axis=-1, keepdims=True) + EPSILON)).astype(BF16)
    copies[0].wait()
    tokens = requests * steps
    row = iota((tokens, 128), 0)
    lane = iota((tokens, 128), 1)
    position = jnp.zeros((tokens, 128), jnp.int32)
    for b in range(requests):
        position = jnp.where(row // steps == b, lengths[b] + row - b * steps, position)
        limits[b] = jnp.full(limits.shape[1:], lengths[b], jnp.int32)
    half = HEAD_DIMENSION // 2
    rates = jnp.exp((lane % half).astype(F32) * (-2.0 / HEAD_DIMENSION * 9.210340371976184))
    angles = position.astype(F32) * rates
    turned = device < devices * 3 // 4
    cosine = jnp.where(turned, jnp.cos(angles), 1.0)
    sine = jnp.where(turned, jnp.sin(angles), 0.0)
    first = lane % HEAD_DIMENSION < half
    sine = jnp.where(first, -sine, sine)
    copies[2].wait()
    y = lax.dot_general(normed, weight[...], (((1,), (1,)), ((), ())), preferred_element_type=F32)
    y = y.astype(BF16).astype(F32)
    parts = []
    for k in range(y.shape[1] // 128):
        v = y[:, k * 128 : (k + 1) * 128]
        other = jnp.where(first, pltpu.roll(v, 128 - half, 1), pltpu.roll(v, half, 1))
        parts.append(v * cosine + other * sine)
    a, b = parts
    low = lane < HEAD_DIMENSION
    even = jnp.where(low, a, pltpu.roll(b, HEAD_DIMENSION, 1))
    odd = jnp.where(low, pltpu.roll(a, HEAD_DIMENSION, 1), b)
    rows = []
    for r in range(requests):
        rows += [even[r * steps : (r + 1) * steps], odd[r * steps : (r + 1) * steps]]
    query = merge_rows(rows)
    plain = merge_rows([a, b])
    out[...] = jnp.where(device < devices // 2, query, plain).astype(BF16)


def fetch_kernel(pieces, beside, operands, *refs):
    count = len(pieces)
    inputs, sources = refs[:operands], refs[operands : operands + count]
    outs, semaphores = refs[operands + count : -1], refs[-1]
    targets = outs[:count]
    pairs = [
        (source.at[first + i], target.at[i])
        for source, target, (first, size) in zip(sources, targets, pieces)
        for i in range(size)
    ]
    copies = start_all(pairs, semaphores)
    if beside is not None:
        beside(*inputs, *outs[count:])
    for copy in copies:
        copy.wait()


def fetch(pieces, after, name, beside=None, outs=()):
    rows = [(first, size) for _, first, size in pieces]
    return call(
        functools.partial(fetch_kernel, rows, beside, len(after)),
        [((size,) + x.shape[1:], x.dtype) for x, _, size in pieces] + list(outs),
        [*after] + [x for x, _, _ in pieces],
        name,
        stay=range(len(after), len(after) + len(pieces)),
        scratch=[pltpu.SemaphoreType.DMA((sum(size for _, size in rows),))],
        cost=sum(x.size * 2 // x.shape[0] * size for x, _, size in pieces),
    )


def fold(x, rows, lanes):
    groups = lanes // HEAD_DIMENSION
    lane = iota((rows, lanes), 1) // HEAD_DIMENSION
    total = jnp.broadcast_to(x[0:rows], (rows, lanes))
    for g in range(1, groups):
        total = jnp.where(lane == g, jnp.broadcast_to(x[g * rows : (g + 1) * rows], (rows, lanes)), total)
    return total


def spread(x, groups):
    rows, lanes = x.shape
    lane = iota((rows, lanes), 1) // HEAD_DIMENSION
    return merge_rows([jnp.where(lane == g, x, 0.0) for g in range(groups)]).astype(BF16)


def pack_stats(peak, total):
    lane = iota(peak.shape, 1)
    return jnp.where(lane % HEAD_DIMENSION < HEAD_DIMENSION // 2, peak, total)


def unpack_stats(stats):
    half = HEAD_DIMENSION // 2
    low = iota(stats.shape, 1) % HEAD_DIMENSION < half
    return (
        jnp.where(low, stats, pltpu.roll(stats, half, 1)),
        jnp.where(low, pltpu.roll(stats, stats.shape[1] - half, 1), stats),
    )


def section(shape):
    return iota(shape, 1) % (HEAD_DIMENSION // 2) // 8


def write_packed(out, part):
    n = part.shape[0] // 2
    out[0:n] = part[0:n].astype(BF16)
    stats = part[n:]
    high = stats.astype(BF16).astype(F32)
    middle = (stats - high).astype(BF16).astype(F32)
    place = section(stats.shape)
    split = jnp.where(place == 0, high, jnp.where(place == 1, middle, stats - high - middle))
    out[n:] = jnp.where(place == 3, 0.0, split).astype(BF16)


def read_packed(ref):
    n = ref.shape[0] // 2
    split = ref[n:].astype(F32)
    lanes = split.shape[1]
    stats = split + pltpu.roll(split, lanes - 8, 1) + pltpu.roll(split, lanes - 16, 1)
    lane = iota(split.shape, 1) % HEAD_DIMENSION
    half = HEAD_DIMENSION // 2
    peak = jnp.where(lane < 8, stats, 0.0)
    total = jnp.where((lane >= half) & (lane < half + 8), stats, 0.0)
    for step in (8, 16):
        peak = peak + pltpu.roll(peak, step, 1)
        total = total + pltpu.roll(total, step, 1)
    peak = peak + pltpu.roll(peak, half, 1)
    total = total + pltpu.roll(total, lanes - half, 1)
    return peak, total, ref[0:n].astype(F32)


def soft(scores, live):
    masked = jnp.where(live, scores, NEGATIVE)
    peak = jnp.max(masked, axis=-1, keepdims=True)
    weights = jnp.where(live, jnp.exp(masked - peak), 0.0)
    return peak, weights.astype(BF16), jnp.sum(weights, axis=-1, keepdims=True)


def attend_blocks(steps, limits, heads, cores, keys, values, store):
    device = lax.axis_index("tp")
    requests, count, _ = keys.shape
    rows = steps * GROUP
    scale = HEAD_DIMENSION**-0.5
    pairs = [(s, r) for s in range(2) for r in range(requests)]
    columns = [pl.ds(pl.multiple_of((2 * s + cores[s]) * 128, 128), 128) for s in range(2)]
    queries = [heads[s].astype(F32) * scale for s in range(2)]
    scores = []
    for s, r in pairs:
        q = spread(queries[s][r * rows : (r + 1) * rows], GROUP)
        scores.append(
            lax.dot_general(q, keys[r, :, columns[s]], (((1,), (1,)), ((), ())), preferred_element_type=F32)
        )
    scores = merge_rows(scores)
    position = device * count + iota(scores.shape, 1)
    limit = merge_rows([limits[r, 0:rows] for _, r in pairs for _ in range(GROUP)])
    peak, weights, total = soft(scores, position < limit)
    n = GROUP * rows
    for i, (s, r) in enumerate(pairs):
        own = slice(i * n, (i + 1) * n)
        summed = jnp.dot(weights[own], values[r, :, columns[s]], preferred_element_type=F32)
        store(s, r * rows, fold(summed, rows, 128))
        store(s, (requests + r) * rows, pack_stats(fold(peak[own], rows, 128), fold(total[own], rows, 128)))


def attend_own_kernel(steps, limits, own, keys, values, out):
    def store(s, row, x):
        out[s, row : row + x.shape[0], :] = x

    attend_blocks(steps, limits, own, [near_core(s) for s in range(2)], keys, values, store)


def attend_sibling_kernel(steps, limits, sibling, keys, values, blocks_own, out0, out1, out2, out3, blocks):
    device = lax.axis_index("tp")
    chip = device // 2
    near = [near_core(s) for s in range(2)]

    def store(s, row, x):
        blocks[2 * s + 1 - near[s], row : row + x.shape[0], :] = x

    for s in range(2):
        blocks[2 * s + near[s]] = blocks_own[s]
    attend_blocks(steps, limits, sibling, [1 - x for x in near], keys, values, store)
    out0[...] = blocks[chip]
    for k, out in ((1, out1), (2, out2), (3, out3)):
        write_packed(out, blocks[partner(chip, k)])


def fresh_part(requests, steps, own, sibling, after, out):
    device = lax.axis_index("tp")
    chip = device // 2
    rows = steps * GROUP
    tokens = requests * steps
    n = requests * rows

    def held(s, at_core):
        return jnp.where(near_core(s) == at_core, own[s].astype(F32), sibling[s].astype(F32))

    def pick(x):
        return jnp.where(chip % 2 == 1, x[tokens:], x[:tokens]).astype(BF16)

    new_keys, new_values = pick(held(2, chip // 2)), pick(held(3, chip // 2))
    q = spread(held(chip // 2, chip % 2) * HEAD_DIMENSION**-0.5, GROUP)
    scores = lax.dot_general(q, new_keys, (((1,), (1,)), ((), ())), preferred_element_type=F32)
    row, column = iota(scores.shape, 0) % n, iota(scores.shape, 1)
    live = (row // rows == column // steps) & (column % steps <= row % steps)
    peak, weights, total = soft(scores, live)
    summed = jnp.dot(weights, new_values, preferred_element_type=F32)
    out[0:n] = fold(summed, n, 128)
    out[n : 2 * n] = pack_stats(fold(peak, n, 128), fold(total, n, 128))


def join(a, b):
    peak = jnp.maximum(a[0], b[0])
    left, right = jnp.exp(a[0] - peak), jnp.exp(b[0] - peak)
    return peak, a[1] * left + b[1] * right, a[2] * left + b[2] * right


def read_part(ref):
    n = ref.shape[0] // 2
    return (*unpack_stats(ref[n:]), ref[0:n])


def join_kernel(order, a, b, c, d, fetched, out):
    a, b, c, d = sort_chips(order, a, (b, c, d))
    peak, total, summed = join(
        join(read_part(a), read_packed(d)), join(read_packed(b), read_packed(c))
    )
    n = summed.shape[0]
    out[0:n] = summed
    out[n:] = pack_stats(peak, total)


def output_kernel(requests, steps, own, sibling, fresh, weight, sibling_weight, out):
    core = lax.axis_index("tp") % 2
    _, total, summed = join(join(read_part(own), read_part(sibling)), read_part(fresh))
    attended = summed / total
    rows = steps * GROUP
    heads = []
    for j in range(GROUP):
        heads.append(merge_rows([attended[r * rows + j * steps : r * rows + (j + 1) * steps] for r in range(requests)]))
    low = iota(heads[0].shape, 1) < HEAD_DIMENSION
    zero = jnp.where(low, heads[0], pltpu.roll(heads[1], HEAD_DIMENSION, 1))
    one = jnp.where(low, pltpu.roll(heads[0], HEAD_DIMENSION, 1), heads[1])
    mine = jnp.where(core == 0, zero, one).astype(BF16)
    theirs = jnp.where(core == 0, one, zero).astype(BF16)
    projected = jnp.dot(mine, weight[...], preferred_element_type=F32) + jnp.dot(
        theirs, sibling_weight[...], preferred_element_type=F32
    )
    out[...] = projected.astype(BF16)


def sort_chips(order, first, parts):
    return [first] + [part for _, part in sorted(zip(order, parts), key=lambda pair: pair[0])]


def gather_kernel(order, a, b, c, d, weight, out, same_weight):
    chip = lax.axis_index("tp") // 2
    own, *others = sort_chips(order, a, (b, c, d))
    out[chip] = own[...]
    for back, x in zip((2, 1, 3), others):
        out[partner(chip, back)] = x[...]


def sum_chips(order, a, b, c, d):
    a, b, c, d = sort_chips(order, a, (b, c, d))
    return (a[...].astype(F32) + d[...].astype(F32)) + (b[...].astype(F32) + c[...].astype(F32))


def expert_kernel(order, inputs, a, b, c, d, ids, shares, down, *refs):
    *gate_up, out, residual_out = refs
    device = lax.axis_index("tp")
    residual = inputs[...] + sum_chips(order, a, b, c, d)
    residual_out[...] = residual
    normed = (
        residual * lax.rsqrt(jnp.mean(residual * residual, axis=-1, keepdims=True) + EPSILON)
    ).astype(BF16)
    requests = ids.shape[0]
    chosen = merge_rows([ids[r] for r in range(requests)])
    share = merge_rows([shares[r].astype(F32) for r in range(requests)]) * (1.0 / 65536.0)
    gate_up = [ref.at[i] for ref in gate_up for i in range(ref.shape[0])]
    experts = len(gate_up)
    total = None
    for e in range(experts):
        united = jnp.dot(normed, gate_up[e][...], preferred_element_type=F32)
        width = united.shape[1] // 2
        gate, up = united[:, :width], united[:, width:]
        active = (gate / (1.0 + jnp.exp(-gate)) * up).astype(BF16)
        outcome = jnp.dot(active, down[e], preferred_element_type=F32)
        factor = jnp.sum(jnp.where(chosen == device * experts + e, share, 0.0), axis=-1, keepdims=True)
        total = factor * outcome if total is None else total + factor * outcome
    out[...] = total.astype(BF16)


def final_kernel(order, requests, steps, residual, a, b, c, d, out):
    result = residual[...] + sum_chips(order, a, b, c, d)
    for r in range(requests):
        out[r] = result[r * steps : (r + 1) * steps].astype(BF16)


def partner(chip, k):
    outer = (chip == 0) | (chip == 3)
    if k == 3:
        return chip ^ 3
    return jnp.where(outer, chip ^ k, chip ^ (3 - k))


def other_chip(x, k, devices):
    to = {1: (1, 3, 0, 2), 2: (2, 0, 3, 1), 3: (3, 2, 1, 0)}[k]
    return lax.ppermute(x, "tp", [(i, 2 * to[i // 2] + 1 - i % 2) for i in range(devices)])


def near_core(s):
    device = lax.axis_index("tp")
    core = device % 2
    return jnp.where(device // 2 == s, core, 1 - core)


def to_chips(parts, devices, order):
    return [parts[0]] + [other_chip(parts[k], k, devices) for k in order]


def other_core(x, devices):
    return lax.ppermute(x, "tp", [(i, i ^ 1) for i in range(devices)])


def fast_device(
    hidden_states,
    lengths,
    qkv_weight,
    rotated_key_cache,
    earlier_value_cache,
    out_weight,
    expert_ids,
    combine_weights,
    gate_up_weight,
    down_weight,
):
    requests, steps, model_width = hidden_states.shape
    tokens = requests * steps
    devices = lax.axis_size("tp")
    chips = devices // 2
    rows = tokens * GROUP
    heads, limits, inputs = call(
        project_kernel,
        [((rows, 128), BF16), ((requests, 8, 128), jnp.int32), ((tokens, model_width), F32)],
        [lengths, hidden_states, qkv_weight],
        "project",
        cost=COST[0],
        stay=range(3),
        scratch=[
            pltpu.SMEM(lengths.shape, jnp.int32),
            pltpu.VMEM(hidden_states.shape, BF16),
            pltpu.VMEM(qkv_weight.shape, BF16),
            pltpu.SemaphoreType.DMA((3,)),
        ],
    )
    caches = [(rotated_key_cache, 0, requests), (earlier_value_cache, 0, requests)]
    small = [(x[None], 0, 1) for x in (out_weight, expert_ids, combine_weights)]
    experts = gate_up_weight.shape[0]
    cuts = [(0, SPLIT[0]), (SPLIT[0], SPLIT[1] - SPLIT[0]), (SPLIT[1], experts - SPLIT[1])]
    gate_up = [[(gate_up_weight, *cut)] if cut[1] else [] for cut in cuts]
    keys, values, own_weight, ids, shares, *gate_up_a = fetch(caches + small + gate_up[0], [heads], "fetch_cache")
    gathered, own_weight = call(
        functools.partial(gather_kernel, ORDER[0]),
        [((chips, rows, 128), BF16), (own_weight.shape, BF16)],
        [*to_chips([heads] * chips, devices, ORDER[0]), own_weight],
        "gather",
        same={chips: 1},
    )
    sibling_weight = other_core(own_weight[0], devices)
    sibling = other_core(gathered, devices)
    (blocks_own,) = call(
        functools.partial(attend_own_kernel, steps),
        [((chips // 2, 2 * rows, 128), F32)],
        [limits, gathered, keys, values],
        "attend_own",
        cost=COST[1],
    )
    parts = call(
        functools.partial(attend_sibling_kernel, steps),
        [((2 * rows, 128), F32)] + [((2 * rows, 128), BF16)] * (chips - 1),
        [limits, sibling, keys, values, blocks_own],
        "attend",
        cost=COST[1],
        scratch=[pltpu.VMEM((chips, 2 * rows, 128), F32)],
    )
    *gate_up_b, fresh = fetch(
        gate_up[1],
        [gathered, sibling, parts[0]],
        "fetch_b",
        beside=functools.partial(fresh_part, requests, steps),
        outs=[((2 * rows, 128), F32)],
    )
    arrived = to_chips(parts[:chips], devices, ORDER[1])
    (joined,) = call(functools.partial(join_kernel, ORDER[1]), [((2 * rows, 128), F32)], [*arrived, gate_up_b[0]], "join", cost=COST[2])
    (projected,) = call(
        functools.partial(output_kernel, requests, steps),
        [((tokens, model_width), BF16)],
        [joined, other_core(joined, devices), fresh, own_weight[0], sibling_weight],
        "output",
        cost=COST[2],
    )
    projections = to_chips([projected] * chips, devices, ORDER[2])
    *gate_up_c, down = fetch(gate_up[2] + [(down_weight, 0, experts)], [projected], "fetch_c")
    mixture, residual = call(
        functools.partial(expert_kernel, ORDER[2]),
        [((tokens, model_width), BF16), ((tokens, model_width), F32)],
        [inputs, *projections, ids[0], shares[0], down, *gate_up_a, *gate_up_b, *gate_up_c],
        "experts",
        cost=COST[3],
    )
    mixture = (mixture.astype(F32) + other_core(mixture, devices).astype(F32)).astype(BF16)
    mixtures = to_chips([mixture] * chips, devices, ORDER[3])
    (result,) = call(
        functools.partial(final_kernel, ORDER[3], requests, steps),
        [(hidden_states.shape, BF16)],
        [residual, *mixtures],
        "final",
        hbm_out=True,
    )
    return result


def merged(part, axis, combine):
    gathered = jax.tree.map(lambda a: lax.all_gather(a, axis), part)

    def take(source):
        return jax.tree.map(lambda a: lax.dynamic_index_in_dim(a, source, 0, False), gathered)

    return lax.fori_loop(
        1, lax.axis_size(axis), lambda source, state: combine(state, take(source)), take(0)
    )


def rms_rows(value_rows):
    return value_rows * lax.rsqrt(
        jnp.mean(value_rows * value_rows, axis=-1, keepdims=True) + EPSILON
    )


def apply_rotation(value_rows, position_index):
    half_width = value_rows.shape[-1] // 2
    rates = ROPE_BASE ** (-2.0 * jnp.arange(half_width, dtype=jnp.float32) / value_rows.shape[-1])
    angles = position_index[:, None, None] * rates
    cosine = jnp.cos(angles)
    sines = jnp.sin(angles)
    front_half = value_rows[..., :half_width]
    back_half = value_rows[..., half_width:]
    return jnp.concatenate(
        [front_half * cosine - back_half * sines, back_half * cosine + front_half * sines], axis=-1
    )


def join_parts(earlier, later):
    highest = jnp.maximum(earlier[0], later[0])
    scale_earlier = jnp.exp(earlier[0] - highest)
    scale_later = jnp.exp(later[0] - highest)
    weight_sum = earlier[1] * scale_earlier + later[1] * scale_later
    value_sum = earlier[2] * scale_earlier[..., None] + later[2] * scale_later[..., None]
    return (highest, weight_sum, value_sum)


def to_columns(value_rows, step_number, group_count):
    request_list, kv_heads, _, head_size = value_rows.shape
    return (
        value_rows.reshape(request_list, kv_heads, step_number, group_count, head_size)
        .transpose(0, 2, 1, 3, 4)
        .reshape(request_list * step_number, kv_heads * group_count * head_size)
    )


def expert_terms(normed, chosen, shares, gate_up_weight, down_weight, first_expert):
    ff_width = down_weight.shape[1]
    united_out = jnp.einsum(
        "nd,edf->enf", normed, gate_up_weight, preferred_element_type=jnp.float32
    )
    activation = (jax.nn.silu(united_out[..., :ff_width]) * united_out[..., ff_width:]).astype(
        jnp.bfloat16
    )
    outcome = jnp.einsum(
        "enf,efd->end", activation, down_weight, preferred_element_type=jnp.float32
    )
    owners = first_expert + jnp.arange(gate_up_weight.shape[0], dtype=jnp.int32)
    factors = jnp.sum(
        jnp.where(chosen[None, :, :] == owners[:, None, None], shares[None, :, :], 0.0), axis=-1
    )
    return jnp.sum(factors[:, :, None] * outcome, axis=0)


def general_device(
    hidden_states,
    lengths,
    qkv_weight,
    rotated_key_cache,
    earlier_value_cache,
    out_weight,
    expert_ids,
    combine_weights,
    gate_up_weight,
    down_weight,
):
    request_list, step_number, model_width = hidden_states.shape
    token_rows = request_list * step_number
    group_count = QUERY_HEADS // KEY_VALUE_HEADS
    query_total_width = QUERY_HEADS * HEAD_DIMENSION
    key_value_width = KEY_VALUE_HEADS * HEAD_DIMENSION
    score_scale = HEAD_DIMENSION ** (-0.5)
    inputs_flat = hidden_states.reshape(token_rows, model_width)
    normed = rms_rows(inputs_flat.astype(jnp.float32)).astype(jnp.bfloat16)
    projected_part = lax.dot_general(
        qkv_weight, normed, (((1,), (1,)), ((), ())), preferred_element_type=jnp.float32
    ).astype(jnp.bfloat16)
    projected_all = lax.all_gather(projected_part, "tp", axis=0, tiled=True)
    query_key_value_rows = projected_all.T
    position_index = (
        (lengths[:, None] + jnp.arange(step_number, dtype=jnp.int32)[None, :])
        .reshape(token_rows)
        .astype(jnp.float32)
    )
    query_rows = apply_rotation(
        query_key_value_rows[:, :query_total_width]
        .reshape(token_rows, QUERY_HEADS, HEAD_DIMENSION)
        .astype(jnp.float32),
        position_index,
    ).astype(jnp.bfloat16)
    fresh_keys = apply_rotation(
        query_key_value_rows[:, query_total_width : query_total_width + key_value_width]
        .reshape(token_rows, KEY_VALUE_HEADS, HEAD_DIMENSION)
        .astype(jnp.float32),
        position_index,
    ).astype(jnp.bfloat16)
    fresh_values = query_key_value_rows[:, query_total_width + key_value_width :].reshape(
        request_list, step_number, KEY_VALUE_HEADS, HEAD_DIMENSION
    )
    grouped_rows = (
        query_rows.reshape(request_list, step_number, KEY_VALUE_HEADS, group_count, HEAD_DIMENSION)
        .transpose(0, 2, 1, 3, 4)
        .reshape(request_list, KEY_VALUE_HEADS, step_number * group_count, HEAD_DIMENSION)
    )
    cache_extent = rotated_key_cache.shape[1]
    stored_keys = rotated_key_cache.reshape(
        request_list, cache_extent, KEY_VALUE_HEADS, HEAD_DIMENSION
    )
    stored_values = earlier_value_cache.reshape(
        request_list, cache_extent, KEY_VALUE_HEADS, HEAD_DIMENSION
    )
    scores = (
        jnp.einsum("bgqd,bcgd->bgqc", grouped_rows, stored_keys, preferred_element_type=jnp.float32)
        * score_scale
    )
    start_pos = lax.axis_index("tp") * cache_extent
    live_rows = (start_pos + jnp.arange(cache_extent, dtype=jnp.int32))[None, :] < lengths[:, None]
    live_mask = live_rows[:, None, None, :]
    masked = jnp.where(live_mask, scores, NEGATIVE)
    highest = jnp.max(masked, axis=-1)
    weights = jnp.where(live_mask, jnp.exp(masked - highest[..., None]), 0.0)
    weight_sum = jnp.sum(weights, axis=-1)
    value_sum = jnp.einsum(
        "bgqc,bcgd->bgqd",
        weights.astype(jnp.bfloat16),
        stored_values,
        preferred_element_type=jnp.float32,
    )
    feature_rows = out_weight.shape[0]
    column_begin = lax.axis_index("tp") * feature_rows
    top_score, total_all, sum_all = merged((highest, weight_sum, value_sum), "tp", join_parts)
    grouped_keys = fresh_keys.reshape(request_list, step_number, KEY_VALUE_HEADS, HEAD_DIMENSION)
    new_scores = (
        jnp.einsum(
            "bgqd,bsgd->bgqs", grouped_rows, grouped_keys, preferred_element_type=jnp.float32
        )
        * score_scale
    )
    query_step = jnp.arange(step_number * group_count, dtype=jnp.int32) // group_count
    causal = jnp.arange(step_number, dtype=jnp.int32)[None, :] <= query_step[:, None]
    new_masked = jnp.where(causal, new_scores, NEGATIVE)
    final_peak = jnp.maximum(top_score, jnp.max(new_masked, axis=-1))
    new_weights = jnp.where(causal, jnp.exp(new_masked - final_peak[..., None]), 0.0)
    carried = jnp.exp(top_score - final_peak)
    denominator = total_all * carried + jnp.sum(new_weights, axis=-1)
    new_part = jnp.einsum(
        "bgqs,bsgd->bgqd",
        new_weights.astype(jnp.bfloat16),
        fresh_values,
        preferred_element_type=jnp.float32,
    )
    numerator = sum_all * carried[..., None] + new_part
    attended = to_columns(numerator / denominator[..., None], step_number, group_count).astype(
        jnp.bfloat16
    )
    attended_part = lax.dynamic_slice_in_dim(attended, column_begin, feature_rows, 1)
    first_expert = lax.axis_index("tp") * gate_up_weight.shape[0]
    chosen = expert_ids.reshape(token_rows, -1)
    shares = combine_weights.reshape(token_rows, -1).astype(jnp.float32) / 65536.0
    head_terms = jnp.dot(attended_part, out_weight, preferred_element_type=jnp.float32)
    projected_rows = lax.psum(head_terms, "tp")
    residual = inputs_flat.astype(jnp.float32) + projected_rows
    normed_second = rms_rows(residual).astype(jnp.bfloat16)
    mixture = lax.psum(
        expert_terms(
            normed_second, chosen, shares, gate_up_weight, down_weight, first_expert
        ).astype(jnp.bfloat16),
        "tp",
    ).astype(jnp.float32)
    final_result = (residual + mixture).astype(jnp.bfloat16)
    return final_result.reshape(request_list, step_number, model_width)


def solution(mesh):
    in_specs = (
        P("req", None, None),
        P("req"),
        P("tp", None),
        P("req", "tp", None),
        P("req", "tp", None),
        P("tp", None),
        P("req", None, None),
        P("req", None, None),
        P("tp", None, None),
        P("tp", None, None),
    )
    out_specs = P("req", None, None)
    per_device = fast_device if mesh.shape["tp"] == 8 else general_device
    return jax.shard_map(
        per_device, mesh=mesh, in_specs=in_specs, out_specs=out_specs, check_vma=False
    )
```

```python
import functools

import jax
import jax.numpy as jnp
from jax import lax
from jax.experimental import pallas as pl
from jax.experimental.pallas import tpu as pltpu
from jax.sharding import PartitionSpec as P

QUERY_HEADS = 16
KEY_VALUE_HEADS = 8
HEAD_DIMENSION = 64
GROUP = QUERY_HEADS // KEY_VALUE_HEADS
EPSILON = 1e-05
ROPE_BASE = 10000.0
NEGATIVE = -1e30
F32 = jnp.float32
BF16 = jnp.bfloat16
VMEM_LIMIT = 16 * 1024 * 1024
SPLIT = (0, 3)
ORDER = ((1, 2, 3), (3, 2, 1), (1, 2, 3), (2, 3, 1))
COST = (8_000_000, 6_000_000, 1_000_000, 12_000_000)


def iota(shape, dim):
    return lax.broadcasted_iota(jnp.int32, shape, dim)


def merge_rows(blocks):
    return jnp.concatenate(blocks, axis=0)


def on(space):
    return pl.BlockSpec(memory_space=space)


def call(kernel, outs, operands, name, stay=(), scratch=(), hbm_out=False, cost=0, same=()):
    operands = [
        pltpu.with_memory_space_constraint(x, pltpu.HBM) if i in stay else x for i, x in enumerate(operands)
    ]
    return pl.pallas_call(
        kernel,
        out_shape=[
            jax.ShapeDtypeStruct(s, d) if hbm_out else pltpu.VMEM(s, d) for s, d in outs
        ],
        in_specs=[on(pltpu.HBM if i in stay else pltpu.VMEM) for i in range(len(operands))],
        out_specs=[on(pltpu.VMEM) for _ in outs],
        scratch_shapes=list(scratch),
        input_output_aliases=dict(same),
        compiler_params=pltpu.CompilerParams(vmem_limit_bytes=VMEM_LIMIT),
        cost_estimate=pl.CostEstimate(flops=0, bytes_accessed=cost, transcendentals=0),
        name=name,
    )(*operands)


def start_all(pairs, semaphores):
    copies = [
        pltpu.make_async_copy(source, target, semaphores.at[i]) for i, (source, target) in enumerate(pairs)
    ]
    for copy in copies:
        copy.start()
    return copies


def project_kernel(
    lengths_in,
    hidden_in,
    weight_in,
    out,
    limits,
    inputs,
    lengths,
    hidden,
    weight,
    semaphores,
):
    copies = start_all(
        [
            (lengths_in, lengths),
            (hidden_in, hidden),
            (weight_in, weight),
        ],
        semaphores,
    )
    requests, steps, _ = hidden.shape
    device = lax.axis_index("tp")
    devices = lax.axis_size("tp")
    copies[1].wait()
    x = merge_rows([hidden[b].astype(F32) for b in range(requests)])
    inputs[...] = x
    normed = (x * lax.rsqrt(jnp.mean(x * x, axis=-1, keepdims=True) + EPSILON)).astype(BF16)
    copies[0].wait()
    tokens = requests * steps
    row = iota((tokens, 128), 0)
    lane = iota((tokens, 128), 1)
    position = jnp.zeros((tokens, 128), jnp.int32)
    for b in range(requests):
        position = jnp.where(row // steps == b, lengths[b] + row - b * steps, position)
        limits[b] = jnp.full(limits.shape[1:], lengths[b], jnp.int32)
    half = HEAD_DIMENSION // 2
    rates = jnp.exp((lane % half).astype(F32) * (-2.0 / HEAD_DIMENSION * 9.210340371976184))
    angles = position.astype(F32) * rates
    turned = device < devices * 3 // 4
    cosine = jnp.where(turned, jnp.cos(angles), 1.0)
    sine = jnp.where(turned, jnp.sin(angles), 0.0)
    first = lane % HEAD_DIMENSION < half
    sine = jnp.where(first, -sine, sine)
    copies[2].wait()
    y = lax.dot_general(normed, weight[...], (((1,), (1,)), ((), ())), preferred_element_type=F32)
    y = y.astype(BF16).astype(F32)
    parts = []
    for k in range(y.shape[1] // 128):
        v = y[:, k * 128 : (k + 1) * 128]
        other = jnp.where(first, pltpu.roll(v, 128 - half, 1), pltpu.roll(v, half, 1))
        parts.append(v * cosine + other * sine)
    a, b = parts
    low = lane < HEAD_DIMENSION
    even = jnp.where(low, a, pltpu.roll(b, HEAD_DIMENSION, 1))
    odd = jnp.where(low, pltpu.roll(a, HEAD_DIMENSION, 1), b)
    rows = []
    for r in range(requests):
        rows += [even[r * steps : (r + 1) * steps], odd[r * steps : (r + 1) * steps]]
    query = merge_rows(rows)
    plain = merge_rows([a, b])
    out[...] = jnp.where(device < devices // 2, query, plain).astype(BF16)


def fetch_kernel(pieces, beside, operands, *refs):
    count = len(pieces)
    inputs, sources = refs[:operands], refs[operands : operands + count]
    outs, semaphores = refs[operands + count : -1], refs[-1]
    targets = outs[:count]
    pairs = [
        (source.at[first + i], target.at[i])
        for source, target, (first, size) in zip(sources, targets, pieces)
        for i in range(size)
    ]
    copies = start_all(pairs, semaphores)
    if beside is not None:
        beside(*inputs, *outs[count:])
    for copy in copies:
        copy.wait()


def fetch(pieces, after, name, beside=None, outs=()):
    rows = [(first, size) for _, first, size in pieces]
    return call(
        functools.partial(fetch_kernel, rows, beside, len(after)),
        [((size,) + x.shape[1:], x.dtype) for x, _, size in pieces] + list(outs),
        [*after] + [x for x, _, _ in pieces],
        name,
        stay=range(len(after), len(after) + len(pieces)),
        scratch=[pltpu.SemaphoreType.DMA((sum(size for _, size in rows),))],
        cost=sum(x.size * 2 // x.shape[0] * size for x, _, size in pieces),
    )


def fold(x, rows, lanes):
    groups = lanes // HEAD_DIMENSION
    lane = iota((rows, lanes), 1) // HEAD_DIMENSION
    total = jnp.broadcast_to(x[0:rows], (rows, lanes))
    for g in range(1, groups):
        total = jnp.where(lane == g, jnp.broadcast_to(x[g * rows : (g + 1) * rows], (rows, lanes)), total)
    return total


def spread(x, groups):
    rows, lanes = x.shape
    lane = iota((rows, lanes), 1) // HEAD_DIMENSION
    return merge_rows([jnp.where(lane == g, x, 0.0) for g in range(groups)]).astype(BF16)


def pack_stats(peak, total):
    lane = iota(peak.shape, 1)
    return jnp.where(lane % HEAD_DIMENSION < HEAD_DIMENSION // 2, peak, total)


def unpack_stats(stats):
    half = HEAD_DIMENSION // 2
    low = iota(stats.shape, 1) % HEAD_DIMENSION < half
    return (
        jnp.where(low, stats, pltpu.roll(stats, half, 1)),
        jnp.where(low, pltpu.roll(stats, stats.shape[1] - half, 1), stats),
    )


def section(shape):
    return iota(shape, 1) % (HEAD_DIMENSION // 2) // 8


def write_packed(out, part):
    n = part.shape[0] // 2
    out[0:n] = part[0:n].astype(BF16)
    stats = part[n:]
    high = stats.astype(BF16).astype(F32)
    middle = (stats - high).astype(BF16).astype(F32)
    place = section(stats.shape)
    split = jnp.where(place == 0, high, jnp.where(place == 1, middle, stats - high - middle))
    out[n:] = jnp.where(place == 3, 0.0, split).astype(BF16)


def read_packed(refs):
    n = refs[0].shape[0] // 2
    shape = (128, 256)
    lane, column = iota(shape, 0), iota(shape, 1)
    piece = lane % HEAD_DIMENSION - jnp.where(column < 128, 0, HEAD_DIMENSION // 2)
    hit = (piece == 0) | (piece == 8) | (piece == 16)
    hit = hit & (lane // HEAD_DIMENSION == column % 128 // HEAD_DIMENSION)
    place = jnp.where(hit, 1.0, 0.0).astype(BF16)
    split = merge_rows([ref[n:] for ref in refs])
    stats = jnp.dot(split, place, preferred_element_type=F32)
    return [
        (stats[i * n : (i + 1) * n, :128], stats[i * n : (i + 1) * n, 128:], ref[0:n].astype(F32))
        for i, ref in enumerate(refs)
    ]


def soft(scores, live):
    masked = jnp.where(live, scores, NEGATIVE)
    peak = jnp.max(masked, axis=-1, keepdims=True)
    weights = jnp.where(live, jnp.exp(masked - peak), 0.0)
    return peak, weights.astype(BF16), jnp.sum(weights, axis=-1, keepdims=True)


def attend_blocks(steps, limits, heads, cores, keys, values, store):
    device = lax.axis_index("tp")
    requests, count, _ = keys.shape
    rows = steps * GROUP
    scale = HEAD_DIMENSION**-0.5
    pairs = [(s, r) for s in range(2) for r in range(requests)]
    columns = [pl.ds(pl.multiple_of((2 * s + cores[s]) * 128, 128), 128) for s in range(2)]
    queries = [heads[s].astype(F32) * scale for s in range(2)]
    scores = []
    for s, r in pairs:
        q = spread(queries[s][r * rows : (r + 1) * rows], GROUP)
        scores.append(
            lax.dot_general(q, keys[r, :, columns[s]], (((1,), (1,)), ((), ())), preferred_element_type=F32)
        )
    scores = merge_rows(scores)
    position = device * count + iota(scores.shape, 1)
    limit = merge_rows([limits[r, 0:rows] for _, r in pairs for _ in range(GROUP)])
    peak, weights, total = soft(scores, position < limit)
    n = GROUP * rows
    for i, (s, r) in enumerate(pairs):
        own = slice(i * n, (i + 1) * n)
        summed = jnp.dot(weights[own], values[r, :, columns[s]], preferred_element_type=F32)
        store(s, r * rows, fold(summed, rows, 128))
        store(s, (requests + r) * rows, pack_stats(fold(peak[own], rows, 128), fold(total[own], rows, 128)))


def attend_own_kernel(steps, limits, own, keys, values, out):
    def store(s, row, x):
        out[s, row : row + x.shape[0], :] = x

    attend_blocks(steps, limits, own, [near_core(s) for s in range(2)], keys, values, store)


def attend_sibling_kernel(steps, limits, sibling, keys, values, blocks_own, out0, out1, out2, out3, blocks):
    device = lax.axis_index("tp")
    chip = device // 2
    near = [near_core(s) for s in range(2)]

    def store(s, row, x):
        blocks[2 * s + 1 - near[s], row : row + x.shape[0], :] = x

    for s in range(2):
        blocks[2 * s + near[s]] = blocks_own[s]
    attend_blocks(steps, limits, sibling, [1 - x for x in near], keys, values, store)
    out0[...] = blocks[chip]
    for k, out in ((1, out1), (2, out2), (3, out3)):
        write_packed(out, blocks[partner(chip, k)])


def fresh_part(requests, steps, own, sibling, after, out):
    device = lax.axis_index("tp")
    chip = device // 2
    rows = steps * GROUP
    tokens = requests * steps
    n = requests * rows

    def held(s, at_core):
        return jnp.where(near_core(s) == at_core, own[s].astype(F32), sibling[s].astype(F32))

    def pick(x):
        return jnp.where(chip % 2 == 1, x[tokens:], x[:tokens]).astype(BF16)

    new_keys, new_values = pick(held(2, chip // 2)), pick(held(3, chip // 2))
    q = spread(held(chip // 2, chip % 2) * HEAD_DIMENSION**-0.5, GROUP)
    scores = lax.dot_general(q, new_keys, (((1,), (1,)), ((), ())), preferred_element_type=F32)
    row, column = iota(scores.shape, 0) % n, iota(scores.shape, 1)
    live = (row // rows == column // steps) & (column % steps <= row % steps)
    peak, weights, total = soft(scores, live)
    summed = jnp.dot(weights, new_values, preferred_element_type=F32)
    out[0:n] = fold(summed, n, 128)
    out[n : 2 * n] = pack_stats(fold(peak, n, 128), fold(total, n, 128))


def join(a, b):
    peak = jnp.maximum(a[0], b[0])
    left, right = jnp.exp(a[0] - peak), jnp.exp(b[0] - peak)
    return peak, a[1] * left + b[1] * right, a[2] * left + b[2] * right


def read_part(ref):
    n = ref.shape[0] // 2
    return (*unpack_stats(ref[n:]), ref[0:n])


def join_kernel(order, a, b, c, d, fetched, out):
    a, b, c, d = sort_chips(order, a, (b, c, d))
    b, c, d = read_packed((b, c, d))
    peak, total, summed = join(join(read_part(a), d), join(b, c))
    n = summed.shape[0]
    out[0:n] = summed
    out[n:] = pack_stats(peak, total)


def output_kernel(requests, steps, own, sibling, fresh, weight, sibling_weight, out):
    core = lax.axis_index("tp") % 2
    _, total, summed = join(join(read_part(own), read_part(sibling)), read_part(fresh))
    attended = summed / total
    rows = steps * GROUP
    heads = []
    for j in range(GROUP):
        heads.append(merge_rows([attended[r * rows + j * steps : r * rows + (j + 1) * steps] for r in range(requests)]))
    low = iota(heads[0].shape, 1) < HEAD_DIMENSION
    zero = jnp.where(low, heads[0], pltpu.roll(heads[1], HEAD_DIMENSION, 1))
    one = jnp.where(low, pltpu.roll(heads[0], HEAD_DIMENSION, 1), heads[1])
    mine = jnp.where(core == 0, zero, one).astype(BF16)
    theirs = jnp.where(core == 0, one, zero).astype(BF16)
    projected = jnp.dot(mine, weight[...], preferred_element_type=F32) + jnp.dot(
        theirs, sibling_weight[...], preferred_element_type=F32
    )
    out[...] = projected.astype(BF16)


def sort_chips(order, first, parts):
    return [first] + [part for _, part in sorted(zip(order, parts), key=lambda pair: pair[0])]


def gather_kernel(order, a, b, c, d, weight, out, same_weight):
    chip = lax.axis_index("tp") // 2
    own, *others = sort_chips(order, a, (b, c, d))
    out[chip] = own[...]
    for back, x in zip((2, 1, 3), others):
        out[partner(chip, back)] = x[...]


def sum_chips(order, a, b, c, d):
    a, b, c, d = sort_chips(order, a, (b, c, d))
    return (a[...].astype(F32) + d[...].astype(F32)) + (b[...].astype(F32) + c[...].astype(F32))


def expert_kernel(order, inputs, a, b, c, d, ids, shares, down, *refs):
    *gate_up, out, residual_out = refs
    device = lax.axis_index("tp")
    residual = inputs[...] + sum_chips(order, a, b, c, d)
    residual_out[...] = residual
    normed = (
        residual * lax.rsqrt(jnp.mean(residual * residual, axis=-1, keepdims=True) + EPSILON)
    ).astype(BF16)
    requests = ids.shape[0]
    chosen = merge_rows([ids[r] for r in range(requests)])
    share = merge_rows([shares[r].astype(F32) for r in range(requests)]) * (1.0 / 65536.0)
    gate_up = [ref.at[i] for ref in gate_up for i in range(ref.shape[0])]
    experts = len(gate_up)
    total = None
    for e in range(experts):
        united = jnp.dot(normed, gate_up[e][...], preferred_element_type=F32)
        width = united.shape[1] // 2
        gate, up = united[:, :width], united[:, width:]
        active = (gate / (1.0 + jnp.exp(-gate)) * up).astype(BF16)
        outcome = jnp.dot(active, down[e], preferred_element_type=F32)
        factor = jnp.sum(jnp.where(chosen == device * experts + e, share, 0.0), axis=-1, keepdims=True)
        total = factor * outcome if total is None else total + factor * outcome
    out[...] = total.astype(BF16)


def final_kernel(order, requests, steps, residual, a, b, c, d, out):
    result = residual[...] + sum_chips(order, a, b, c, d)
    for r in range(requests):
        out[r] = result[r * steps : (r + 1) * steps].astype(BF16)


def partner(chip, k):
    outer = (chip == 0) | (chip == 3)
    if k == 3:
        return chip ^ 3
    return jnp.where(outer, chip ^ k, chip ^ (3 - k))


def other_chip(x, k, devices):
    to = {1: (1, 3, 0, 2), 2: (2, 0, 3, 1), 3: (3, 2, 1, 0)}[k]
    return lax.ppermute(x, "tp", [(i, 2 * to[i // 2] + 1 - i % 2) for i in range(devices)])


def near_core(s):
    device = lax.axis_index("tp")
    core = device % 2
    return jnp.where(device // 2 == s, core, 1 - core)


def to_chips(parts, devices, order):
    return [parts[0]] + [other_chip(parts[k], k, devices) for k in order]


def other_core(x, devices):
    return lax.ppermute(x, "tp", [(i, i ^ 1) for i in range(devices)])


def fast_device(
    hidden_states,
    lengths,
    qkv_weight,
    rotated_key_cache,
    earlier_value_cache,
    out_weight,
    expert_ids,
    combine_weights,
    gate_up_weight,
    down_weight,
):
    requests, steps, model_width = hidden_states.shape
    tokens = requests * steps
    devices = lax.axis_size("tp")
    chips = devices // 2
    rows = tokens * GROUP
    heads, limits, inputs = call(
        project_kernel,
        [((rows, 128), BF16), ((requests, 8, 128), jnp.int32), ((tokens, model_width), F32)],
        [lengths, hidden_states, qkv_weight],
        "project",
        cost=COST[0],
        stay=range(3),
        scratch=[
            pltpu.SMEM(lengths.shape, jnp.int32),
            pltpu.VMEM(hidden_states.shape, BF16),
            pltpu.VMEM(qkv_weight.shape, BF16),
            pltpu.SemaphoreType.DMA((3,)),
        ],
    )
    caches = [(rotated_key_cache, 0, requests), (earlier_value_cache, 0, requests)]
    small = [(x[None], 0, 1) for x in (out_weight, expert_ids, combine_weights)]
    experts = gate_up_weight.shape[0]
    cuts = [(0, SPLIT[0]), (SPLIT[0], SPLIT[1] - SPLIT[0]), (SPLIT[1], experts - SPLIT[1])]
    gate_up = [[(gate_up_weight, *cut)] if cut[1] else [] for cut in cuts]
    keys, values, own_weight, ids, shares, *gate_up_a = fetch(caches + small + gate_up[0], [heads], "fetch_cache")
    gathered, own_weight = call(
        functools.partial(gather_kernel, ORDER[0]),
        [((chips, rows, 128), BF16), (own_weight.shape, BF16)],
        [*to_chips([heads] * chips, devices, ORDER[0]), own_weight],
        "gather",
        same={chips: 1},
    )
    sibling_weight = other_core(own_weight[0], devices)
    sibling = other_core(gathered, devices)
    (blocks_own,) = call(
        functools.partial(attend_own_kernel, steps),
        [((chips // 2, 2 * rows, 128), F32)],
        [limits, gathered, keys, values],
        "attend_own",
        cost=COST[1],
    )
    parts = call(
        functools.partial(attend_sibling_kernel, steps),
        [((2 * rows, 128), F32)] + [((2 * rows, 128), BF16)] * (chips - 1),
        [limits, sibling, keys, values, blocks_own],
        "attend",
        cost=COST[1],
        scratch=[pltpu.VMEM((chips, 2 * rows, 128), F32)],
    )
    *gate_up_b, fresh = fetch(
        gate_up[1],
        [gathered, sibling, parts[0]],
        "fetch_b",
        beside=functools.partial(fresh_part, requests, steps),
        outs=[((2 * rows, 128), F32)],
    )
    arrived = to_chips(parts[:chips], devices, ORDER[1])
    (joined,) = call(functools.partial(join_kernel, ORDER[1]), [((2 * rows, 128), F32)], [*arrived, gate_up_b[0]], "join", cost=COST[2])
    (projected,) = call(
        functools.partial(output_kernel, requests, steps),
        [((tokens, model_width), BF16)],
        [joined, other_core(joined, devices), fresh, own_weight[0], sibling_weight],
        "output",
        cost=COST[2],
    )
    projections = to_chips([projected] * chips, devices, ORDER[2])
    *gate_up_c, down = fetch(gate_up[2] + [(down_weight, 0, experts)], [projected], "fetch_c")
    mixture, residual = call(
        functools.partial(expert_kernel, ORDER[2]),
        [((tokens, model_width), BF16), ((tokens, model_width), F32)],
        [inputs, *projections, ids[0], shares[0], down, *gate_up_a, *gate_up_b, *gate_up_c],
        "experts",
        cost=COST[3],
    )
    mixture = (mixture.astype(F32) + other_core(mixture, devices).astype(F32)).astype(BF16)
    mixtures = to_chips([mixture] * chips, devices, ORDER[3])
    (result,) = call(
        functools.partial(final_kernel, ORDER[3], requests, steps),
        [(hidden_states.shape, BF16)],
        [residual, *mixtures],
        "final",
        hbm_out=True,
    )
    return result


def merged(part, axis, combine):
    gathered = jax.tree.map(lambda a: lax.all_gather(a, axis), part)

    def take(source):
        return jax.tree.map(lambda a: lax.dynamic_index_in_dim(a, source, 0, False), gathered)

    return lax.fori_loop(
        1, lax.axis_size(axis), lambda source, state: combine(state, take(source)), take(0)
    )


def rms_rows(value_rows):
    return value_rows * lax.rsqrt(
        jnp.mean(value_rows * value_rows, axis=-1, keepdims=True) + EPSILON
    )


def apply_rotation(value_rows, position_index):
    half_width = value_rows.shape[-1] // 2
    rates = ROPE_BASE ** (-2.0 * jnp.arange(half_width, dtype=jnp.float32) / value_rows.shape[-1])
    angles = position_index[:, None, None] * rates
    cosine = jnp.cos(angles)
    sines = jnp.sin(angles)
    front_half = value_rows[..., :half_width]
    back_half = value_rows[..., half_width:]
    return jnp.concatenate(
        [front_half * cosine - back_half * sines, back_half * cosine + front_half * sines], axis=-1
    )


def join_parts(earlier, later):
    highest = jnp.maximum(earlier[0], later[0])
    scale_earlier = jnp.exp(earlier[0] - highest)
    scale_later = jnp.exp(later[0] - highest)
    weight_sum = earlier[1] * scale_earlier + later[1] * scale_later
    value_sum = earlier[2] * scale_earlier[..., None] + later[2] * scale_later[..., None]
    return (highest, weight_sum, value_sum)


def to_columns(value_rows, step_number, group_count):
    request_list, kv_heads, _, head_size = value_rows.shape
    return (
        value_rows.reshape(request_list, kv_heads, step_number, group_count, head_size)
        .transpose(0, 2, 1, 3, 4)
        .reshape(request_list * step_number, kv_heads * group_count * head_size)
    )


def expert_terms(normed, chosen, shares, gate_up_weight, down_weight, first_expert):
    ff_width = down_weight.shape[1]
    united_out = jnp.einsum(
        "nd,edf->enf", normed, gate_up_weight, preferred_element_type=jnp.float32
    )
    activation = (jax.nn.silu(united_out[..., :ff_width]) * united_out[..., ff_width:]).astype(
        jnp.bfloat16
    )
    outcome = jnp.einsum(
        "enf,efd->end", activation, down_weight, preferred_element_type=jnp.float32
    )
    owners = first_expert + jnp.arange(gate_up_weight.shape[0], dtype=jnp.int32)
    factors = jnp.sum(
        jnp.where(chosen[None, :, :] == owners[:, None, None], shares[None, :, :], 0.0), axis=-1
    )
    return jnp.sum(factors[:, :, None] * outcome, axis=0)


def general_device(
    hidden_states,
    lengths,
    qkv_weight,
    rotated_key_cache,
    earlier_value_cache,
    out_weight,
    expert_ids,
    combine_weights,
    gate_up_weight,
    down_weight,
):
    request_list, step_number, model_width = hidden_states.shape
    token_rows = request_list * step_number
    group_count = QUERY_HEADS // KEY_VALUE_HEADS
    query_total_width = QUERY_HEADS * HEAD_DIMENSION
    key_value_width = KEY_VALUE_HEADS * HEAD_DIMENSION
    score_scale = HEAD_DIMENSION ** (-0.5)
    inputs_flat = hidden_states.reshape(token_rows, model_width)
    normed = rms_rows(inputs_flat.astype(jnp.float32)).astype(jnp.bfloat16)
    projected_part = lax.dot_general(
        qkv_weight, normed, (((1,), (1,)), ((), ())), preferred_element_type=jnp.float32
    ).astype(jnp.bfloat16)
    projected_all = lax.all_gather(projected_part, "tp", axis=0, tiled=True)
    query_key_value_rows = projected_all.T
    position_index = (
        (lengths[:, None] + jnp.arange(step_number, dtype=jnp.int32)[None, :])
        .reshape(token_rows)
        .astype(jnp.float32)
    )
    query_rows = apply_rotation(
        query_key_value_rows[:, :query_total_width]
        .reshape(token_rows, QUERY_HEADS, HEAD_DIMENSION)
        .astype(jnp.float32),
        position_index,
    ).astype(jnp.bfloat16)
    fresh_keys = apply_rotation(
        query_key_value_rows[:, query_total_width : query_total_width + key_value_width]
        .reshape(token_rows, KEY_VALUE_HEADS, HEAD_DIMENSION)
        .astype(jnp.float32),
        position_index,
    ).astype(jnp.bfloat16)
    fresh_values = query_key_value_rows[:, query_total_width + key_value_width :].reshape(
        request_list, step_number, KEY_VALUE_HEADS, HEAD_DIMENSION
    )
    grouped_rows = (
        query_rows.reshape(request_list, step_number, KEY_VALUE_HEADS, group_count, HEAD_DIMENSION)
        .transpose(0, 2, 1, 3, 4)
        .reshape(request_list, KEY_VALUE_HEADS, step_number * group_count, HEAD_DIMENSION)
    )
    cache_extent = rotated_key_cache.shape[1]
    stored_keys = rotated_key_cache.reshape(
        request_list, cache_extent, KEY_VALUE_HEADS, HEAD_DIMENSION
    )
    stored_values = earlier_value_cache.reshape(
        request_list, cache_extent, KEY_VALUE_HEADS, HEAD_DIMENSION
    )
    scores = (
        jnp.einsum("bgqd,bcgd->bgqc", grouped_rows, stored_keys, preferred_element_type=jnp.float32)
        * score_scale
    )
    start_pos = lax.axis_index("tp") * cache_extent
    live_rows = (start_pos + jnp.arange(cache_extent, dtype=jnp.int32))[None, :] < lengths[:, None]
    live_mask = live_rows[:, None, None, :]
    masked = jnp.where(live_mask, scores, NEGATIVE)
    highest = jnp.max(masked, axis=-1)
    weights = jnp.where(live_mask, jnp.exp(masked - highest[..., None]), 0.0)
    weight_sum = jnp.sum(weights, axis=-1)
    value_sum = jnp.einsum(
        "bgqc,bcgd->bgqd",
        weights.astype(jnp.bfloat16),
        stored_values,
        preferred_element_type=jnp.float32,
    )
    feature_rows = out_weight.shape[0]
    column_begin = lax.axis_index("tp") * feature_rows
    top_score, total_all, sum_all = merged((highest, weight_sum, value_sum), "tp", join_parts)
    grouped_keys = fresh_keys.reshape(request_list, step_number, KEY_VALUE_HEADS, HEAD_DIMENSION)
    new_scores = (
        jnp.einsum(
            "bgqd,bsgd->bgqs", grouped_rows, grouped_keys, preferred_element_type=jnp.float32
        )
        * score_scale
    )
    query_step = jnp.arange(step_number * group_count, dtype=jnp.int32) // group_count
    causal = jnp.arange(step_number, dtype=jnp.int32)[None, :] <= query_step[:, None]
    new_masked = jnp.where(causal, new_scores, NEGATIVE)
    final_peak = jnp.maximum(top_score, jnp.max(new_masked, axis=-1))
    new_weights = jnp.where(causal, jnp.exp(new_masked - final_peak[..., None]), 0.0)
    carried = jnp.exp(top_score - final_peak)
    denominator = total_all * carried + jnp.sum(new_weights, axis=-1)
    new_part = jnp.einsum(
        "bgqs,bsgd->bgqd",
        new_weights.astype(jnp.bfloat16),
        fresh_values,
        preferred_element_type=jnp.float32,
    )
    numerator = sum_all * carried[..., None] + new_part
    attended = to_columns(numerator / denominator[..., None], step_number, group_count).astype(
        jnp.bfloat16
    )
    attended_part = lax.dynamic_slice_in_dim(attended, column_begin, feature_rows, 1)
    first_expert = lax.axis_index("tp") * gate_up_weight.shape[0]
    chosen = expert_ids.reshape(token_rows, -1)
    shares = combine_weights.reshape(token_rows, -1).astype(jnp.float32) / 65536.0
    head_terms = jnp.dot(attended_part, out_weight, preferred_element_type=jnp.float32)
    projected_rows = lax.psum(head_terms, "tp")
    residual = inputs_flat.astype(jnp.float32) + projected_rows
    normed_second = rms_rows(residual).astype(jnp.bfloat16)
    mixture = lax.psum(
        expert_terms(
            normed_second, chosen, shares, gate_up_weight, down_weight, first_expert
        ).astype(jnp.bfloat16),
        "tp",
    ).astype(jnp.float32)
    final_result = (residual + mixture).astype(jnp.bfloat16)
    return final_result.reshape(request_list, step_number, model_width)


def solution(mesh):
    in_specs = (
        P("req", None, None),
        P("req"),
        P("tp", None),
        P("req", "tp", None),
        P("req", "tp", None),
        P("tp", None),
        P("req", None, None),
        P("req", None, None),
        P("tp", None, None),
        P("tp", None, None),
    )
    out_specs = P("req", None, None)
    per_device = fast_device if mesh.shape["tp"] == 8 else general_device
    return jax.shard_map(
        per_device, mesh=mesh, in_specs=in_specs, out_specs=out_specs, check_vma=False
    )
```

```python
import functools

import jax
import jax.numpy as jnp
from jax import lax
from jax.experimental import pallas as pl
from jax.experimental.pallas import tpu as pltpu
from jax.sharding import PartitionSpec as P

QUERY_HEADS = 16
KEY_VALUE_HEADS = 8
HEAD_DIMENSION = 64
GROUP = QUERY_HEADS // KEY_VALUE_HEADS
EPSILON = 1e-05
ROPE_BASE = 10000.0
NEGATIVE = -1e30
F32 = jnp.float32
BF16 = jnp.bfloat16
VMEM_LIMIT = 16 * 1024 * 1024
SPLIT = (0, 3)
ORDER = ((1, 2, 3), (3, 2, 1), (1, 2, 3), (2, 3, 1))
COST = (8_000_000, 6_000_000, 1_000_000, 12_000_000)


def iota(shape, dim):
    return lax.broadcasted_iota(jnp.int32, shape, dim)


def merge_rows(blocks):
    return jnp.concatenate(blocks, axis=0)


def on(space):
    return pl.BlockSpec(memory_space=space)


def call(kernel, outs, operands, name, stay=(), scratch=(), hbm_out=False, cost=0, same=()):
    operands = [
        pltpu.with_memory_space_constraint(x, pltpu.HBM) if i in stay else x for i, x in enumerate(operands)
    ]
    return pl.pallas_call(
        kernel,
        out_shape=[
            jax.ShapeDtypeStruct(s, d) if hbm_out else pltpu.VMEM(s, d) for s, d in outs
        ],
        in_specs=[on(pltpu.HBM if i in stay else pltpu.VMEM) for i in range(len(operands))],
        out_specs=[on(pltpu.VMEM) for _ in outs],
        scratch_shapes=list(scratch),
        input_output_aliases=dict(same),
        compiler_params=pltpu.CompilerParams(vmem_limit_bytes=VMEM_LIMIT),
        cost_estimate=pl.CostEstimate(flops=0, bytes_accessed=cost, transcendentals=0),
        name=name,
    )(*operands)


def start_all(pairs, semaphores):
    copies = [
        pltpu.make_async_copy(source, target, semaphores.at[i]) for i, (source, target) in enumerate(pairs)
    ]
    for copy in copies:
        copy.start()
    return copies


def project_kernel(
    lengths_in,
    hidden_in,
    weight_in,
    out,
    limits,
    inputs,
    lengths,
    hidden,
    weight,
    semaphores,
):
    copies = start_all(
        [
            (lengths_in, lengths),
            (hidden_in, hidden),
            (weight_in, weight),
        ],
        semaphores,
    )
    requests, steps, _ = hidden.shape
    device = lax.axis_index("tp")
    devices = lax.axis_size("tp")
    copies[1].wait()
    x = merge_rows([hidden[b].astype(F32) for b in range(requests)])
    inputs[...] = x
    normed = (x * lax.rsqrt(jnp.mean(x * x, axis=-1, keepdims=True) + EPSILON)).astype(BF16)
    copies[0].wait()
    tokens = requests * steps
    row = iota((tokens, 128), 0)
    lane = iota((tokens, 128), 1)
    position = jnp.zeros((tokens, 128), jnp.int32)
    for b in range(requests):
        position = jnp.where(row // steps == b, lengths[b] + row - b * steps, position)
        limits[b] = jnp.full(limits.shape[1:], lengths[b], jnp.int32)
    half = HEAD_DIMENSION // 2
    rates = jnp.exp((lane % half).astype(F32) * (-2.0 / HEAD_DIMENSION * 9.210340371976184))
    angles = position.astype(F32) * rates
    turned = device < devices * 3 // 4
    cosine = jnp.where(turned, jnp.cos(angles), 1.0)
    sine = jnp.where(turned, jnp.sin(angles), 0.0)
    first = lane % HEAD_DIMENSION < half
    sine = jnp.where(first, -sine, sine)
    copies[2].wait()
    y = lax.dot_general(normed, weight[...], (((1,), (1,)), ((), ())), preferred_element_type=F32)
    y = y.astype(BF16).astype(F32)
    parts = []
    for k in range(y.shape[1] // 128):
        v = y[:, k * 128 : (k + 1) * 128]
        other = jnp.where(first, pltpu.roll(v, 128 - half, 1), pltpu.roll(v, half, 1))
        parts.append(v * cosine + other * sine)
    a, b = parts
    low = lane < HEAD_DIMENSION
    even = jnp.where(low, a, pltpu.roll(b, HEAD_DIMENSION, 1))
    odd = jnp.where(low, pltpu.roll(a, HEAD_DIMENSION, 1), b)
    rows = []
    for r in range(requests):
        rows += [even[r * steps : (r + 1) * steps], odd[r * steps : (r + 1) * steps]]
    query = merge_rows(rows)
    plain = merge_rows([a, b])
    out[...] = jnp.where(device < devices // 2, query, plain).astype(BF16)


def fetch_kernel(pieces, beside, operands, *refs):
    count = len(pieces)
    inputs, sources = refs[:operands], refs[operands : operands + count]
    outs, semaphores = refs[operands + count : -1], refs[-1]
    targets = outs[:count]
    pairs = [
        (source.at[first + i], target.at[i])
        for source, target, (first, size) in zip(sources, targets, pieces)
        for i in range(size)
    ]
    copies = start_all(pairs, semaphores)
    if beside is not None:
        beside(*inputs, *outs[count:])
    for copy in copies:
        copy.wait()


def fetch(pieces, after, name, beside=None, outs=()):
    rows = [(first, size) for _, first, size in pieces]
    return call(
        functools.partial(fetch_kernel, rows, beside, len(after)),
        [((size,) + x.shape[1:], x.dtype) for x, _, size in pieces] + list(outs),
        [*after] + [x for x, _, _ in pieces],
        name,
        stay=range(len(after), len(after) + len(pieces)),
        scratch=[pltpu.SemaphoreType.DMA((sum(size for _, size in rows),))],
        cost=sum(x.size * 2 // x.shape[0] * size for x, _, size in pieces),
    )


def fold(x, rows, lanes):
    groups = lanes // HEAD_DIMENSION
    lane = iota((rows, lanes), 1) // HEAD_DIMENSION
    total = jnp.broadcast_to(x[0:rows], (rows, lanes))
    for g in range(1, groups):
        total = jnp.where(lane == g, jnp.broadcast_to(x[g * rows : (g + 1) * rows], (rows, lanes)), total)
    return total


def spread(x, groups):
    rows, lanes = x.shape
    lane = iota((rows, lanes), 1) // HEAD_DIMENSION
    return merge_rows([jnp.where(lane == g, x, 0.0) for g in range(groups)]).astype(BF16)


def pack_stats(peak, total):
    lane = iota(peak.shape, 1)
    return jnp.where(lane % HEAD_DIMENSION < HEAD_DIMENSION // 2, peak, total)


def unpack_stats(stats):
    half = HEAD_DIMENSION // 2
    low = iota(stats.shape, 1) % HEAD_DIMENSION < half
    return (
        jnp.where(low, stats, pltpu.roll(stats, half, 1)),
        jnp.where(low, pltpu.roll(stats, stats.shape[1] - half, 1), stats),
    )


def section(shape):
    return iota(shape, 1) % (HEAD_DIMENSION // 2) // 8


def write_packed(out, part):
    n = part.shape[0] // 2
    out[0:n] = part[0:n].astype(BF16)
    stats = part[n:]
    high = stats.astype(BF16).astype(F32)
    middle = (stats - high).astype(BF16).astype(F32)
    place = section(stats.shape)
    split = jnp.where(place == 0, high, jnp.where(place == 1, middle, stats - high - middle))
    out[n:] = jnp.where(place == 3, 0.0, split).astype(BF16)


def read_packed(refs):
    n = refs[0].shape[0] // 2
    shape = (128, 256)
    lane, column = iota(shape, 0), iota(shape, 1)
    piece = lane % HEAD_DIMENSION - jnp.where(column < 128, 0, HEAD_DIMENSION // 2)
    hit = (piece == 0) | (piece == 8) | (piece == 16)
    hit = hit & (lane // HEAD_DIMENSION == column % 128 // HEAD_DIMENSION)
    place = jnp.where(hit, 1.0, 0.0).astype(BF16)
    split = merge_rows([ref[n:] for ref in refs])
    stats = jnp.dot(split, place, preferred_element_type=F32)
    return [
        (stats[i * n : (i + 1) * n, :128], stats[i * n : (i + 1) * n, 128:], ref[0:n].astype(F32))
        for i, ref in enumerate(refs)
    ]


def soft(scores, live):
    masked = jnp.where(live, scores, NEGATIVE)
    peak = jnp.max(masked, axis=-1, keepdims=True)
    weights = jnp.where(live, jnp.exp(masked - peak), 0.0)
    return peak, weights.astype(BF16), jnp.sum(weights, axis=-1, keepdims=True)


def attend_blocks(steps, limits, heads, cores, keys, values, store):
    device = lax.axis_index("tp")
    requests, count, _ = keys.shape
    rows = steps * GROUP
    scale = HEAD_DIMENSION**-0.5
    pairs = [(s, r) for s in range(2) for r in range(requests)]
    columns = [pl.ds(pl.multiple_of((2 * s + cores[s]) * 128, 128), 128) for s in range(2)]
    queries = [heads[s].astype(F32) * scale for s in range(2)]
    scores = []
    for s, r in pairs:
        q = spread(queries[s][r * rows : (r + 1) * rows], GROUP)
        scores.append(
            lax.dot_general(q, keys[r, :, columns[s]], (((1,), (1,)), ((), ())), preferred_element_type=F32)
        )
    scores = merge_rows(scores)
    position = device * count + iota(scores.shape, 1)
    limit = merge_rows([limits[r, 0:rows] for _, r in pairs for _ in range(GROUP)])
    peak, weights, total = soft(scores, position < limit)
    n = GROUP * rows
    for i, (s, r) in enumerate(pairs):
        own = slice(i * n, (i + 1) * n)
        summed = jnp.dot(weights[own], values[r, :, columns[s]], preferred_element_type=F32)
        store(s, r * rows, fold(summed, rows, 128))
        store(s, (requests + r) * rows, pack_stats(fold(peak[own], rows, 128), fold(total[own], rows, 128)))


def attend_own_kernel(steps, limits, own, keys, values, out):
    def store(s, row, x):
        out[s, row : row + x.shape[0], :] = x

    attend_blocks(steps, limits, own, [near_core(s) for s in range(2)], keys, values, store)


def attend_sibling_kernel(steps, limits, sibling, keys, values, blocks_own, out0, out1, out2, out3, blocks):
    device = lax.axis_index("tp")
    chip = device // 2
    near = [near_core(s) for s in range(2)]

    def store(s, row, x):
        blocks[2 * s + 1 - near[s], row : row + x.shape[0], :] = x

    for s in range(2):
        blocks[2 * s + near[s]] = blocks_own[s]
    attend_blocks(steps, limits, sibling, [1 - x for x in near], keys, values, store)
    out0[...] = blocks[chip]
    for k, out in ((1, out1), (2, out2), (3, out3)):
        write_packed(out, blocks[partner(chip, k)])


def fresh_part(requests, steps, own, sibling, after, out):
    device = lax.axis_index("tp")
    chip = device // 2
    rows = steps * GROUP
    tokens = requests * steps
    n = requests * rows

    def held(s, at_core):
        return jnp.where(near_core(s) == at_core, own[s].astype(F32), sibling[s].astype(F32))

    def pick(x):
        return jnp.where(chip % 2 == 1, x[tokens:], x[:tokens]).astype(BF16)

    new_keys, new_values = pick(held(2, chip // 2)), pick(held(3, chip // 2))
    q = spread(held(chip // 2, chip % 2) * HEAD_DIMENSION**-0.5, GROUP)
    scores = lax.dot_general(q, new_keys, (((1,), (1,)), ((), ())), preferred_element_type=F32)
    row, column = iota(scores.shape, 0) % n, iota(scores.shape, 1)
    live = (row // rows == column // steps) & (column % steps <= row % steps)
    peak, weights, total = soft(scores, live)
    summed = jnp.dot(weights, new_values, preferred_element_type=F32)
    out[0:n] = fold(summed, n, 128)
    out[n : 2 * n] = pack_stats(fold(peak, n, 128), fold(total, n, 128))


def join(a, b):
    peak = jnp.maximum(a[0], b[0])
    left, right = jnp.exp(a[0] - peak), jnp.exp(b[0] - peak)
    return peak, a[1] * left + b[1] * right, a[2] * left + b[2] * right


def read_part(ref):
    n = ref.shape[0] // 2
    return (*unpack_stats(ref[n:]), ref[0:n])


def join_kernel(order, a, b, c, d, fetched, out):
    a, b, c, d = sort_chips(order, a, (b, c, d))
    b, c, d = read_packed((b, c, d))
    peak, total, summed = join(join(read_part(a), d), join(b, c))
    n = summed.shape[0]
    out[0:n] = summed
    out[n:] = pack_stats(peak, total)


def output_kernel(requests, steps, own, sibling, fresh, weight, sibling_weight, out):
    core = lax.axis_index("tp") % 2
    _, total, summed = join(join(read_part(own), read_part(sibling)), read_part(fresh))
    attended = summed / total
    rows = steps * GROUP
    heads = []
    for j in range(GROUP):
        heads.append(merge_rows([attended[r * rows + j * steps : r * rows + (j + 1) * steps] for r in range(requests)]))
    low = iota(heads[0].shape, 1) < HEAD_DIMENSION
    zero = jnp.where(low, heads[0], pltpu.roll(heads[1], HEAD_DIMENSION, 1))
    one = jnp.where(low, pltpu.roll(heads[0], HEAD_DIMENSION, 1), heads[1])
    mine = jnp.where(core == 0, zero, one).astype(BF16)
    theirs = jnp.where(core == 0, one, zero).astype(BF16)
    projected = jnp.dot(mine, weight[...], preferred_element_type=F32) + jnp.dot(
        theirs, sibling_weight[...], preferred_element_type=F32
    )
    out[...] = projected.astype(BF16)


def sort_chips(order, first, parts):
    return [first] + [part for _, part in sorted(zip(order, parts), key=lambda pair: pair[0])]


def gather_kernel(order, a, b, c, d, weight, out):
    chip = lax.axis_index("tp") // 2
    own, *others = sort_chips(order, a, (b, c, d))
    out[chip] = own[...]
    for back, x in zip((2, 1, 3), others):
        out[partner(chip, back)] = x[...]


def sum_chips(order, a, b, c, d):
    a, b, c, d = sort_chips(order, a, (b, c, d))
    return (a[...].astype(F32) + d[...].astype(F32)) + (b[...].astype(F32) + c[...].astype(F32))


def expert_kernel(order, inputs, a, b, c, d, ids, shares, down, *refs):
    *gate_up, out, residual_out = refs
    device = lax.axis_index("tp")
    residual = inputs[...] + sum_chips(order, a, b, c, d)
    residual_out[...] = residual
    normed = (
        residual * lax.rsqrt(jnp.mean(residual * residual, axis=-1, keepdims=True) + EPSILON)
    ).astype(BF16)
    requests = ids.shape[0]
    chosen = merge_rows([ids[r] for r in range(requests)])
    share = merge_rows([shares[r].astype(F32) for r in range(requests)]) * (1.0 / 65536.0)
    gate_up = [ref.at[i] for ref in gate_up for i in range(ref.shape[0])]
    experts = len(gate_up)
    total = None
    for e in range(experts):
        united = jnp.dot(normed, gate_up[e][...], preferred_element_type=F32)
        width = united.shape[1] // 2
        gate, up = united[:, :width], united[:, width:]
        active = (gate / (1.0 + jnp.exp(-gate)) * up).astype(BF16)
        outcome = jnp.dot(active, down[e], preferred_element_type=F32)
        factor = jnp.sum(jnp.where(chosen == device * experts + e, share, 0.0), axis=-1, keepdims=True)
        total = factor * outcome if total is None else total + factor * outcome
    out[...] = total.astype(BF16)


def final_kernel(order, requests, steps, residual, a, b, c, d, out):
    result = residual[...] + sum_chips(order, a, b, c, d)
    for r in range(requests):
        out[r] = result[r * steps : (r + 1) * steps].astype(BF16)


def partner(chip, k):
    outer = (chip == 0) | (chip == 3)
    if k == 3:
        return chip ^ 3
    return jnp.where(outer, chip ^ k, chip ^ (3 - k))


def other_chip(x, k, devices):
    to = {1: (1, 3, 0, 2), 2: (2, 0, 3, 1), 3: (3, 2, 1, 0)}[k]
    return lax.ppermute(x, "tp", [(i, 2 * to[i // 2] + 1 - i % 2) for i in range(devices)])


def near_core(s):
    device = lax.axis_index("tp")
    core = device % 2
    return jnp.where(device // 2 == s, core, 1 - core)


def to_chips(parts, devices, order):
    return [parts[0]] + [other_chip(parts[k], k, devices) for k in order]


def other_core(x, devices):
    return lax.ppermute(x, "tp", [(i, i ^ 1) for i in range(devices)])


def fast_device(
    hidden_states,
    lengths,
    qkv_weight,
    rotated_key_cache,
    earlier_value_cache,
    out_weight,
    expert_ids,
    combine_weights,
    gate_up_weight,
    down_weight,
):
    requests, steps, model_width = hidden_states.shape
    tokens = requests * steps
    devices = lax.axis_size("tp")
    chips = devices // 2
    rows = tokens * GROUP
    sibling_weight = other_core(out_weight, devices)
    heads, limits, inputs = call(
        project_kernel,
        [((rows, 128), BF16), ((requests, 8, 128), jnp.int32), ((tokens, model_width), F32)],
        [lengths, hidden_states, qkv_weight],
        "project",
        cost=COST[0],
        stay=range(3),
        scratch=[
            pltpu.SMEM(lengths.shape, jnp.int32),
            pltpu.VMEM(hidden_states.shape, BF16),
            pltpu.VMEM(qkv_weight.shape, BF16),
            pltpu.SemaphoreType.DMA((3,)),
        ],
    )
    caches = [(rotated_key_cache, 0, requests), (earlier_value_cache, 0, requests)]
    small = [(x[None], 0, 1) for x in (out_weight, expert_ids, combine_weights)]
    experts = gate_up_weight.shape[0]
    cuts = [(0, SPLIT[0]), (SPLIT[0], SPLIT[1] - SPLIT[0]), (SPLIT[1], experts - SPLIT[1])]
    gate_up = [[(gate_up_weight, *cut)] if cut[1] else [] for cut in cuts]
    keys, values, own_weight, ids, shares, *gate_up_a = fetch(caches + small + gate_up[0], [heads], "fetch_cache")
    (gathered,) = call(
        functools.partial(gather_kernel, ORDER[0]),
        [((chips, rows, 128), BF16)],
        [*to_chips([heads] * chips, devices, ORDER[0]), own_weight],
        "gather",
    )
    sibling = other_core(gathered, devices)
    (blocks_own,) = call(
        functools.partial(attend_own_kernel, steps),
        [((chips // 2, 2 * rows, 128), F32)],
        [limits, gathered, keys, values],
        "attend_own",
        cost=COST[1],
    )
    parts = call(
        functools.partial(attend_sibling_kernel, steps),
        [((2 * rows, 128), F32)] + [((2 * rows, 128), BF16)] * (chips - 1),
        [limits, sibling, keys, values, blocks_own],
        "attend",
        cost=COST[1],
        scratch=[pltpu.VMEM((chips, 2 * rows, 128), F32)],
    )
    *gate_up_b, fresh = fetch(
        gate_up[1],
        [gathered, sibling, parts[0]],
        "fetch_b",
        beside=functools.partial(fresh_part, requests, steps),
        outs=[((2 * rows, 128), F32)],
    )
    arrived = to_chips(parts[:chips], devices, ORDER[1])
    (joined,) = call(functools.partial(join_kernel, ORDER[1]), [((2 * rows, 128), F32)], [*arrived, gate_up_b[0]], "join", cost=COST[2])
    (projected,) = call(
        functools.partial(output_kernel, requests, steps),
        [((tokens, model_width), BF16)],
        [joined, other_core(joined, devices), fresh, own_weight[0], sibling_weight],
        "output",
        cost=COST[2],
    )
    projections = to_chips([projected] * chips, devices, ORDER[2])
    *gate_up_c, down = fetch(gate_up[2] + [(down_weight, 0, experts)], [projected], "fetch_c")
    mixture, residual = call(
        functools.partial(expert_kernel, ORDER[2]),
        [((tokens, model_width), BF16), ((tokens, model_width), F32)],
        [inputs, *projections, ids[0], shares[0], down, *gate_up_a, *gate_up_b, *gate_up_c],
        "experts",
        cost=COST[3],
    )
    mixture = (mixture.astype(F32) + other_core(mixture, devices).astype(F32)).astype(BF16)
    mixtures = to_chips([mixture] * chips, devices, ORDER[3])
    (result,) = call(
        functools.partial(final_kernel, ORDER[3], requests, steps),
        [(hidden_states.shape, BF16)],
        [residual, *mixtures],
        "final",
        hbm_out=True,
    )
    return result


def merged(part, axis, combine):
    gathered = jax.tree.map(lambda a: lax.all_gather(a, axis), part)

    def take(source):
        return jax.tree.map(lambda a: lax.dynamic_index_in_dim(a, source, 0, False), gathered)

    return lax.fori_loop(
        1, lax.axis_size(axis), lambda source, state: combine(state, take(source)), take(0)
    )


def rms_rows(value_rows):
    return value_rows * lax.rsqrt(
        jnp.mean(value_rows * value_rows, axis=-1, keepdims=True) + EPSILON
    )


def apply_rotation(value_rows, position_index):
    half_width = value_rows.shape[-1] // 2
    rates = ROPE_BASE ** (-2.0 * jnp.arange(half_width, dtype=jnp.float32) / value_rows.shape[-1])
    angles = position_index[:, None, None] * rates
    cosine = jnp.cos(angles)
    sines = jnp.sin(angles)
    front_half = value_rows[..., :half_width]
    back_half = value_rows[..., half_width:]
    return jnp.concatenate(
        [front_half * cosine - back_half * sines, back_half * cosine + front_half * sines], axis=-1
    )


def join_parts(earlier, later):
    highest = jnp.maximum(earlier[0], later[0])
    scale_earlier = jnp.exp(earlier[0] - highest)
    scale_later = jnp.exp(later[0] - highest)
    weight_sum = earlier[1] * scale_earlier + later[1] * scale_later
    value_sum = earlier[2] * scale_earlier[..., None] + later[2] * scale_later[..., None]
    return (highest, weight_sum, value_sum)


def to_columns(value_rows, step_number, group_count):
    request_list, kv_heads, _, head_size = value_rows.shape
    return (
        value_rows.reshape(request_list, kv_heads, step_number, group_count, head_size)
        .transpose(0, 2, 1, 3, 4)
        .reshape(request_list * step_number, kv_heads * group_count * head_size)
    )


def expert_terms(normed, chosen, shares, gate_up_weight, down_weight, first_expert):
    ff_width = down_weight.shape[1]
    united_out = jnp.einsum(
        "nd,edf->enf", normed, gate_up_weight, preferred_element_type=jnp.float32
    )
    activation = (jax.nn.silu(united_out[..., :ff_width]) * united_out[..., ff_width:]).astype(
        jnp.bfloat16
    )
    outcome = jnp.einsum(
        "enf,efd->end", activation, down_weight, preferred_element_type=jnp.float32
    )
    owners = first_expert + jnp.arange(gate_up_weight.shape[0], dtype=jnp.int32)
    factors = jnp.sum(
        jnp.where(chosen[None, :, :] == owners[:, None, None], shares[None, :, :], 0.0), axis=-1
    )
    return jnp.sum(factors[:, :, None] * outcome, axis=0)


def general_device(
    hidden_states,
    lengths,
    qkv_weight,
    rotated_key_cache,
    earlier_value_cache,
    out_weight,
    expert_ids,
    combine_weights,
    gate_up_weight,
    down_weight,
):
    request_list, step_number, model_width = hidden_states.shape
    token_rows = request_list * step_number
    group_count = QUERY_HEADS // KEY_VALUE_HEADS
    query_total_width = QUERY_HEADS * HEAD_DIMENSION
    key_value_width = KEY_VALUE_HEADS * HEAD_DIMENSION
    score_scale = HEAD_DIMENSION ** (-0.5)
    inputs_flat = hidden_states.reshape(token_rows, model_width)
    normed = rms_rows(inputs_flat.astype(jnp.float32)).astype(jnp.bfloat16)
    projected_part = lax.dot_general(
        qkv_weight, normed, (((1,), (1,)), ((), ())), preferred_element_type=jnp.float32
    ).astype(jnp.bfloat16)
    projected_all = lax.all_gather(projected_part, "tp", axis=0, tiled=True)
    query_key_value_rows = projected_all.T
    position_index = (
        (lengths[:, None] + jnp.arange(step_number, dtype=jnp.int32)[None, :])
        .reshape(token_rows)
        .astype(jnp.float32)
    )
    query_rows = apply_rotation(
        query_key_value_rows[:, :query_total_width]
        .reshape(token_rows, QUERY_HEADS, HEAD_DIMENSION)
        .astype(jnp.float32),
        position_index,
    ).astype(jnp.bfloat16)
    fresh_keys = apply_rotation(
        query_key_value_rows[:, query_total_width : query_total_width + key_value_width]
        .reshape(token_rows, KEY_VALUE_HEADS, HEAD_DIMENSION)
        .astype(jnp.float32),
        position_index,
    ).astype(jnp.bfloat16)
    fresh_values = query_key_value_rows[:, query_total_width + key_value_width :].reshape(
        request_list, step_number, KEY_VALUE_HEADS, HEAD_DIMENSION
    )
    grouped_rows = (
        query_rows.reshape(request_list, step_number, KEY_VALUE_HEADS, group_count, HEAD_DIMENSION)
        .transpose(0, 2, 1, 3, 4)
        .reshape(request_list, KEY_VALUE_HEADS, step_number * group_count, HEAD_DIMENSION)
    )
    cache_extent = rotated_key_cache.shape[1]
    stored_keys = rotated_key_cache.reshape(
        request_list, cache_extent, KEY_VALUE_HEADS, HEAD_DIMENSION
    )
    stored_values = earlier_value_cache.reshape(
        request_list, cache_extent, KEY_VALUE_HEADS, HEAD_DIMENSION
    )
    scores = (
        jnp.einsum("bgqd,bcgd->bgqc", grouped_rows, stored_keys, preferred_element_type=jnp.float32)
        * score_scale
    )
    start_pos = lax.axis_index("tp") * cache_extent
    live_rows = (start_pos + jnp.arange(cache_extent, dtype=jnp.int32))[None, :] < lengths[:, None]
    live_mask = live_rows[:, None, None, :]
    masked = jnp.where(live_mask, scores, NEGATIVE)
    highest = jnp.max(masked, axis=-1)
    weights = jnp.where(live_mask, jnp.exp(masked - highest[..., None]), 0.0)
    weight_sum = jnp.sum(weights, axis=-1)
    value_sum = jnp.einsum(
        "bgqc,bcgd->bgqd",
        weights.astype(jnp.bfloat16),
        stored_values,
        preferred_element_type=jnp.float32,
    )
    feature_rows = out_weight.shape[0]
    column_begin = lax.axis_index("tp") * feature_rows
    top_score, total_all, sum_all = merged((highest, weight_sum, value_sum), "tp", join_parts)
    grouped_keys = fresh_keys.reshape(request_list, step_number, KEY_VALUE_HEADS, HEAD_DIMENSION)
    new_scores = (
        jnp.einsum(
            "bgqd,bsgd->bgqs", grouped_rows, grouped_keys, preferred_element_type=jnp.float32
        )
        * score_scale
    )
    query_step = jnp.arange(step_number * group_count, dtype=jnp.int32) // group_count
    causal = jnp.arange(step_number, dtype=jnp.int32)[None, :] <= query_step[:, None]
    new_masked = jnp.where(causal, new_scores, NEGATIVE)
    final_peak = jnp.maximum(top_score, jnp.max(new_masked, axis=-1))
    new_weights = jnp.where(causal, jnp.exp(new_masked - final_peak[..., None]), 0.0)
    carried = jnp.exp(top_score - final_peak)
    denominator = total_all * carried + jnp.sum(new_weights, axis=-1)
    new_part = jnp.einsum(
        "bgqs,bsgd->bgqd",
        new_weights.astype(jnp.bfloat16),
        fresh_values,
        preferred_element_type=jnp.float32,
    )
    numerator = sum_all * carried[..., None] + new_part
    attended = to_columns(numerator / denominator[..., None], step_number, group_count).astype(
        jnp.bfloat16
    )
    attended_part = lax.dynamic_slice_in_dim(attended, column_begin, feature_rows, 1)
    first_expert = lax.axis_index("tp") * gate_up_weight.shape[0]
    chosen = expert_ids.reshape(token_rows, -1)
    shares = combine_weights.reshape(token_rows, -1).astype(jnp.float32) / 65536.0
    head_terms = jnp.dot(attended_part, out_weight, preferred_element_type=jnp.float32)
    projected_rows = lax.psum(head_terms, "tp")
    residual = inputs_flat.astype(jnp.float32) + projected_rows
    normed_second = rms_rows(residual).astype(jnp.bfloat16)
    mixture = lax.psum(
        expert_terms(
            normed_second, chosen, shares, gate_up_weight, down_weight, first_expert
        ).astype(jnp.bfloat16),
        "tp",
    ).astype(jnp.float32)
    final_result = (residual + mixture).astype(jnp.bfloat16)
    return final_result.reshape(request_list, step_number, model_width)


def solution(mesh):
    in_specs = (
        P("req", None, None),
        P("req"),
        P("tp", None),
        P("req", "tp", None),
        P("req", "tp", None),
        P("tp", None),
        P("req", None, None),
        P("req", None, None),
        P("tp", None, None),
        P("tp", None, None),
    )
    out_specs = P("req", None, None)
    per_device = fast_device if mesh.shape["tp"] == 8 else general_device
    return jax.shard_map(
        per_device, mesh=mesh, in_specs=in_specs, out_specs=out_specs, check_vma=False
    )
```
